32 devices in a mesh: seq: 8 (over y, x, core), wt: 4 (over z).
Axes of the slice: x: 2, y: 2, z: 4, core: 2. Of those that a mesh axis runs over, the one named last changes fastest.
Arguments:
- tokens: bfloat16 [4, 2048, 2048], P('wt', 'seq'), may hold values from -6 to 6
- cotangent: bfloat16 [4, 2048, 2048], P('wt', 'seq'), may hold values from -6 to 6
- w_in: bfloat16 [2048, 8192], P(None, 'wt'), may hold values from -0.125 to 0.125
- w_out: bfloat16 [2048, 2048], P(None, 'wt'), may hold values from -0.125 to 0.125
- w_ffn: bfloat16 [2048, 11264], P(None, 'wt'), may hold values from -0.125 to 0.125
- w_down: bfloat16 [5632, 2048], P(None, 'wt'), may hold values from -0.078125 to 0.078125
- gain_mix: float32 [2048], replicated, may hold values from 0.1 to 1.9
- gain_gate: float32 [2048], replicated, may hold values from 0.1 to 1.9
- gain_ffn: float32 [2048], replicated, may hold values from 0.1 to 1.9
- forget_gap: float32 [2048], replicated, may hold values from 0.003 to 0.3
- in_a: bfloat16 [2048, 512], replicated, may hold values from -0.125 to 0.125
- in_b: bfloat16 [8192, 128], replicated, may hold values from -1 to 1
- out_a: bfloat16 [2048, 128], replicated, may hold values from -0.125 to 0.125
- out_b: bfloat16 [2048, 128], replicated, may hold values from -1 to 1
- ffn_a: bfloat16 [2048, 256], replicated, may hold values from -0.125 to 0.125
- ffn_b: bfloat16 [11264, 128], replicated, may hold values from -1 to 1
- down_a: bfloat16 [5632, 128], replicated, may hold values from -0.078125 to 0.078125
- down_b: bfloat16 [2048, 128], replicated, may hold values from -1 to 1
- order: int32 [4, 2048], P('wt'), may hold values from 0 to 2047, each once within a row
- lengths: int32 [4, 4], P('wt'), may hold values from 1 to 1024, 2048 in all within a row
- adapter_ids: int32 [4, 4], P('wt'), may hold values from 0 to 7
Outputs:
- block_out: bfloat16 [4, 2048, 2048], P('wt', 'seq')
- tokens_grad: bfloat16 [4, 2048, 2048], P('wt', 'seq')
- in_a_grad: float32 [2048, 512], P(('seq', 'wt'))
- in_b_grad: float32 [8192, 128], P(('seq', 'wt'))
- out_a_grad: float32 [2048, 128], P(('seq', 'wt'))
- out_b_grad: float32 [2048, 128], P(('seq', 'wt'))
- ffn_a_grad: float32 [2048, 256], P(('seq', 'wt'))
- ffn_b_grad: float32 [11264, 128], P(('seq', 'wt'))
- down_a_grad: float32 [5632, 128], P(('seq', 'wt'))
- down_b_grad: float32 [2048, 128], P(('seq', 'wt'))
The draws below stay inside these ranges and needn't reach their ends.
Inputs may be any that keep to these rules, and one draw needn't show every extreme that they name: `order`: each row is a permutation of the group's positions. `lengths`: each row sums to 2048; its largest entry is exactly 1024.
All inputs are finite; a program needn't handle non-finite values.
Results may differ from the reference program's by a relative error of at most 0.015.
Values may be sent and summed in bfloat16 or wider, within the bound.
No kernel may reach another device: no remote copies, remote signals or barrier semaphores. Data moves between devices by JAX's collectives and lax.ppermute only.
A program may use at most 384 MiB of HBM per device.

```python
import math
import jax
import jax.numpy as jnp
import numpy as np
from jax import lax

D = 2048
FF = 5632
HEAD = 128
RANK = 16
ADAPTERS = 8
NSEQ = 4
SPAN = 64
BLOCK = 512
GROUP = 2048
LONGEST = 1024
N_WT = 4


def set_ends(entries, rng, low, high):
    shape = entries.shape
    place = [jax.random.randint(jax.random.fold_in(rng, axis), (), 0, shape[axis]) for axis in range(len(shape))]
    entries = entries.at[tuple(place)].set(low)
    longest = shape.index(max(shape))
    place[longest] = (place[longest] + 1) % shape[longest]
    return entries.at[tuple(place)].set(high)


def with_spikes(values, rng, source, target, shards_of, factor):
    owner, partner = [(jnp.arange(values.shape[position]) // (values.shape[position] // shards_of)).reshape([-1 if axis == position else 1 for axis in range(values.ndim)]) for position in (source, target)]
    chosen = jax.random.permutation(rng, shards_of)[partner]
    strong = (owner == chosen) | (owner == (partner + shards_of // 2) % shards_of)
    return jnp.where(strong, factor * values, values)


def steps_of(key, extent, cuts, low, high):
    def one(axis_at, shards_of):
        steps = jax.random.uniform(jax.random.fold_in(jax.random.fold_in(key, 6), axis_at), (shards_of,), jnp.float32, low / len(cuts), high / len(cuts))
        return jnp.repeat(jnp.exp(steps), extent[axis_at] // shards_of).reshape((-1,) + (1,) * (len(extent) - axis_at - 1))

    level = one(*cuts[0])
    for cut in cuts[1:]:
        level = level * one(*cut)
    return level


def length_profile(number_of, total, bound, lean):
    portions = [(1 << 20) // math.isqrt(standing ** lean) + 1 for standing in range(2, number_of + 1)]
    surplus, holding = total - bound - (number_of - 1), [1] * (number_of - 1)
    while surplus > 0:
        movable = [i for i in range(number_of - 1) if holding[i] < bound]
        mass, left = sum([portions[i] for i in movable]), surplus
        for i in movable:
            more = min(bound - holding[i], max(1, left * portions[i] // mass), surplus)
            holding[i] = holding[i] + more
            surplus = surplus - more
    return np.array([bound] + holding)


def uneven(key, number_of, total, reach, lean):
    if number_of == 2:
        one = jax.random.randint(key, (), max(1, total - reach), min(reach, total - 1) + 1)
        return jnp.stack([one, total - one])
    sizes = jnp.asarray(length_profile(number_of, total, reach, lean), jnp.int32)
    twos = (number_of - 1) // 2
    giver, taker = sizes[1:1 + 2 * twos:2], sizes[2:2 + 2 * twos:2]
    slack = jnp.minimum(giver - 1, reach - taker)
    passed = jax.random.randint(jax.random.fold_in(key, 1), (twos,), 0, 1 << 20) % (slack + 1)
    sizes = sizes.at[1:1 + 2 * twos:2].set(giver - passed).at[2:2 + 2 * twos:2].set(taker + passed)
    return sizes[jax.random.permutation(jax.random.fold_in(key, 2), number_of)]


def bell_draw(rng, dims, scale, limit, cuts=(), kind=jnp.bfloat16):
    factor_of = steps_of(rng, dims, cuts, -0.22, 0.18) if cuts else 1.0
    entries = jax.random.normal(rng, dims, jnp.float32) * scale * factor_of
    return jnp.minimum(jnp.maximum(entries, -limit), limit).astype(kind)


def gaussian_with(rng, shape, scale, bound, cuts, heavy, kind=jnp.bfloat16):
    entries = scale * jax.random.normal(rng, shape, jnp.float32)
    if cuts:
        entries = entries * steps_of(rng, shape, cuts, -0.22, 0.18)
    return jnp.clip(with_spikes(entries, jax.random.fold_in(rng, 3), *heavy), -bound, bound).astype(kind)


def setup_inputs(seed: int = 0) -> dict:
    seeds = jax.random.split(jax.random.key(seed), 22)
    return {
        "tokens": bell_draw(seeds[0], (N_WT, GROUP, D), 1.0, 6.0, ((0, 4), (1, 8))),
        "cotangent": gaussian_with(seeds[1], (N_WT, GROUP, D), 1.0, 6.0, ((0, 4), (1, 8)), (1, 2, 8, 2.0)),
        "w_in": bell_draw(seeds[2], (D, 4 * D), D ** -0.5, 0.125, ((1, 4),)),
        "w_out": bell_draw(seeds[3], (D, D), D ** -0.5, 0.125, ((1, 4),)),
        "w_ffn": bell_draw(seeds[4], (D, 2 * FF), D ** -0.5, 0.125, ((1, 4),)),
        "w_down": bell_draw(seeds[5], (FF, D), FF ** -0.5, 0.078125, ((1, 4),)),
        "gain_mix": jnp.clip(1.0 + 0.18 * jax.random.normal(seeds[6], (D,), jnp.float32), 0.1, 1.9),
        "gain_gate": jnp.clip(1.0 + 0.18 * jax.random.normal(seeds[7], (D,), jnp.float32), 0.1, 1.9),
        "gain_ffn": jnp.clip(1.0 + 0.18 * jax.random.normal(seeds[8], (D,), jnp.float32), 0.1, 1.9),
        "forget_gap": jnp.clip(jnp.exp(jax.random.uniform(seeds[9], (D,), jnp.float32, math.log(0.003), math.log(0.3))), 0.003, 0.3),
        "in_a": bell_draw(seeds[10], (D, 4 * ADAPTERS * RANK), D ** -0.5, 0.125),
        "in_b": bell_draw(seeds[11], (4 * D, ADAPTERS * RANK), (2 * RANK) ** -0.5, 1.0),
        "out_a": bell_draw(seeds[12], (D, ADAPTERS * RANK), D ** -0.5, 0.125),
        "out_b": bell_draw(seeds[13], (D, ADAPTERS * RANK), (2 * RANK) ** -0.5, 1.0),
        "ffn_a": bell_draw(seeds[14], (D, 2 * ADAPTERS * RANK), D ** -0.5, 0.125),
        "ffn_b": bell_draw(seeds[15], (2 * FF, ADAPTERS * RANK), (2 * RANK) ** -0.5, 1.0),
        "down_a": bell_draw(seeds[16], (FF, ADAPTERS * RANK), FF ** -0.5, 0.078125),
        "down_b": bell_draw(seeds[17], (D, ADAPTERS * RANK), (2 * RANK) ** -0.5, 1.0),
        "order": jax.vmap(lambda own: jax.random.permutation(own, GROUP))(jax.random.split(seeds[18], N_WT)).reshape((N_WT, GROUP)).astype(jnp.int32),
        "lengths": jax.vmap(lambda own: uneven(own, NSEQ, GROUP, LONGEST, 2))(jax.random.split(seeds[19], N_WT)).reshape((N_WT, NSEQ)).astype(jnp.int32),
        "adapter_ids": set_ends(jax.random.randint(seeds[20], (N_WT, NSEQ), 0, ADAPTERS), jax.random.fold_in(seeds[20], 1), 0, ADAPTERS - 1).astype(jnp.int32),
    }


highest = lax.Precision.HIGHEST
eps_norm = 1e-06

@jax.custom_vjp
def low(v):
    return lax.optimization_barrier(v.astype(jnp.bfloat16)).astype(jnp.float32)

@jax.custom_vjp
def low_back(v):
    return v

def low_keep(v):
    return (low(v), None)

def low_pass(kept, grad):
    return (grad,)

def back_keep(v):
    return (v, None)

def back_low(kept, grad):
    return (low(grad),)
low.defvjp(low_keep, low_pass)
low_back.defvjp(back_keep, back_low)

def matmul(left, right):
    return jnp.dot(left, right, precision=highest, preferred_element_type=jnp.float32)

def rms_scale(values, gain):
    return values * lax.rsqrt(lax.optimization_barrier(jnp.mean(values * values, axis=-1, keepdims=True)) + eps_norm) * gain

def sequence_of(positions, seq_lengths):
    bounds = jnp.cumsum(seq_lengths)[:-1]
    return lax.optimization_barrier(jnp.sum((positions[:, None] >= bounds[None, :]).astype(jnp.int32), axis=1))

def adapter_of(seq_numbers, seq_ids):
    numbers = jnp.arange(seq_ids.shape[0], dtype=jnp.int32)
    return lax.optimization_barrier(jnp.sum((seq_numbers[:, None] == numbers[None, :]).astype(jnp.int32) * seq_ids[None, :], axis=1))

def adapter_mask(adapter):
    columns = jnp.arange(ADAPTERS * RANK, dtype=jnp.int32) // RANK
    return (columns[None, :] == adapter[:, None]).astype(jnp.float32)

def block_terms(inputs):
    query_block, key_block, logf_block, value_block, seg_block = inputs
    width = query_block.shape[1]
    cumulative = jnp.cumsum(logf_block, axis=1)
    places = jnp.arange(width, dtype=jnp.int32)
    causal = places[:, None] >= places[None, :]
    allowed = causal[None] & (seg_block[:, :, None] == seg_block[:, None, :])
    log_gap = cumulative[:, :, None] - cumulative[:, None, :]
    decays = jnp.exp(jnp.where(allowed[:, :, :, None, None], log_gap, -1e+30))
    scores = lax.optimization_barrier(jnp.sum(query_block[:, :, None] * key_block[:, None, :] * decays, axis=-1))
    intra = jnp.einsum('btsh,bshv->bthv', scores, value_block, precision=highest)
    final_log = cumulative[:, -1]
    tail_ok = (seg_block == seg_block[:, -1:]).astype(jnp.float32)
    tail_keys = jnp.exp(final_log[:, None] - cumulative) * key_block * tail_ok[:, :, None, None]
    update = jnp.einsum('bshk,bshv->bhkv', tail_keys, value_block, precision=highest)
    return (intra, update, jnp.exp(final_log), query_block * jnp.exp(cumulative))

def mixer(queries, keys, logf, values, seg_nat):
    total, heads, width = queries.shape
    nchunk = total // SPAN
    per_block = BLOCK // SPAN

    def shape_blocks(array):
        return array.reshape((total // BLOCK, per_block, SPAN) + array.shape[1:])
    parts = lax.map(jax.checkpoint(block_terms), (shape_blocks(queries), shape_blocks(keys), shape_blocks(logf), shape_blocks(values), shape_blocks(seg_nat)))
    intra, update, decay, query_decayed = [piece.reshape((nchunk,) + piece.shape[2:]) for piece in parts]
    seg_spans = seg_nat.reshape(nchunk, SPAN)
    before = jnp.concatenate([jnp.full((1,), -1, jnp.int32), seg_spans[:-1, -1]])
    carry_keep = (seg_spans[:, -1] == before).astype(jnp.float32)
    factor = decay * carry_keep[:, None, None]

    def combine(first, second):
        return (first[0] * second[0], second[0][..., None] * first[1] + second[1])
    scanned = lax.associative_scan(combine, (factor, update))
    end_states = scanned[1]
    start_states = jnp.concatenate([jnp.zeros_like(end_states[:1]), end_states[:-1]])
    carry_ok = (seg_spans == before[:, None]).astype(jnp.float32)
    inter = jnp.einsum('cthk,chkv->cthv', query_decayed, start_states, precision=highest) * carry_ok[:, :, None, None]
    return (intra + inter).reshape(total, heads, width)

def branch(inputs, a_mat, b_mat, mask, count):
    row_count = inputs.shape[0]
    rank_all = ADAPTERS * RANK
    hid = low(low_back(matmul(inputs, a_mat) * jnp.tile(mask, (1, count))))
    result = jnp.einsum('tpr,pdr->tpd', hid.reshape(row_count, count, rank_all), b_mat.reshape(count, -1, rank_all), precision=highest)
    return result.reshape(row_count, -1)

def layer(inputs, adapters, frozen, forget_gap, order_g, lengths_g, ids_g):
    in_a, in_b, out_a, out_b, ffn_a, ffn_b, down_a, down_b = adapters
    w_in, w_out, w_ffn, w_down, gain_mix, gain_gate, gain_ffn = frozen
    row_count = inputs.shape[0]
    seg_nat = sequence_of(jnp.arange(row_count, dtype=jnp.int32), lengths_g)
    adapter = adapter_of(seg_nat, ids_g)[order_g]
    mask = adapter_mask(adapter)
    inverse = jnp.zeros((row_count,), jnp.int32).at[order_g].set(jnp.arange(row_count, dtype=jnp.int32))
    normed = low(rms_scale(inputs, gain_mix))
    proj = low_back(matmul(normed, w_in) + branch(normed, in_a, in_b, mask, 4))
    zq, zf, zv, zg = jnp.split(proj, 4, axis=1)
    queries = low(low_back(jax.nn.silu(zq)))
    forget_in = low(zf)
    values = low(zv)
    heads = D // HEAD
    gap_heads = forget_gap.reshape(heads, HEAD)
    keys = gap_heads * (1.0 - jax.nn.sigmoid(forget_in[inverse].reshape(row_count, heads, HEAD)))
    logf = jnp.log1p(-keys)
    mixed_nat = mixer(queries[inverse].reshape(row_count, heads, HEAD), keys, logf, values[inverse].reshape(row_count, heads, HEAD), seg_nat)
    mixed = low(low_back(mixed_nat.reshape(row_count, D)[order_g]))
    gated = low(rms_scale(mixed, gain_gate) * jax.nn.silu(zg))
    attn = low_back(matmul(gated, w_out) + branch(gated, out_a, out_b, mask, 1))
    resid = inputs + attn
    normed2 = low(rms_scale(resid, gain_ffn))
    both = low_back(matmul(normed2, w_ffn) + branch(normed2, ffn_a, ffn_b, mask, 2))
    gate, upper = jnp.split(both, 2, axis=1)
    hidden = low(jax.nn.silu(gate) * upper)
    down = low_back(matmul(hidden, w_down) + branch(hidden, down_a, down_b, mask, 1))
    return resid + down

def reference(tokens, cotangent, w_in, w_out, w_ffn, w_down, gain_mix, gain_gate, gain_ffn, forget_gap, in_a, in_b, out_a, out_b, ffn_a, ffn_b, down_a, down_b, order, lengths, adapter_ids):
    frozen = tuple((array.astype(jnp.float32) for array in (w_in, w_out, w_ffn, w_down, gain_mix, gain_gate, gain_ffn)))
    adapters = tuple((array.astype(jnp.float32) for array in (in_a, in_b, out_a, out_b, ffn_a, ffn_b, down_a, down_b)))
    gap_values = forget_gap.astype(jnp.float32)

    def one_group(totals, group_data):
        inputs, cot_group, order_g, lengths_g, ids_g = group_data

        def forward(input_values, adapter_values):
            return layer(input_values, adapter_values, frozen, gap_values, order_g, lengths_g, ids_g)
        result, pullback = jax.vjp(forward, inputs.astype(jnp.float32), adapters)
        grad_inputs, grad_adapters = pullback(cot_group.astype(jnp.float32))
        totals = jax.tree.map(lambda first, second: first + second, totals, grad_adapters)
        return (totals, (result.astype(jnp.bfloat16), grad_inputs.astype(jnp.bfloat16)))
    zeros = tuple((jnp.zeros(array.shape, jnp.float32) for array in adapters))
    totals, stacked = lax.scan(one_group, zeros, (tokens, cotangent, order, lengths, adapter_ids))
    return (stacked[0], stacked[1], totals[0], totals[1], totals[2], totals[3], totals[4], totals[5], totals[6], totals[7])
```

```python
import jax
import jax.numpy as jnp
from jax import lax
from jax.sharding import PartitionSpec as P
from jax.experimental import pallas as pl
from jax.experimental.pallas import tpu as pltpu

HEAD = 128
CHUNK = 128
TILE = 512
NN = (((1,), (0,)), ((), ()))
NT = (((1,), (1,)), ((), ()))
TN = (((0,), (0,)), ((), ()))


def mm(left, right, dims=NN):
    return lax.dot_general(left, right, dims, preferred_element_type=jnp.float32)


def halves(values):
    high = values.astype(jnp.bfloat16)
    return high, (values - high.astype(jnp.float32)).astype(jnp.bfloat16)


def mm3(left, right, dims=NN):
    return mm(left[0], right[0], dims) + (mm(left[0], right[1], dims) + mm(left[1], right[0], dims))


def mm2(left, right, dims=NN):
    return mm(left[0], right, dims) + mm(left[1], right, dims)


def mm2r(left, right, dims=NN):
    return mm(left, right[0], dims) + mm(left, right[1], dims)


def sum_with(ones, values):
    high, rest = halves(values)
    mid = (values - high.astype(jnp.float32) - rest.astype(jnp.float32)).astype(jnp.bfloat16)
    return mm(ones, high) + (mm(ones, rest) + mm(ones, mid))


def move_rows(picks, pairs):
    total = pairs[0][0].shape[0]

    @pl.loop(0, total // TILE)
    def _(tile):
        start = pl.multiple_of(tile * TILE, TILE)
        chosen = picks(start, total)
        for source, target in pairs:
            target[pl.ds(start, TILE), :] = mm(chosen, source[...]).astype(jnp.bfloat16)


def picks_natural(order_row_ref):
    def picks(start, total):
        places = lax.broadcasted_iota(jnp.int32, (TILE, total), 0) + start
        return jnp.where(order_row_ref[...] == places, 1.0, 0.0).astype(jnp.bfloat16)

    return picks


def picks_packed(order_column_ref):
    def picks(start, total):
        places = lax.broadcasted_iota(jnp.int32, (TILE, total), 1)
        return jnp.where(order_column_ref[pl.ds(start, TILE), :] == places, 1.0, 0.0).astype(jnp.bfloat16)

    return picks


def segment_terms(ends_ref, start):
    count = ends_ref.shape[0] - 1

    def seg_of(positions):
        return sum((positions >= ends_ref[j]).astype(jnp.int32) for j in range(count))

    rows = lax.broadcasted_iota(jnp.int32, (CHUNK, CHUNK), 0)
    cols = lax.broadcasted_iota(jnp.int32, (CHUNK, CHUNK), 1)
    same = seg_of(rows + start) == seg_of(cols + start)
    wide = seg_of(lax.broadcasted_iota(jnp.int32, (CHUNK, HEAD), 0) + start)
    before = jnp.where(start == 0, -1, seg_of(start - 1))
    last = seg_of(start + CHUNK - 1)
    carry_ok = (wide == before).astype(jnp.float32)
    tail_ok = (wide == last).astype(jnp.float32)
    keep = (last == before).astype(jnp.float32)
    return (rows >= cols) & same, (rows <= cols) & same, carry_ok, tail_ok, keep


def chunk_decays(forget, gap, lower):
    sigma = jax.nn.sigmoid(forget)
    keys = gap * (1.0 - sigma)
    cumulative = sum_with(lower, jnp.log1p(-keys))
    middle = cumulative[CHUNK // 2 - 1 : CHUNK // 2]
    total = cumulative[CHUNK - 1 : CHUNK]
    return sigma, keys, cumulative, middle, total


def lower_ones():
    rows = lax.broadcasted_iota(jnp.int32, (CHUNK, CHUNK), 0)
    cols = lax.broadcasted_iota(jnp.int32, (CHUNK, CHUNK), 1)
    return jnp.where(rows >= cols, 1.0, 0.0).astype(jnp.bfloat16)


def forward_kernel(
    ends_ref, order_row_ref, order_column_ref, query_ref, forget_ref, value_ref, gap_ref,
    mixed_ref, query_nat, forget_nat, value_nat, states_ref, out_nat, state_now,
):
    total, width = query_ref.shape
    heads = width // HEAD
    move_rows(
        picks_natural(order_row_ref),
        ((query_ref, query_nat), (forget_ref, forget_nat), (value_ref, value_nat)),
    )
    state_now[...] = jnp.zeros_like(state_now)
    lower = lower_ones()

    @pl.loop(0, total // CHUNK)
    def _(chunk):
        start = pl.multiple_of(chunk * CHUNK, CHUNK)
        rows = pl.ds(start, CHUNK)
        allowed, _, carry_ok, tail_ok, keep = segment_terms(ends_ref, start)
        for head in range(heads):
            lanes = slice(head * HEAD, (head + 1) * HEAD)
            query = query_nat[rows, lanes].astype(jnp.float32)
            value = value_nat[rows, lanes]
            _, keys, cumulative, middle, final = chunk_decays(
                forget_nat[rows, lanes].astype(jnp.float32), gap_ref[:, lanes], lower
            )
            grown = jnp.exp(cumulative - middle)
            shrunk = jnp.exp(middle - cumulative)
            scores = mm3(halves(query * grown), halves(keys * shrunk), NT)
            scores = jnp.where(allowed, scores, 0.0)
            state = state_now[head]
            states_ref[chunk, head] = state
            inter = mm3(halves(query * jnp.exp(cumulative) * carry_ok), halves(state), NT)
            out_nat[rows, lanes] = (mm2(halves(scores), value) + inter).astype(jnp.bfloat16)
            tail = keys * jnp.exp(final - cumulative) * tail_ok
            state_now[head] = state * (jnp.exp(final) * keep) + mm2r(value, halves(tail), TN)

    states_ref[total // CHUNK] = state_now[...]
    move_rows(picks_packed(order_column_ref), ((out_nat, mixed_ref),))


def backward_kernel(
    ends_ref, order_row_ref, order_column_ref, grad_ref, query_nat, forget_nat, value_nat, states_ref, gap_ref,
    d_query_ref, d_forget_ref, d_value_ref, grad_nat, d_query_nat, d_forget_nat, d_value_nat, slope_now,
):
    total, width = grad_ref.shape
    heads = width // HEAD
    move_rows(picks_natural(order_row_ref), ((grad_ref, grad_nat),))
    slope_now[...] = jnp.zeros_like(slope_now)
    lower = lower_ones()

    @pl.loop(0, total // CHUNK)
    def _(step):
        chunk = total // CHUNK - 1 - step
        start = pl.multiple_of(chunk * CHUNK, CHUNK)
        rows = pl.ds(start, CHUNK)
        allowed, later, carry_ok, tail_ok, keep = segment_terms(ends_ref, start)
        later = jnp.where(later, 1.0, 0.0).astype(jnp.bfloat16)
        for head in range(heads):
            lanes = slice(head * HEAD, (head + 1) * HEAD)
            query = query_nat[rows, lanes].astype(jnp.float32)
            value = value_nat[rows, lanes]
            grad = grad_nat[rows, lanes]
            sigma, keys, cumulative, middle, final = chunk_decays(
                forget_nat[rows, lanes].astype(jnp.float32), gap_ref[:, lanes], lower
            )
            grown = jnp.exp(cumulative - middle)
            shrunk = jnp.exp(middle - cumulative)
            query_grown = halves(query * grown)
            keys_shrunk = halves(keys * shrunk)
            scores = halves(jnp.where(allowed, mm3(query_grown, keys_shrunk, NT), 0.0))
            d_scores = halves(jnp.where(allowed, mm(grad, value, NT), 0.0))
            state = halves(states_ref[chunk, head])
            slope = slope_now[head]
            slope_parts = halves(slope)
            from_start = jnp.exp(cumulative) * carry_ok
            to_end = jnp.exp(final - cumulative) * tail_ok
            d_query = mm3(d_scores, keys_shrunk) * grown + mm2r(grad, state) * from_start
            d_keys = mm3(d_scores, query_grown, TN) * shrunk + mm2r(value, slope_parts) * to_end
            d_value = mm2(scores, grad, TN) + mm3(halves(keys * to_end), slope_parts, NT)
            past = jnp.sum(states_ref[chunk + 1, head] * slope, axis=0, keepdims=True)
            d_logf = sum_with(later, query * d_query - keys * d_keys) + tail_ok * past
            d_keys = d_keys - d_logf / (1.0 - keys)
            slope_now[head] = slope * (jnp.exp(final) * keep) + mm2r(grad, halves(query * from_start), TN)
            d_query_nat[rows, lanes] = d_query.astype(jnp.bfloat16)
            d_forget_nat[rows, lanes] = (-d_keys * keys * sigma).astype(jnp.bfloat16)
            d_value_nat[rows, lanes] = d_value.astype(jnp.bfloat16)

    move_rows(
        picks_packed(order_column_ref),
        ((d_query_nat, d_query_ref), (d_forget_nat, d_forget_ref), (d_value_nat, d_value_ref)),
    )


def mixer_cost(total, width, matmuls):
    flops = 2 * total * width * (CHUNK * matmuls + total * 4)
    return pl.CostEstimate(flops=flops, bytes_accessed=20 * total * width, transcendentals=6 * total * width)


VMEM = pl.BlockSpec(memory_space=pltpu.VMEM)
SMEM = pl.BlockSpec(memory_space=pltpu.SMEM)


def mixer_forward(ends, order, queries, forgets, values, gap):
    total, width = queries.shape
    heads = width // HEAD
    rows = jax.ShapeDtypeStruct((total, width), jnp.bfloat16)
    states = jax.ShapeDtypeStruct((total // CHUNK + 1, heads, HEAD, HEAD), jnp.float32)
    return pl.pallas_call(
        forward_kernel,
        out_shape=(rows, rows, rows, rows, states),
        in_specs=[SMEM] + [VMEM] * 6,
        out_specs=(VMEM,) * 5,
        scratch_shapes=[
            pltpu.VMEM((total, width), jnp.bfloat16),
            pltpu.VMEM((heads, HEAD, HEAD), jnp.float32),
        ],
        compiler_params=pltpu.CompilerParams(vmem_limit_bytes=40 * 2**20),
        cost_estimate=mixer_cost(total, width, 12),
    )(ends, order.reshape(1, total), order.reshape(total, 1), queries, forgets, values, gap.reshape(1, width))


def mixer_backward(ends, order, grads, kept, gap):
    total, width = grads.shape
    heads = width // HEAD
    rows = jax.ShapeDtypeStruct((total, width), jnp.bfloat16)
    return pl.pallas_call(
        backward_kernel,
        out_shape=(rows, rows, rows),
        in_specs=[SMEM] + [VMEM] * 8,
        out_specs=(VMEM,) * 3,
        scratch_shapes=[pltpu.VMEM((total, width), jnp.bfloat16)] * 4
        + [pltpu.VMEM((heads, HEAD, HEAD), jnp.float32)],
        compiler_params=pltpu.CompilerParams(vmem_limit_bytes=40 * 2**20),
        cost_estimate=mixer_cost(total, width, 40),
    )(ends, order.reshape(1, total), order.reshape(total, 1), grads, *kept, gap.reshape(1, width))


ADAPTERS = 8
RANK = 16
RANKS = ADAPTERS * RANK
PROJECTIONS = 4
eps_norm = 1e-06
f32 = jnp.float32
bf16 = jnp.bfloat16


def sequence_of(positions, seq_lengths):
    bounds = jnp.cumsum(seq_lengths)[:-1]
    return jnp.sum((positions[:, None] >= bounds[None, :]).astype(jnp.int32), axis=1)


def adapter_of(seq_numbers, seq_ids):
    numbers = jnp.arange(seq_ids.shape[0], dtype=jnp.int32)
    return jnp.sum(
        (seq_numbers[:, None] == numbers[None, :]).astype(jnp.int32) * seq_ids[None, :], axis=1
    )


def adapter_mask(adapter):
    columns = jnp.arange(RANKS, dtype=jnp.int32) // RANK
    return (columns[None, :] == adapter[:, None]).astype(f32)


def norm_factor(values):
    return lax.rsqrt(jnp.mean(values * values, axis=-1, keepdims=True) + eps_norm)


def norm_back(values, factor, gain, grad):
    scaled = grad * gain
    return factor * scaled - values * factor**3 * jnp.mean(values * scaled, axis=-1, keepdims=True)


def silu_slope(values, sigma):
    return sigma * (1.0 + values * (1.0 - sigma))


def relative(blocks, index):
    count, rest = blocks.shape[0], blocks.shape[1:]
    bit = 1
    while bit < count:
        pairs = blocks.reshape((count // (2 * bit), 2, bit) + rest)
        blocks = jnp.where((index & bit) != 0, pairs[:, ::-1], pairs).reshape((count,) + rest)
        bit *= 2
    return blocks


def across(values, bits, axis="seq"):
    size = lax.axis_size(axis)
    return lax.ppermute(values, axis, [(i, i ^ bits) for i in range(size)])


def gather_direct(block):
    return [block] + [across(block, k) for k in range(1, lax.axis_size("seq"))]


def scatter_direct(parts, axis="seq"):
    total = parts[0].astype(f32)
    for k in range(1, lax.axis_size(axis)):
        total = total + across(parts[k], k, axis).astype(f32)
    return total


def gather_blocks(block):
    if lax.axis_size("seq") != 8:
        return gather_direct(block)
    half = block.shape[0] // 2
    by_x, by_y = across(block, 2), across(block, 4)
    far = jnp.concatenate([across(by_x[:half], 4), across(by_y[half:], 2)])
    near = [block, by_x, by_y, far]
    return [piece for own in near for piece in (own, across(own, 1))]


def scatter_blocks(parts):
    if lax.axis_size("seq") != 8:
        return scatter_direct(parts)
    half = parts[0].shape[0] // 2
    far, by_y, by_x, own = [
        parts[k].astype(f32) + across(parts[k + 1], 1).astype(f32) for k in (6, 4, 2, 0)
    ]
    by_x_more = by_x[half:] + across(far[half:].astype(bf16), 4).astype(f32)
    by_y_more = by_y[:half] + across(far[:half].astype(bf16), 2).astype(f32)
    from_x = [across(by_x[:half].astype(bf16), 2), across(by_x_more.astype(bf16), 2)]
    from_y = [across(by_y_more.astype(bf16), 4), across(by_y[half:].astype(bf16), 4)]
    return (
        own
        + jnp.concatenate(from_x).astype(f32)
        + jnp.concatenate(from_y).astype(f32)
    )


def exchange(parts):
    return [parts[0]] + [across(parts[k], k) for k in range(1, len(parts))]


def line_gather(block):
    count, place = lax.axis_size("wt"), lax.axis_index("wt")
    rising, falling = [block], [block]
    for step in range(1, count):
        rising.append(
            lax.ppermute(rising[-1], "wt", [(i, i + 1) for i in range(step - 1, count - 1)])
        )
        falling.append(
            lax.ppermute(falling[-1], "wt", [(i, i - 1) for i in range(1, count - step + 1)])
        )
    result = jnp.zeros((count,) + block.shape, block.dtype)
    result = lax.dynamic_update_index_in_dim(result, block, place, 0)
    for step in range(1, count):
        piece = jnp.where(place + step < count, falling[step], rising[count - step])
        result = lax.dynamic_update_index_in_dim(result, piece, (place + step) % count, 0)
    return result


def line_reduce(values):
    count, place = lax.axis_size("wt"), lax.axis_index("wt")
    parts = [lax.dynamic_index_in_dim(values, place ^ k, 0, False) for k in range(count)]
    return scatter_direct(parts, "wt")


def to_rows(pieces):
    count = pieces.shape[0]
    size, place = lax.axis_size("seq"), lax.axis_index("seq")
    span = size // count
    result = jnp.zeros_like(pieces)
    for k in range(count):
        piece = lax.dynamic_index_in_dim(pieces, (place % count + k) % count, 0, False)
        moves = [(i, ((i % count + k) % count) * span + i // count) for i in range(size)]
        got = lax.ppermute(piece, "seq", moves)
        result = lax.dynamic_update_index_in_dim(result, got, (place // span + count - k) % count, 0)
    return result.reshape((-1,) + pieces.shape[2:])


def with_scalars(block, scalars):
    rows, columns = block.shape
    lines = []
    for values in scalars:
        high, rest = halves(values)
        last = (values - high.astype(f32) - rest.astype(f32)).astype(bf16)
        lines += [high, rest, last]
    lines = jnp.concatenate(lines).reshape(-1, columns)
    return jnp.concatenate([block, jnp.pad(lines, ((0, -lines.shape[0] % 16), (0, 0)))])


def split_scalars(packed, rows, count):
    columns = packed.shape[1]
    lines = packed[rows : rows + 3 * count * rows // columns].astype(f32).reshape(count, 3, rows)
    return packed[:rows], [lines[i, 0] + lines[i, 1] + lines[i, 2] for i in range(count)]


def fold_columns(count):
    source = jnp.arange(count * RANKS)
    target = jnp.arange(RANKS)
    wanted = (source // RANKS) * RANK + source % RANK
    return (wanted[:, None] == target[None, :]).astype(bf16)


def local(
    tokens,
    cotangent,
    w_in,
    w_out,
    w_ffn,
    w_down,
    gain_mix,
    gain_gate,
    gain_ffn,
    forget_gap,
    in_a,
    in_b,
    out_a,
    out_b,
    ffn_a,
    ffn_b,
    down_a,
    down_b,
    order,
    lengths,
    adapter_ids,
):
    n, wt = lax.axis_size("seq"), lax.axis_size("wt")
    mine = lax.axis_index("seq")
    inputs = tokens[0].astype(f32)
    cot_rows = cotangent[0]
    rows, model = inputs.shape
    total = n * rows
    wide = model // n
    pair = 2 * rows
    pairs = n // 2

    def my_columns(values, extent, axis):
        return lax.dynamic_slice_in_dim(values, mine * extent, extent, axis)

    def my_piece(values, axis):
        return lax.dynamic_index_in_dim(values, mine, axis, False)

    def in_pairs(blocks):
        return [jnp.concatenate(blocks[2 * i : 2 * i + 2]) for i in range(pairs)]

    def of_pair(values, i):
        return values[i * pair : (i + 1) * pair]

    def blocks_of(values):
        return [values[k * rows : (k + 1) * rows] for k in range(n)]

    order_mine = relative(order[0].reshape(n, rows), mine).reshape(total)
    ends = jnp.cumsum(lengths[0])
    mask = adapter_mask(adapter_of(sequence_of(order_mine, lengths[0]), adapter_ids[0]))
    mask_own = mask[:rows]
    gap_mine = my_columns(forget_gap, wide, 0)
    gain_mine = my_columns(gain_gate, wide, 0)

    if wt == PROJECTIONS:
        win = line_gather(my_columns(w_in, wide, 1).T)
    else:
        whole = lax.all_gather(w_in, "wt", axis=1, tiled=True)
        win = jnp.transpose(my_piece(whole.reshape(model, PROJECTIONS, n, wide), 2), (1, 2, 0))
    win = win.reshape(PROJECTIONS * wide, model)
    in_b_mine = my_piece(in_b.reshape(PROJECTIONS, n, wide, RANKS), 1)

    factor_one = norm_factor(inputs)
    normed = (inputs * factor_one * gain_mix).astype(bf16)
    normed_pairs = in_pairs(gather_blocks(normed))

    wout = line_gather(my_columns(w_out, wide, 0))
    wout = jnp.transpose(wout, (1, 0, 2)).reshape(wide, model)
    wout = jnp.concatenate(gather_blocks(wout))
    out_a_mine = relative(out_a.reshape(n, wide, RANKS), mine).reshape(model, RANKS)

    units = w_ffn.shape[1] // n
    wffn = line_gather(my_columns(w_ffn, units, 1).T)
    w_gate = wffn[: wt // 2].reshape(-1, model)
    w_up = wffn[wt // 2 :].reshape(-1, model)
    wdown = my_piece(w_down.reshape(wt // 2, n, units, -1), 1).reshape(wt // 2 * units, -1)
    wdown = jnp.transpose(line_gather(wdown), (1, 0, 2)).reshape(wt // 2 * units, model)
    ffn_b_mine = my_piece(ffn_b.reshape(wt, n, units, RANKS), 1)
    b_gate = ffn_b_mine[: wt // 2].reshape(-1, RANKS)
    b_up = ffn_b_mine[wt // 2 :].reshape(-1, RANKS)
    down_a_mine = my_piece(down_a.reshape(wt // 2, n, units, RANKS), 1).reshape(-1, RANKS)

    masks = [of_pair(mask, i) for i in range(pairs)]
    hid_in, projected = [], []
    for i in range(pairs):
        hid = (mm(normed_pairs[i], in_a) * jnp.tile(masks[i], (1, PROJECTIONS))).astype(bf16)
        main = mm(normed_pairs[i], win, NT)
        projected.append(
            [
                main[:, j * wide : (j + 1) * wide] + mm(hid[:, j * RANKS : (j + 1) * RANKS], in_b_mine[j], NT)
                for j in range(PROJECTIONS)
            ]
        )
        hid_in.append(hid)
    zq, zf, zv, zg = [jnp.concatenate(pieces) for pieces in zip(*projected)]
    sigma_q = jax.nn.sigmoid(zq)
    mixed_bf, *kept = mixer_forward(
        ends, order_mine, (zq * sigma_q).astype(bf16), zf.astype(bf16), zv.astype(bf16), gap_mine
    )
    mixed = mixed_bf.astype(f32)
    sigma_g = jax.nn.sigmoid(zg)
    silu_g = zg * sigma_g
    raw = (mixed * gain_mine * silu_g).astype(bf16)
    squares = jnp.sum(mixed * mixed, axis=-1)
    sent = [with_scalars(part, [sq]) for part, sq in zip(blocks_of(raw), blocks_of(squares))]
    came = [split_scalars(packed, rows, 1) for packed in exchange(sent)]
    factor_two = lax.rsqrt(sum(sq[0] for _, sq in came) / model + eps_norm)[:, None]
    raw_own = jnp.concatenate([part for part, _ in came], axis=1).astype(f32)

    gated = (raw_own * factor_two).astype(bf16)
    hid_out = (mm(gated, out_a_mine) * mask_own).astype(bf16)
    resid = inputs + mm(gated, wout) + mm(hid_out, out_b, NT)
    factor_three = norm_factor(resid)
    normed2 = (resid * factor_three * gain_ffn).astype(bf16)

    cot_pairs = in_pairs(gather_blocks(cot_rows))
    normed2_pairs = in_pairs(gather_blocks(normed2))
    hid_ffn, d_hid_down, hidden, d_gates, d_uppers, back_parts, small_parts, down_parts = [[] for _ in range(8)]
    fold_ffn = fold_columns(3)
    for i in range(pairs):
        mask_two = jnp.tile(masks[i], (1, 2))
        hid = (mm(normed2_pairs[i], ffn_a) * mask_two).astype(bf16)
        gate = mm(normed2_pairs[i], w_gate, NT) + mm(hid[:, :RANKS], b_gate, NT)
        upper = mm(normed2_pairs[i], w_up, NT) + mm(hid[:, RANKS:], b_up, NT)
        d_hid = (mm(cot_pairs[i], down_b) * masks[i]).astype(bf16)
        d_hidden = mm(cot_pairs[i], wdown, NT) + mm(d_hid, down_a_mine, NT)
        sigma = jax.nn.sigmoid(gate)
        silu_gate = gate * sigma
        hidden.append((silu_gate * upper).astype(bf16))
        d_gates.append((d_hidden * upper * silu_slope(gate, sigma)).astype(bf16))
        d_uppers.append((d_hidden * silu_gate).astype(bf16))
        through = jnp.concatenate([mm(d_gates[i], b_gate), mm(d_uppers[i], b_up)], axis=1)
        through = (through * mask_two).astype(bf16)
        back = mm(d_gates[i], w_gate) + mm(d_uppers[i], w_up) + mm(through, ffn_a, NT)
        lowered = (mm(hidden[i], down_a_mine) * masks[i]).astype(bf16)
        down = mm(hidden[i], wdown) + mm(lowered, down_b, NT)
        small = mm(jnp.concatenate([lowered, through], axis=1), fold_ffn).astype(bf16)
        hid_ffn.append(hid)
        d_hid_down.append(d_hid)
        back_parts += [back[:rows].astype(bf16), back[rows:].astype(bf16)]
        down_parts += [down[:rows].astype(bf16), down[rows:].astype(bf16)]
        small_parts += [small[:rows], small[rows:]]
    d_normed2 = scatter_blocks(back_parts)
    d_resid = cot_rows.astype(f32) + norm_back(resid, factor_three, gain_ffn, d_normed2)

    g_attn = d_resid.astype(bf16)
    d_hid_out = (mm(g_attn, out_b) * mask_own).astype(bf16)
    d_gated = mm(g_attn, wout, NT) + mm(d_hid_out, out_a_mine, NT)
    mean_two = jnp.mean(raw_own * d_gated, axis=-1)
    sent = [
        with_scalars(d_gated[:, k * wide : (k + 1) * wide].astype(bf16), [factor_two[:, 0], mean_two])
        for k in range(n)
    ]
    came = [split_scalars(packed, rows, 2) for packed in exchange(sent)]
    d_gated_heads = jnp.concatenate([part for part, _ in came]).astype(f32)
    factor_heads = jnp.concatenate([pieces[0] for _, pieces in came])[:, None]
    mean_heads = jnp.concatenate([pieces[1] for _, pieces in came])[:, None]
    d_zg = d_gated_heads * (mixed * factor_heads * gain_mine) * silu_slope(zg, sigma_g)
    d_mixed = factor_heads * (d_gated_heads * gain_mine * silu_g) - mixed * factor_heads**3 * mean_heads

    d_query, d_forget, d_value = mixer_backward(ends, order_mine, d_mixed.astype(bf16), kept, gap_mine)
    d_zq = d_query.astype(f32) * silu_slope(zq, sigma_q)
    g_proj = [d_zq.astype(bf16), d_forget, d_value, d_zg.astype(bf16)]
    mask_four = jnp.tile(mask, (1, PROJECTIONS))
    through = jnp.concatenate([mm(g_proj[j], in_b_mine[j]) for j in range(PROJECTIONS)], axis=1)
    fold_in = fold_columns(PROJECTIONS)
    small_in = mm((through * mask_four).astype(bf16), fold_in).astype(bf16)
    small_in = jnp.concatenate(gather_direct(scatter_direct(blocks_of(small_in)).astype(bf16)))
    d_hid_in = (mm(small_in, fold_in, NT) * mask_four).astype(bf16)
    g_proj_all = jnp.concatenate(g_proj, axis=1)
    in_parts = []
    for i in range(pairs):
        back = mm(of_pair(g_proj_all, i), win)
        in_parts += [back[:rows].astype(bf16), back[rows:].astype(bf16)]
    d_normed = scatter_blocks(in_parts) + mm(d_hid_in[:rows], in_a, NT)
    tokens_grad = (d_resid + norm_back(inputs, factor_one, gain_mix, d_normed)).astype(bf16)

    block_out = (resid + scatter_blocks(down_parts)).astype(bf16)

    small_ffn = jnp.concatenate(gather_direct(scatter_direct(small_parts).astype(bf16)))
    spread = (mm(small_ffn, fold_ffn, NT) * jnp.tile(mask, (1, 3))).astype(bf16)
    hid_down, d_hid_ffn = spread[:, :RANKS], spread[:, RANKS:]

    def over_pairs(lefts, rights):
        return sum(mm(left, right, TN) for left, right in zip(lefts, rights))

    def my_features(values):
        return [my_columns(piece, wide, 1) for piece in values]

    split_pairs = lambda values: [of_pair(values, i) for i in range(pairs)]
    down_b_rows = over_pairs(my_features(cot_pairs), split_pairs(hid_down))
    ffn_a_rows = over_pairs(my_features(normed2_pairs), split_pairs(d_hid_ffn))
    down_a_rows = over_pairs(hidden, d_hid_down).reshape(wt // 2, units, RANKS)
    ffn_b_rows = jnp.concatenate(
        [
            over_pairs(d_gates, [hid[:, :RANKS] for hid in hid_ffn]),
            over_pairs(d_uppers, [hid[:, RANKS:] for hid in hid_ffn]),
        ]
    ).reshape(wt, units, RANKS)
    d_hid_out_all = jnp.concatenate(gather_direct(d_hid_out))
    gated_heads = (raw.astype(f32) * factor_heads).astype(bf16)
    out_a_rows = mm(gated_heads, d_hid_out_all, TN)
    out_b_parts = relative(mm(g_attn, hid_out, TN).reshape(n, wide, RANKS), mine)
    out_b_rows = scatter_direct([out_b_parts[k] for k in range(n)])
    in_a_rows = over_pairs(my_features(normed_pairs), split_pairs(d_hid_in))
    in_b_rows = jnp.stack(
        [
            over_pairs(split_pairs(g_proj[j]), [hid[:, j * RANKS : (j + 1) * RANKS] for hid in hid_in])
            for j in range(PROJECTIONS)
        ]
    )

    def reduced(arrays):
        packed = [
            jnp.concatenate(
                [
                    array[:, c * RANKS : (c + 1) * RANKS].reshape(wt, -1, RANKS)
                    for c in range(array.shape[1] // RANKS)
                ],
                axis=1,
            )
            for array in arrays
        ]
        summed = line_reduce(jnp.concatenate(packed, axis=1))
        results, start = [], 0
        for array in arrays:
            height = array.shape[0] // wt
            count = array.shape[1] // RANKS
            results.append(
                jnp.concatenate(
                    [summed[start + c * height : start + (c + 1) * height] for c in range(count)], axis=1
                )
            )
            start += count * height
        return results

    ffn_b_grad, down_a_grad, down_b_grad, ffn_a_grad = reduced(
        [to_rows(ffn_b_rows), to_rows(down_a_rows), down_b_rows, ffn_a_rows]
    )
    out_a_grad, out_b_grad = reduced([out_a_rows, out_b_rows])
    in_a_grad, in_b_grad = reduced([in_a_rows, to_rows(in_b_rows)])
    return (
        block_out[None],
        tokens_grad[None],
        in_a_grad,
        in_b_grad,
        out_a_grad,
        out_b_grad,
        ffn_a_grad,
        ffn_b_grad,
        down_a_grad,
        down_b_grad,
    )


def solution(mesh):
    placed = (
        P("wt", "seq", None),
        P("wt", "seq", None),
        P(None, "wt"),
        P(None, "wt"),
        P(None, "wt"),
        P(None, "wt"),
        P(),
        P(),
        P(),
        P(),
        P(),
        P(),
        P(),
        P(),
        P(),
        P(),
        P(),
        P(),
        P("wt", None),
        P("wt", None),
        P("wt", None),
    )
    return jax.shard_map(
        local,
        mesh=mesh,
        in_specs=placed,
        out_specs=(
            P("wt", "seq", None),
            P("wt", "seq", None),
            P(("seq", "wt"), None),
            P(("seq", "wt"), None),
            P(("seq", "wt"), None),
            P(("seq", "wt"), None),
            P(("seq", "wt"), None),
            P(("seq", "wt"), None),
            P(("seq", "wt"), None),
            P(("seq", "wt"), None),
        ),
        check_vma=False,
    )
```

```python
import jax
import jax.numpy as jnp
from jax import lax
from jax.sharding import PartitionSpec as P
from jax.experimental import pallas as pl
from jax.experimental.pallas import tpu as pltpu

HEAD = 128
CHUNK = 128
TILE = 512
NN = (((1,), (0,)), ((), ()))
NT = (((1,), (1,)), ((), ()))
TN = (((0,), (0,)), ((), ()))


def mm(left, right, dims=NN):
    return lax.dot_general(left, right, dims, preferred_element_type=jnp.float32)


def halves(values):
    high = values.astype(jnp.bfloat16)
    return high, (values - high.astype(jnp.float32)).astype(jnp.bfloat16)


def mm3(left, right, dims=NN):
    return mm(left[0], right[0], dims) + (mm(left[0], right[1], dims) + mm(left[1], right[0], dims))


def mm2(left, right, dims=NN):
    return mm(left[0], right, dims) + mm(left[1], right, dims)


def mm2r(left, right, dims=NN):
    return mm(left, right[0], dims) + mm(left, right[1], dims)


def sum_with(ones, values):
    high, rest = halves(values)
    mid = (values - high.astype(jnp.float32) - rest.astype(jnp.float32)).astype(jnp.bfloat16)
    return mm(ones, high) + (mm(ones, rest) + mm(ones, mid))


def move_rows(picks, pairs):
    total = pairs[0][0].shape[0]

    @pl.loop(0, total // TILE)
    def _(tile):
        start = pl.multiple_of(tile * TILE, TILE)
        chosen = picks(start, total)
        for source, target in pairs:
            target[pl.ds(start, TILE), :] = mm(chosen, source[...]).astype(jnp.bfloat16)


def picks_natural(order_row_ref):
    def picks(start, total):
        places = lax.broadcasted_iota(jnp.int32, (TILE, total), 0) + start
        return jnp.where(order_row_ref[...] == places, 1.0, 0.0).astype(jnp.bfloat16)

    return picks


def picks_packed(order_column_ref):
    def picks(start, total):
        places = lax.broadcasted_iota(jnp.int32, (TILE, total), 1)
        return jnp.where(order_column_ref[pl.ds(start, TILE), :] == places, 1.0, 0.0).astype(jnp.bfloat16)

    return picks


def segment_terms(ends_ref, start):
    count = ends_ref.shape[0] - 1

    def seg_of(positions):
        return sum((positions >= ends_ref[j]).astype(jnp.int32) for j in range(count))

    rows = lax.broadcasted_iota(jnp.int32, (CHUNK, CHUNK), 0)
    cols = lax.broadcasted_iota(jnp.int32, (CHUNK, CHUNK), 1)
    same = seg_of(rows + start) == seg_of(cols + start)
    wide = seg_of(lax.broadcasted_iota(jnp.int32, (CHUNK, HEAD), 0) + start)
    before = jnp.where(start == 0, -1, seg_of(start - 1))
    last = seg_of(start + CHUNK - 1)
    carry_ok = (wide == before).astype(jnp.float32)
    tail_ok = (wide == last).astype(jnp.float32)
    keep = (last == before).astype(jnp.float32)
    return (rows >= cols) & same, (rows <= cols) & same, carry_ok, tail_ok, keep


def chunk_decays(forget, gap, lower):
    sigma = jax.nn.sigmoid(forget)
    keys = gap * (1.0 - sigma)
    cumulative = sum_with(lower, jnp.log1p(-keys))
    middle = cumulative[CHUNK // 2 - 1 : CHUNK // 2]
    total = cumulative[CHUNK - 1 : CHUNK]
    return sigma, keys, cumulative, middle, total


def lower_ones():
    rows = lax.broadcasted_iota(jnp.int32, (CHUNK, CHUNK), 0)
    cols = lax.broadcasted_iota(jnp.int32, (CHUNK, CHUNK), 1)
    return jnp.where(rows >= cols, 1.0, 0.0).astype(jnp.bfloat16)


VMEM = pl.BlockSpec(memory_space=pltpu.VMEM)
SMEM = pl.BlockSpec(memory_space=pltpu.SMEM)
ANY = pl.BlockSpec(memory_space=pl.ANY)


def params(mebibytes):
    return pltpu.CompilerParams(vmem_limit_bytes=mebibytes * 2**20)


def cost(flops, read):
    return pl.CostEstimate(flops=int(flops), bytes_accessed=int(read), transcendentals=0)


def block_order(count):
    return list(range(0, count, 2)) + list(range(1, count, 2))


def tile_spec(rows, columns):
    return pl.BlockSpec((rows, columns), lambda i: (i, 0))


def row_to_column(row):
    size = row.shape[1]
    eye = lax.broadcasted_iota(jnp.int32, (size, size), 0) == lax.broadcasted_iota(jnp.int32, (size, size), 1)
    return jnp.sum(jnp.where(eye, row, 0.0), axis=1, keepdims=True)


def column_to_row(column):
    size = column.shape[0]
    eye = lax.broadcasted_iota(jnp.int32, (size, size), 0) == lax.broadcasted_iota(jnp.int32, (size, size), 1)
    return jnp.sum(jnp.where(eye, column, 0.0), axis=0, keepdims=True)


def packed_lines(rows_of, width):
    lines = []
    for row in rows_of:
        high, rest = halves(row)
        last = row - high.astype(jnp.float32) - rest.astype(jnp.float32)
        for part in (high.astype(jnp.float32), rest.astype(jnp.float32), last):
            lines += [part[:, i : i + width] for i in range(0, row.shape[1], width)]
    lines.append(jnp.zeros((16 - len(lines), width), jnp.float32))
    return jnp.concatenate(lines, axis=0).astype(jnp.bfloat16)


def unpacked_row(lines, which, each):
    first = 3 * each * which
    return [
        lines[first + i : first + i + 1]
        + lines[first + each + i : first + each + i + 1]
        + lines[first + 2 * each + i : first + 2 * each + i + 1]
        for i in range(each)
    ]


def line_copies(refs, place, target, sem):
    if len(refs) == 1:
        return [(None, pltpu.make_async_copy(refs[0], target(None), sem))]
    count = (len(refs) + 1) // 2
    rising, falling = refs[1:count], refs[count:]
    copies = []
    for step in range(count):
        where = lax.rem(place + step, count)
        if step == 0:
            copies.append((None, pltpu.make_async_copy(refs[0], target(where), sem)))
        else:
            up = place + step < count
            copies.append((up, pltpu.make_async_copy(falling[step - 1], target(where), sem)))
            copies.append((jnp.logical_not(up), pltpu.make_async_copy(rising[count - step - 1], target(where), sem)))
    return copies


def go(copies, what):
    for condition, copy in copies:
        if condition is None:
            getattr(copy, what)()
        else:
            pl.when(condition)(getattr(copy, what))


class Stream:
    def __init__(self, blocks):
        self.pieces = [piece for block in blocks for piece in block]
        self.shapes = [[piece.shape[0] for piece in block] for block in blocks]

    def bind(self, refs, slots, sems):
        self.refs, self.slots, self.sems = refs, slots, sems

    def copies(self, block, slot):
        first = sum(len(shape) for shape in self.shapes[:block])
        result, start = [], 0
        for i, size in enumerate(self.shapes[block]):
            result.append(
                pltpu.make_async_copy(
                    self.refs[first + i], self.slots.at[slot, pl.ds(start, size)], self.sems.at[slot, i]
                )
            )
            start += size
        return result

    def fetch(self, step):
        count = len(self.shapes)

        @pl.when(step == 0)
        def _():
            for copy in self.copies(0, 0):
                copy.start()

        for block in range(count):

            @pl.when(step == block)
            def _(block=block):
                if block + 1 < count:
                    for copy in self.copies(block + 1, (block + 1) % 2):
                        copy.start()
                for copy in self.copies(block, block % 2):
                    copy.wait()

        return self.slots[lax.rem(step, 2)]


def stream_scratch(rows, columns):
    return [pltpu.VMEM((2, rows, columns), jnp.bfloat16), pltpu.SemaphoreType.DMA((2, 2))]


def lower_kernel(stream, wide, *refs):
    mine_ref, refs = refs[0], refs[1:]
    pieces, refs = refs[: len(stream.pieces)], refs[len(stream.pieces) :]
    a_ref, mask_ref, hid_ref, mine_out_ref, slots, sems = refs
    stream.bind(pieces, slots, sems)
    step = pl.program_id(0)
    block = stream.fetch(step)
    lowered = mm(block, a_ref[...])
    mask = mask_ref[...].astype(jnp.float32)
    ranks = mask.shape[1]
    for j in range(lowered.shape[1] // ranks):
        lanes = slice(j * ranks, (j + 1) * ranks)
        hid_ref[:, lanes] = (lowered[:, lanes] * mask).astype(jnp.bfloat16)
    columns = pl.ds(pl.multiple_of(mine_ref[0] * wide, 128), wide)
    mine_out_ref[...] = slots[lax.rem(step, 2), :, columns]


def lower(mine, blocks, a_mat, mask, wide):
    stream = Stream(blocks)
    rows, columns = blocks[0][0].shape
    total = rows * len(blocks)
    ranks = a_mat.shape[1]
    return pl.pallas_call(
        lambda *refs: lower_kernel(stream, wide, *refs),
        grid=(len(blocks),),
        out_shape=(
            jax.ShapeDtypeStruct((total, ranks), jnp.bfloat16),
            jax.ShapeDtypeStruct((total, wide), jnp.bfloat16),
        ),
        in_specs=[SMEM] + [ANY] * len(stream.pieces)
        + [pl.BlockSpec(a_mat.shape, lambda i: (0, 0)), tile_spec(rows, mask.shape[1])],
        out_specs=(tile_spec(rows, ranks), tile_spec(rows, wide)),
        scratch_shapes=stream_scratch(rows, columns),
        compiler_params=params(32),
        cost_estimate=cost(2 * total * columns * ranks, 2 * total * columns),
    )(mine, *stream.pieces, a_mat, mask)


def forward_kernel(stream, win_count, *refs):
    ends_ref, mine_ref, place_ref, refs = refs[0], refs[1], refs[2], refs[3:]
    pieces, refs = refs[: len(stream.pieces)], refs[len(stream.pieces) :]
    win_pieces, refs = refs[:win_count], refs[win_count:]
    (
        order_row_ref, order_column_ref, hid_ref, b_ref, gap_ref, gain_ref,
        sent_ref, win_ref, zq_ref, zg_ref, mixed_ref, query_nat, forget_nat, value_nat, states_ref,
        query_ref, forget_ref, value_ref, out_nat, state_now, slots, sems, win_sem,
    ) = refs
    total, width = mixed_ref.shape
    heads = width // HEAD
    devices = sent_ref.shape[0]
    rows_each = total // devices
    stream.bind(pieces, slots, sems)
    win_copies = line_copies(
        win_pieces,
        place_ref[0],
        lambda w: win_ref if w is None else win_ref.at[pl.ds(pl.multiple_of(w * width, 128), width)],
        win_sem,
    )
    go(win_copies, "start")
    go(win_copies, "wait")

    @pl.loop(0, devices)
    def _(step):
        block = stream.fetch(step)
        rows = pl.ds(pl.multiple_of(step * rows_each, rows_each), rows_each)
        main = mm(block, win_ref[...], NT) + mm(hid_ref[rows, :], b_ref[...], NT)
        zq = main[:, 0:width]
        zq_ref[rows, :] = zq
        query_ref[rows, :] = (zq * jax.nn.sigmoid(zq)).astype(jnp.bfloat16)
        forget_ref[rows, :] = main[:, width : 2 * width].astype(jnp.bfloat16)
        value_ref[rows, :] = main[:, 2 * width : 3 * width].astype(jnp.bfloat16)
        zg_ref[rows, :] = main[:, 3 * width : 4 * width]

    move_rows(
        picks_natural(order_row_ref),
        ((query_ref, query_nat), (forget_ref, forget_nat), (value_ref, value_nat)),
    )
    state_now[...] = jnp.zeros_like(state_now)
    lower = lower_ones()

    @pl.loop(0, total // CHUNK)
    def _(chunk):
        start = pl.multiple_of(chunk * CHUNK, CHUNK)
        rows = pl.ds(start, CHUNK)
        allowed, _, carry_ok, tail_ok, keep = segment_terms(ends_ref, start)
        for head in range(heads):
            lanes = slice(head * HEAD, (head + 1) * HEAD)
            query = query_nat[rows, lanes].astype(jnp.float32)
            value = value_nat[rows, lanes]
            _, keys, cumulative, middle, final = chunk_decays(
                forget_nat[rows, lanes].astype(jnp.float32), gap_ref[:, lanes], lower
            )
            grown = jnp.exp(cumulative - middle)
            shrunk = jnp.exp(middle - cumulative)
            scores = mm3(halves(query * grown), halves(keys * shrunk), NT)
            scores = jnp.where(allowed, scores, 0.0)
            state = state_now[head]
            states_ref[chunk, head] = state
            inter = mm3(halves(query * jnp.exp(cumulative) * carry_ok), halves(state), NT)
            out_nat[rows, lanes] = (mm2(halves(scores), value) + inter).astype(jnp.bfloat16)
            tail = keys * jnp.exp(final - cumulative) * tail_ok
            state_now[head] = state * (jnp.exp(final) * keep) + mm2r(value, halves(tail), TN)

    states_ref[total // CHUNK] = state_now[...]
    move_rows(picks_packed(order_column_ref), ((out_nat, mixed_ref),))

    for place, bits in enumerate(block_order(devices)):
        rows = slice(place * rows_each, (place + 1) * rows_each)
        target = mine_ref[0] ^ bits
        mixed = mixed_ref[rows, :].astype(jnp.float32)
        zg = zg_ref[rows, :]
        raw = mixed * gain_ref[...] * (zg * jax.nn.sigmoid(zg))
        sent_ref[target, 0:rows_each, :] = raw.astype(jnp.bfloat16)
        squares = halves(mixed * mixed)
        ones = jnp.ones((8, width), jnp.bfloat16)
        squares = (mm(ones, squares[0], NT) + mm(ones, squares[1], NT))[0:1]
        sent_ref[target, rows_each : rows_each + 16, :] = packed_lines([squares], width)


def mixer_forward(ends, mine, place, order, blocks, win_pieces, hid_in, in_b_wide, gap, gain):
    stream = Stream(blocks)
    devices = len(blocks)
    rows_each, model = blocks[0][0].shape
    total, width = rows_each * devices, gap.shape[0]
    heads = width // HEAD
    rows = jax.ShapeDtypeStruct((total, width), jnp.bfloat16)
    wide_rows = jax.ShapeDtypeStruct((total, width), jnp.float32)
    states = jax.ShapeDtypeStruct((total // CHUNK + 1, heads, HEAD, HEAD), jnp.float32)
    sent = jax.ShapeDtypeStruct((devices, rows_each + 16, width), jnp.bfloat16)
    win = jax.ShapeDtypeStruct((4 * width, model), jnp.bfloat16)
    return pl.pallas_call(
        lambda *refs: forward_kernel(stream, len(win_pieces), *refs),
        out_shape=(sent, win, wide_rows, wide_rows, rows, rows, rows, rows, states),
        in_specs=[SMEM] * 3 + [ANY] * (len(stream.pieces) + len(win_pieces)) + [VMEM] * 6,
        out_specs=(VMEM,) * 9,
        scratch_shapes=[pltpu.VMEM((total, width), jnp.bfloat16)] * 4
        + [pltpu.VMEM((heads, HEAD, HEAD), jnp.float32)]
        + stream_scratch(rows_each, model)
        + [pltpu.SemaphoreType.DMA(())],
        compiler_params=params(56),
        cost_estimate=cost(2 * total * width * (4 * model + CHUNK * 12 + total * 4), 24 * total * width),
    )(
        ends, mine, place, *stream.pieces, *win_pieces, order.reshape(1, total), order.reshape(total, 1),
        hid_in, in_b_wide, gap.reshape(1, width), gain.reshape(1, width),
    )


def backward_kernel(
    ends_ref, mine_ref, order_row_ref, order_column_ref, came_ref, zq_ref, zg_ref, mixed_ref,
    query_nat, forget_nat, value_nat, states_ref, gap_ref, gain_ref, hid_ref, b_ref, mask_ref, fold_ref,
    g_proj_ref, gated_ref, small_ref, b_rows_ref,
    grad_ref, grad_nat, d_query_nat, d_forget_nat, d_value_nat, slope_now,
):
    total, width = mixed_ref.shape
    heads = width // HEAD
    devices = came_ref.shape[0]
    rows_each = total // devices

    for place, bits in enumerate(block_order(devices)):
        rows = slice(place * rows_each, (place + 1) * rows_each)
        source = mine_ref[0] ^ bits
        d_gated = came_ref[source, 0:rows_each, :].astype(jnp.float32)
        scalars = came_ref[source, rows_each : rows_each + 16, :].astype(jnp.float32)
        factor, mean = [
            jnp.concatenate([row_to_column(row) for row in unpacked_row(scalars, i, rows_each // width)])
            for i in range(2)
        ]
        mixed = mixed_ref[rows, :].astype(jnp.float32)
        zg = zg_ref[rows, :]
        sigma = jax.nn.sigmoid(zg)
        silu = zg * sigma
        gained = mixed * gain_ref[...]
        gated_ref[rows, :] = ((gained * silu).astype(jnp.bfloat16).astype(jnp.float32) * factor).astype(jnp.bfloat16)
        d_zg = d_gated * (gained * factor) * (sigma * (1.0 + zg * (1.0 - sigma)))
        g_proj_ref[rows, 3 * width : 4 * width] = d_zg.astype(jnp.bfloat16)
        scaled = d_gated * gain_ref[...] * silu
        cube = factor * factor * factor
        grad_ref[rows, :] = (factor * scaled - mixed * (cube * mean)).astype(jnp.bfloat16)

    move_rows(picks_natural(order_row_ref), ((grad_ref, grad_nat),))
    slope_now[...] = jnp.zeros_like(slope_now)
    lower = lower_ones()

    @pl.loop(0, total // CHUNK)
    def _(step):
        chunk = total // CHUNK - 1 - step
        start = pl.multiple_of(chunk * CHUNK, CHUNK)
        rows = pl.ds(start, CHUNK)
        allowed, later, carry_ok, tail_ok, keep = segment_terms(ends_ref, start)
        later = jnp.where(later, 1.0, 0.0).astype(jnp.bfloat16)
        for head in range(heads):
            lanes = slice(head * HEAD, (head + 1) * HEAD)
            query = query_nat[rows, lanes].astype(jnp.float32)
            value = value_nat[rows, lanes]
            grad = grad_nat[rows, lanes]
            sigma, keys, cumulative, middle, final = chunk_decays(
                forget_nat[rows, lanes].astype(jnp.float32), gap_ref[:, lanes], lower
            )
            grown = jnp.exp(cumulative - middle)
            shrunk = jnp.exp(middle - cumulative)
            query_grown = halves(query * grown)
            keys_shrunk = halves(keys * shrunk)
            scores = halves(jnp.where(allowed, mm3(query_grown, keys_shrunk, NT), 0.0))
            d_scores = halves(jnp.where(allowed, mm(grad, value, NT), 0.0))
            state = halves(states_ref[chunk, head])
            slope = slope_now[head]
            slope_parts = halves(slope)
            from_start = jnp.exp(cumulative) * carry_ok
            to_end = jnp.exp(final - cumulative) * tail_ok
            d_query = mm3(d_scores, keys_shrunk) * grown + mm2r(grad, state) * from_start
            d_keys = mm3(d_scores, query_grown, TN) * shrunk + mm2r(value, slope_parts) * to_end
            d_value = mm2(scores, grad, TN) + mm3(halves(keys * to_end), slope_parts, NT)
            past = jnp.sum(states_ref[chunk + 1, head] * slope, axis=0, keepdims=True)
            d_logf = sum_with(later, query * d_query - keys * d_keys) + tail_ok * past
            d_keys = d_keys - d_logf / (1.0 - keys)
            slope_now[head] = slope * (jnp.exp(final) * keep) + mm2r(grad, halves(query * from_start), TN)
            d_query_nat[rows, lanes] = d_query.astype(jnp.bfloat16)
            d_forget_nat[rows, lanes] = (-d_keys * keys * sigma).astype(jnp.bfloat16)
            d_value_nat[rows, lanes] = d_value.astype(jnp.bfloat16)

    picks = picks_packed(order_column_ref)

    @pl.loop(0, total // TILE)
    def _(tile):
        start = pl.multiple_of(tile * TILE, TILE)
        rows = pl.ds(start, TILE)
        chosen = picks(start, total)
        zq = zq_ref[rows, :]
        sigma = jax.nn.sigmoid(zq)
        d_query = mm(chosen, d_query_nat[...])
        g_proj_ref[rows, 0:width] = (d_query * (sigma * (1.0 + zq * (1.0 - sigma)))).astype(jnp.bfloat16)
        g_proj_ref[rows, width : 2 * width] = mm(chosen, d_forget_nat[...]).astype(jnp.bfloat16)
        g_proj_ref[rows, 2 * width : 3 * width] = mm(chosen, d_value_nat[...]).astype(jnp.bfloat16)
        mask = mask_ref[rows, :].astype(jnp.float32)
        through = mm(g_proj_ref[rows, :], b_ref[...])
        ranks = mask.shape[1]
        parts = [(through[:, j * ranks : (j + 1) * ranks] * mask).astype(jnp.bfloat16) for j in range(4)]
        small_ref[rows, :] = mm(jnp.concatenate(parts, axis=1), fold_ref[...]).astype(jnp.bfloat16)

    ranks = mask_ref.shape[1]
    for j in range(4):
        b_rows_ref[j * width : (j + 1) * width, :] = mm(
            g_proj_ref[:, j * width : (j + 1) * width], hid_ref[:, j * ranks : (j + 1) * ranks], TN
        )


def mixer_backward(ends, mine, order, came, kept, gap, gain, hid_in, in_b_wide, mask, fold):
    total, width = kept[0].shape
    ranks = mask.shape[1]
    heads = width // HEAD
    rows = jax.ShapeDtypeStruct((total, width), jnp.bfloat16)
    return pl.pallas_call(
        backward_kernel,
        out_shape=(
            jax.ShapeDtypeStruct((total, 4 * width), jnp.bfloat16),
            rows,
            jax.ShapeDtypeStruct((total, ranks), jnp.bfloat16),
            jax.ShapeDtypeStruct((4 * width, ranks), jnp.float32),
        ),
        in_specs=[SMEM] * 2 + [VMEM] * 16,
        out_specs=(VMEM,) * 4,
        scratch_shapes=[pltpu.VMEM((total, width), jnp.bfloat16)] * 5
        + [pltpu.VMEM((heads, HEAD, HEAD), jnp.float32)],
        compiler_params=params(56),
        cost_estimate=cost(2 * total * width * (CHUNK * 60 + total * 4), 30 * total * width),
    )(
        ends, mine, order.reshape(1, total), order.reshape(total, 1), came, *kept,
        gap.reshape(1, width), gain.reshape(1, width), hid_in, in_b_wide, mask, fold,
    )


def spans(blocks):
    result = []
    for index, block in enumerate(blocks):
        start = 0
        for piece in block:
            result.append((index, start, piece.shape[0]))
            start += piece.shape[0]
    return result


def token_forward_kernel(where, count, *refs):
    mine_ref, came_ref, x_ref, a_ref, b_ref, mask_ref, gain_ref = refs[:7]
    weights, refs = refs[7 : 7 + count], refs[7 + count :]
    resid_ref, normed_ref, hid_ref, all_ref, gated_ref, a_mine, sems = refs
    devices = came_ref.shape[0]
    rows, model = x_ref.shape
    width = came_ref.shape[2]
    bits = block_order(devices)
    copies = [
        pltpu.make_async_copy(weights[i], all_ref.at[pl.ds(block * width + start, size)], sems.at[i])
        for i, (block, start, size) in enumerate(where)
    ]
    for copy in copies:
        copy.start()
    squares = jnp.zeros((1, rows), jnp.float32)
    for d in range(devices):
        lines = came_ref[d, rows : rows + 16, :].astype(jnp.float32)
        squares = squares + jnp.concatenate(unpacked_row(lines, 0, rows // width), axis=1)
    factor = lax.rsqrt(row_to_column(squares) / model + eps_norm)
    for place, bit in enumerate(bits):
        source = mine_ref[0] ^ bit
        lanes = slice(place * width, (place + 1) * width)
        raw = came_ref[source, 0:rows, :].astype(jnp.float32)
        gated_ref[:, lanes] = (raw * factor).astype(jnp.bfloat16)
        a_mine[lanes, :] = a_ref[pl.ds(pl.multiple_of(source * width, 128), width), :]
    gated = gated_ref[...]
    hid = (mm(gated, a_mine[...]) * mask_ref[...].astype(jnp.float32)).astype(jnp.bfloat16)
    hid_ref[...] = hid
    extra = mm(hid, b_ref[...], NT)
    for copy in copies:
        copy.wait()
    resid = x_ref[...].astype(jnp.float32) + mm(gated, all_ref[...]) + extra
    resid_ref[...] = resid
    factor = lax.rsqrt(jnp.mean(resid * resid, axis=-1, keepdims=True) + eps_norm)
    normed_ref[...] = (resid * factor * gain_ref[...]).astype(jnp.bfloat16)


def token_forward(mine, came, x, out_a, out_b, mask_own, gain, weights):
    rows, model = x.shape
    where = spans(weights)
    pieces = [piece for block in weights for piece in block]
    ranks = out_a.shape[1]
    return pl.pallas_call(
        lambda *refs: token_forward_kernel(where, len(pieces), *refs),
        out_shape=(
            jax.ShapeDtypeStruct((rows, model), jnp.float32),
            jax.ShapeDtypeStruct((rows, model), jnp.bfloat16),
            jax.ShapeDtypeStruct((rows, ranks), jnp.bfloat16),
        ),
        in_specs=[SMEM] + [VMEM] * 6 + [ANY] * len(pieces),
        out_specs=(VMEM,) * 3,
        scratch_shapes=[
            pltpu.VMEM((model, model), jnp.bfloat16),
            pltpu.VMEM((rows, model), jnp.bfloat16),
            pltpu.VMEM((model, ranks), jnp.bfloat16),
            pltpu.SemaphoreType.DMA((len(pieces),)),
        ],
        compiler_params=params(40),
        cost_estimate=cost(2 * rows * model * model, 2 * model * model),
    )(mine, came, x, out_a, out_b, mask_own, gain.reshape(1, model), *pieces)


def summed(refs):
    own, other, from_x, from_y = refs
    total = own[...].astype(jnp.float32) + other[...].astype(jnp.float32)
    for pieces in (from_x, from_y):
        if pieces:
            total = total + jnp.concatenate([piece[...] for piece in pieces]).astype(jnp.float32)
    return total


def first_block(rows, columns):
    return pl.BlockSpec((rows, columns), lambda i: (0, 0))


def whole(array):
    return pl.BlockSpec(array.shape, lambda i: (0,) * array.ndim)


def token_backward_kernel(where, count, near, nears, *refs):
    mine_ref, came_ref, cot_ref, resid_ref, a_ref, b_ref, mask_ref, gain_ref, hid_ref, own, other = refs[:11]
    refs = refs[11:]
    from_x, from_y, refs = refs[:near], refs[near:nears], refs[nears:]
    weights, refs = refs[:count], refs[count:]
    sent_ref, d_resid_ref, d_hid_ref, b_rows_ref, all_ref, sems = refs
    devices = came_ref.shape[0]
    rows, model = resid_ref.shape
    width = came_ref.shape[2]
    copies = [
        pltpu.make_async_copy(weights[i], all_ref.at[pl.ds(block * width + start, size)], sems.at[i])
        for i, (block, start, size) in enumerate(where)
    ]
    for copy in copies:
        copy.start()
    squares = jnp.zeros((1, rows), jnp.float32)
    for d in range(devices):
        lines = came_ref[d, rows : rows + 16, :].astype(jnp.float32)
        squares = squares + jnp.concatenate(unpacked_row(lines, 0, rows // width), axis=1)
    factor_two = lax.rsqrt(squares / model + eps_norm)

    resid = resid_ref[...]
    factor = lax.rsqrt(jnp.mean(resid * resid, axis=-1, keepdims=True) + eps_norm)
    scaled = summed((own, other, from_x, from_y)) * gain_ref[...]
    mean = jnp.mean(resid * scaled, axis=-1, keepdims=True)
    d_resid = cot_ref[...].astype(jnp.float32) + factor * scaled - resid * (factor * factor * factor * mean)
    d_resid_ref[...] = d_resid
    g_attn = d_resid.astype(jnp.bfloat16)
    d_hid = (mm(g_attn, b_ref[...]) * mask_ref[...].astype(jnp.float32)).astype(jnp.bfloat16)
    d_hid_ref[...] = d_hid
    b_rows_ref[...] = mm(g_attn, hid_ref[...], TN)
    for copy in copies:
        copy.wait()
    total = jnp.zeros((rows, 1), jnp.float32)
    for place, bit in enumerate(block_order(devices)):
        target = mine_ref[0] ^ bit
        block = slice(place * width, (place + 1) * width)
        a_block = a_ref[pl.ds(pl.multiple_of(target * width, 128), width), :]
        d_gated = mm(g_attn, all_ref[block, :], NT) + mm(d_hid, a_block, NT)
        raw = came_ref[target, 0:rows, :].astype(jnp.float32)
        total = total + jnp.sum(raw * d_gated, axis=-1, keepdims=True)
        sent_ref[target, 0:rows, :] = d_gated.astype(jnp.bfloat16)
    lines = packed_lines([factor_two, column_to_row(total / model)], width)
    for d in range(devices):
        sent_ref[d, rows : rows + 16, :] = lines


def token_backward(mine, came, cot, resid, out_a, out_b, mask_own, gain, hid, parts, weights):
    rows, model = resid.shape
    own, other, from_x, from_y = parts
    where = spans(weights)
    pieces = [piece for block in weights for piece in block]
    ranks = out_a.shape[1]
    fixed = [came, cot, resid, out_a, out_b, mask_own, gain.reshape(1, model), hid]
    return pl.pallas_call(
        lambda *refs: token_backward_kernel(where, len(pieces), len(from_x), len(from_x + from_y), *refs),
        grid=(1,),
        out_shape=(
            jax.ShapeDtypeStruct(came.shape, jnp.bfloat16),
            jax.ShapeDtypeStruct((rows, model), jnp.float32),
            jax.ShapeDtypeStruct((rows, ranks), jnp.bfloat16),
            jax.ShapeDtypeStruct((model, ranks), jnp.float32),
        ),
        in_specs=[SMEM] + [whole(array) for array in fixed] + [first_block(rows, model)] * 2
        + [whole(piece) for piece in from_x + from_y] + [ANY] * len(pieces),
        out_specs=(
            pl.BlockSpec(came.shape, lambda i: (0, 0, 0)),
            first_block(rows, model),
            first_block(rows, ranks),
            first_block(model, ranks),
        ),
        scratch_shapes=[
            pltpu.VMEM((model, model), jnp.bfloat16),
            pltpu.SemaphoreType.DMA((len(pieces),)),
        ],
        compiler_params=params(56),
        cost_estimate=cost(2 * rows * model * model, 2 * model * model),
    )(mine, *fixed, own, other, *from_x, *from_y, *pieces)


def token_end_kernel(near, nears, *refs):
    x_ref, d_resid_ref, d_hid_ref, a_ref, gain_ref, own, other = refs[:7]
    refs = refs[7:]
    from_x, from_y, out_ref = refs[:near], refs[near:nears], refs[nears]
    x = x_ref[...].astype(jnp.float32)
    factor = lax.rsqrt(jnp.mean(x * x, axis=-1, keepdims=True) + eps_norm)
    d_normed = summed((own, other, from_x, from_y)) + mm(d_hid_ref[...], a_ref[...], NT)
    scaled = d_normed * gain_ref[...]
    mean = jnp.mean(x * scaled, axis=-1, keepdims=True)
    out = d_resid_ref[...] + factor * scaled - x * (factor * factor * factor * mean)
    out_ref[...] = out.astype(jnp.bfloat16)


def token_end(x, d_resid, d_hid, in_a, gain, parts):
    rows, model = x.shape
    own, other, from_x, from_y = parts
    fixed = [x, d_resid]
    return pl.pallas_call(
        lambda *refs: token_end_kernel(len(from_x), len(from_x + from_y), *refs),
        grid=(1,),
        out_shape=jax.ShapeDtypeStruct((rows, model), jnp.bfloat16),
        in_specs=[whole(x), whole(d_resid), first_block(rows, d_hid.shape[1]), whole(in_a), first_block(1, model)]
        + [first_block(rows, model)] * 2 + [whole(piece) for piece in from_x + from_y],
        out_specs=first_block(rows, model),
        compiler_params=params(40),
        cost_estimate=cost(2 * rows * model * in_a.shape[1], 16 * rows * model),
    )(x, d_resid, d_hid, in_a, gain.reshape(1, model), own, other, *from_x, *from_y)


def ffn_kernel(streams, counts, wt, *refs):
    mine_ref, place_ref, refs = refs[0], refs[1], refs[2:]
    normed_pieces, refs = refs[: len(streams[0].pieces)], refs[len(streams[0].pieces) :]
    cot_pieces, refs = refs[: len(streams[1].pieces)], refs[len(streams[1].pieces) :]
    ffn_pieces, refs = refs[: counts[0]], refs[counts[0] :]
    down_pieces, refs = refs[: counts[1]], refs[counts[1] :]
    (
        mask_ref, ffn_a_ref, b_gate_ref, b_up_ref, down_a_ref, down_b_ref, fold_ref,
        back_ref, down_ref, small_ref, normed_mine_ref, cot_mine_ref, down_a_rows, gate_rows, up_rows,
        w_both, w_down, normed_slots, normed_sems, cot_slots, cot_sems, ffn_sem, down_sem,
    ) = refs
    step = pl.program_id(0)
    streams[0].bind(normed_pieces, normed_slots, normed_sems)
    streams[1].bind(cot_pieces, cot_slots, cot_sems)
    hidden_units, model = w_down.shape
    wide = normed_mine_ref.shape[1]
    ranks = mask_ref.shape[1]
    each, narrow = 2 * hidden_units // wt, model // wt

    @pl.when(step == 0)
    def _():
        ffn = line_copies(
            ffn_pieces,
            place_ref[0],
            lambda w: w_both if w is None else w_both.at[pl.ds(pl.multiple_of(w * each, 16), each)],
            ffn_sem,
        )
        down = line_copies(
            down_pieces,
            place_ref[0],
            lambda w: w_down if w is None else w_down.at[:, pl.ds(pl.multiple_of(w * narrow, 128), narrow)],
            down_sem,
        )
        go(ffn, "start")
        go(down, "start")
        go(ffn, "wait")
        go(down, "wait")
        down_a_rows[...] = jnp.zeros_like(down_a_rows)
        gate_rows[...] = jnp.zeros_like(gate_rows)
        up_rows[...] = jnp.zeros_like(up_rows)

    normed = streams[0].fetch(step)
    cot = streams[1].fetch(step)
    slot = lax.rem(step, 2)
    columns = pl.ds(pl.multiple_of(mine_ref[0] * wide, 128), wide)
    normed_mine_ref[...] = normed_slots[slot, :, columns]
    cot_mine_ref[...] = cot_slots[slot, :, columns]
    mask = mask_ref[...].astype(jnp.float32)
    lowered = mm(normed, ffn_a_ref[...])
    hid_gate = (lowered[:, :ranks] * mask).astype(jnp.bfloat16)
    hid_up = (lowered[:, ranks:] * mask).astype(jnp.bfloat16)
    gate = mm(normed, w_both[0:hidden_units, :], NT) + mm(hid_gate, b_gate_ref[...], NT)
    upper = mm(normed, w_both[hidden_units:, :], NT) + mm(hid_up, b_up_ref[...], NT)
    sigma = jax.nn.sigmoid(gate)
    silu = gate * sigma
    hidden = (silu * upper).astype(jnp.bfloat16)
    d_hid = (mm(cot, down_b_ref[...]) * mask).astype(jnp.bfloat16)
    d_hidden = mm(cot, w_down[...], NT) + mm(d_hid, down_a_ref[...], NT)
    d_gate = (d_hidden * upper * (sigma * (1.0 + gate * (1.0 - sigma)))).astype(jnp.bfloat16)
    d_upper = (d_hidden * silu).astype(jnp.bfloat16)
    through_gate = (mm(d_gate, b_gate_ref[...]) * mask).astype(jnp.bfloat16)
    through_up = (mm(d_upper, b_up_ref[...]) * mask).astype(jnp.bfloat16)
    through = jnp.concatenate([through_gate, through_up], axis=1)
    back = mm(d_gate, w_both[0:hidden_units, :]) + mm(d_upper, w_both[hidden_units:, :])
    back_ref[...] = (back + mm(through, ffn_a_ref[...], NT)).astype(jnp.bfloat16)
    low = (mm(hidden, down_a_ref[...]) * mask).astype(jnp.bfloat16)
    down_ref[...] = (mm(hidden, w_down[...]) + mm(low, down_b_ref[...], NT)).astype(jnp.bfloat16)
    small_ref[...] = mm(jnp.concatenate([low, through], axis=1), fold_ref[...]).astype(jnp.bfloat16)
    down_a_rows[...] += mm(hidden, d_hid, TN)
    gate_rows[...] += mm(d_gate, hid_gate, TN)
    up_rows[...] += mm(d_upper, hid_up, TN)


def feed_forward(mine, place, normed, cot, ffn_pieces, down_pieces, mask, ffn_a, b_gate, b_up, down_a, down_b, fold, wide, wt):
    streams = [Stream(normed), Stream(cot)]
    rows, model = normed[0][0].shape
    blocks = len(normed)
    total = rows * blocks
    hidden_units, ranks = down_a.shape
    fixed = [ffn_a, b_gate, b_up, down_a, down_b, fold]
    grown = jax.ShapeDtypeStruct((total, model), jnp.bfloat16)
    mine_columns = jax.ShapeDtypeStruct((total, wide), jnp.bfloat16)
    term = jax.ShapeDtypeStruct((hidden_units, ranks), jnp.float32)
    return pl.pallas_call(
        lambda *refs: ffn_kernel(streams, (len(ffn_pieces), len(down_pieces)), wt, *refs),
        grid=(blocks,),
        out_shape=(
            grown, grown, jax.ShapeDtypeStruct((total, ranks), jnp.bfloat16), mine_columns, mine_columns,
            term, term, term,
        ),
        in_specs=[SMEM] * 2
        + [ANY] * (len(streams[0].pieces) + len(streams[1].pieces) + len(ffn_pieces) + len(down_pieces))
        + [tile_spec(rows, ranks)]
        + [whole(array) for array in fixed],
        out_specs=(
            tile_spec(rows, model), tile_spec(rows, model), tile_spec(rows, ranks),
            tile_spec(rows, wide), tile_spec(rows, wide),
        ) + (first_block(hidden_units, ranks),) * 3,
        scratch_shapes=[
            pltpu.VMEM((2 * hidden_units, model), jnp.bfloat16),
            pltpu.VMEM((hidden_units, model), jnp.bfloat16),
        ]
        + stream_scratch(rows, model) * 2
        + [pltpu.SemaphoreType.DMA(()), pltpu.SemaphoreType.DMA(())],
        compiler_params=params(58),
        cost_estimate=cost(14 * total * model * hidden_units, 6 * hidden_units * model + 8 * total * model),
    )(
        mine, place, *streams[0].pieces, *streams[1].pieces, *ffn_pieces, *down_pieces, mask, *fixed,
    )


def assemble_kernel(count, *refs):
    place_ref, pieces, out, sem = refs[0], refs[1 : 1 + count], refs[1 + count], refs[2 + count]
    width = pieces[0].shape[1]
    copies = line_copies(
        pieces,
        place_ref[0],
        lambda w: out if w is None else out.at[:, pl.ds(pl.multiple_of(w * width, 128), width)],
        sem,
    )
    go(copies, "start")
    go(copies, "wait")


def assemble(place, pieces, rows, columns):
    return pl.pallas_call(
        lambda *refs: assemble_kernel(len(pieces), *refs),
        out_shape=jax.ShapeDtypeStruct((rows, columns), pieces[0].dtype),
        in_specs=[SMEM] + [ANY] * len(pieces),
        out_specs=VMEM,
        scratch_shapes=[pltpu.SemaphoreType.DMA(())],
        cost_estimate=cost(0, 4 * rows * columns),
    )(place, *pieces)


ADAPTERS = 8
RANK = 16
RANKS = ADAPTERS * RANK
PROJECTIONS = 4
eps_norm = 1e-06
f32 = jnp.float32
bf16 = jnp.bfloat16


def sequence_of(positions, seq_lengths):
    bounds = jnp.cumsum(seq_lengths)[:-1]
    return jnp.sum((positions[:, None] >= bounds[None, :]).astype(jnp.int32), axis=1)


def adapter_of(seq_numbers, seq_ids):
    numbers = jnp.arange(seq_ids.shape[0], dtype=jnp.int32)
    return jnp.sum(
        (seq_numbers[:, None] == numbers[None, :]).astype(jnp.int32) * seq_ids[None, :], axis=1
    )


def adapter_mask(adapter):
    columns = jnp.arange(RANKS, dtype=jnp.int32) // RANK
    return (columns[None, :] == adapter[:, None]).astype(f32)


def norm_factor(values):
    return lax.rsqrt(jnp.mean(values * values, axis=-1, keepdims=True) + eps_norm)


def norm_back(values, factor, gain, grad):
    scaled = grad * gain
    return factor * scaled - values * factor**3 * jnp.mean(values * scaled, axis=-1, keepdims=True)


def silu_slope(values, sigma):
    return sigma * (1.0 + values * (1.0 - sigma))


def relative(blocks, index):
    count, rest = blocks.shape[0], blocks.shape[1:]
    bit = 1
    while bit < count:
        pairs = blocks.reshape((count // (2 * bit), 2, bit) + rest)
        blocks = jnp.where((index & bit) != 0, pairs[:, ::-1], pairs).reshape((count,) + rest)
        bit *= 2
    return blocks


def to_order(blocks, index):
    count = blocks.shape[0]
    blocks = relative(blocks, index)
    pairs = blocks.reshape((count // 2, 2) + blocks.shape[1:])
    return jnp.concatenate([pairs[:, 0], pairs[:, 1]])


def from_order(blocks, index):
    count = blocks.shape[0]
    pairs = jnp.stack([blocks[: count // 2], blocks[count // 2 :]], axis=1)
    return relative(pairs.reshape(blocks.shape), index)


def across(values, bits, axis="seq"):
    size = lax.axis_size(axis)
    return lax.ppermute(values, axis, [(i, i ^ bits) for i in range(size)])


def gather_near(block):
    size = lax.axis_size("seq")
    if size != 8:
        return [[block]] + [[across(block, k)] for k in range(2, size, 2)]
    half = block.shape[0] // 2
    by_x, by_y = across(block, 2), across(block, 4)
    return [[block], [by_x], [by_y], [across(by_x[:half], 4), across(by_y[half:], 2)]]


def other_core(blocks):
    return [[across(piece, 1) for piece in block] for block in blocks]


def scatter_near(near, other):
    size = lax.axis_size("seq")
    rows = near.shape[0] // (size // 2)

    def part(block, start, stop):
        at = slice(block * rows + start, block * rows + stop)
        return near[at].astype(f32) + other[at].astype(f32)

    if size != 8:
        rest = sum([across(part(i, 0, rows).astype(bf16), 2 * i).astype(f32) for i in range(1, size // 2)])
        return near, other, [rest.astype(bf16)], []
    half = rows // 2
    far_x, far_y = [part(3, i * half, (i + 1) * half).astype(bf16) for i in range(2)]
    far_x, far_y = across(far_x, 2), across(far_y, 4)
    by_x, by_y = part(1, 0, half).astype(bf16), part(2, half, rows).astype(bf16)
    by_x, by_y = across(by_x, 2), across(by_y, 4)
    by_x_more = across((part(1, half, rows) + far_y.astype(f32)).astype(bf16), 2)
    by_y_more = across((part(2, 0, half) + far_x.astype(f32)).astype(bf16), 4)
    return near, other, [by_x, by_x_more], [by_y_more, by_y]


def swap(values, axis="seq"):
    return lax.all_to_all(values, axis, split_axis=0, concat_axis=0, tiled=False)


def line_pieces(block):
    count = lax.axis_size("wt")
    rising, falling = [block], [block]
    for step in range(1, count):
        rising.append(
            lax.ppermute(rising[-1], "wt", [(i, i + 1) for i in range(step - 1, count - 1)])
        )
        falling.append(
            lax.ppermute(falling[-1], "wt", [(i, i - 1) for i in range(1, count - step + 1)])
        )
    return [block] + rising[1:] + falling[1:]


def after(values, *others):
    return lax.optimization_barrier((values,) + others)[0]


def to_owner(piece, count):
    size, lines = lax.axis_size("seq"), lax.axis_size("wt")
    each = lines // count
    moves = []
    for s in range(size):
        for q in range(lines):
            whole = (q // each) * size * each + s * each + q % each
            moves.append((s * lines + q, whole))
    return lax.ppermute(piece, ("seq", "wt"), moves)


def fold_columns(count):
    source = jnp.arange(count * RANKS)
    target = jnp.arange(RANKS)
    wanted = (source // RANKS) * RANK + source % RANK
    return (wanted[:, None] == target[None, :]).astype(bf16)


def local(
    tokens,
    cotangent,
    w_in,
    w_out,
    w_ffn,
    w_down,
    gain_mix,
    gain_gate,
    gain_ffn,
    forget_gap,
    in_a,
    in_b,
    out_a,
    out_b,
    ffn_a,
    ffn_b,
    down_a,
    down_b,
    order,
    lengths,
    adapter_ids,
):
    n, wt = lax.axis_size("seq"), lax.axis_size("wt")
    mine = lax.axis_index("seq")
    mine_ref = mine.astype(jnp.int32).reshape(1)
    place_ref = lax.axis_index("wt").astype(jnp.int32).reshape(1)
    x_rows = tokens[0]
    cot_rows = cotangent[0]
    rows, model = x_rows.shape
    total = n * rows
    wide = model // n
    half = total // 2
    units = w_ffn.shape[1] // n
    hidden_units = wt // 2 * units
    on_line = wt == PROJECTIONS and n == 8

    def my_columns(values, extent, axis):
        return lax.dynamic_slice_in_dim(values, mine * extent, extent, axis)

    def my_piece(values, axis):
        return lax.dynamic_index_in_dim(values, mine, axis, False)

    if on_line:
        win_pieces = line_pieces(my_columns(w_in, wide, 1).T)
        w_out = after(w_out, win_pieces[2])
    else:
        spread_in = lax.all_gather(w_in, "wt", axis=1, tiled=True)
        spread_in = my_piece(spread_in.reshape(model, PROJECTIONS, n, wide), 2)
        win_pieces = [jnp.transpose(spread_in, (1, 2, 0)).reshape(PROJECTIONS * wide, model)]

    order_mine = to_order(order[0].reshape(n, rows), mine).reshape(total)
    ends = jnp.cumsum(lengths[0])
    mask = adapter_mask(adapter_of(sequence_of(order_mine, lengths[0]), adapter_ids[0])).astype(bf16)
    mask_own = mask[:rows]
    gap_mine = my_columns(forget_gap, wide, 0)
    gain_mine = my_columns(gain_gate, wide, 0)
    in_b_mine = my_piece(in_b.reshape(PROJECTIONS, n, wide, RANKS), 1)
    in_b_wide = jnp.concatenate(
        [jnp.pad(in_b_mine[j], ((0, 0), (j * RANKS, (PROJECTIONS - 1 - j) * RANKS))) for j in range(PROJECTIONS)]
    )
    fold_in, fold_ffn = fold_columns(PROJECTIONS), fold_columns(3)

    inputs = x_rows.astype(f32)
    normed = (inputs * norm_factor(inputs) * gain_mix).astype(bf16)
    normed_near = gather_near(normed)
    normed_blocks = normed_near + other_core(normed_near)
    hid_in, normed_mine = lower(mine_ref, normed_blocks, in_a, mask, wide)

    cot_near = gather_near(after(cot_rows, normed_near[1][0]))
    cot_other = other_core(cot_near)

    sent, win, *kept = mixer_forward(
        ends, mine_ref, place_ref, order_mine, normed_blocks, win_pieces, hid_in, in_b_wide, gap_mine, gain_mine
    )

    if on_line:
        wout_pieces = line_pieces(my_columns(w_out, wide, 0))
        w_ffn, w_down = after((w_ffn, w_down), wout_pieces[2])
        ffn_pieces = line_pieces(my_columns(w_ffn, units, 1).T)
        w_down = after(w_down, ffn_pieces[2])
        down_pieces = my_piece(w_down.reshape(wt // 2, n, units, -1), 1).reshape(hidden_units, -1)
        down_pieces = line_pieces(down_pieces)
    else:
        wout_pieces = [lax.all_gather(my_columns(w_out, wide, 0), "wt", axis=1, tiled=True)]
        ffn_pieces = [lax.all_gather(my_columns(w_ffn, units, 1).T, "wt", axis=0, tiled=True)]
        down_pieces = my_piece(w_down.reshape(wt // 2, n, units, -1), 1).reshape(hidden_units, -1)
        down_pieces = [lax.all_gather(down_pieces, "wt", axis=1, tiled=True)]
    wout_near = gather_near(assemble(place_ref, wout_pieces, wide, model))
    wout_blocks = wout_near + other_core(wout_near)
    ffn_b_mine = my_piece(ffn_b.reshape(wt, n, units, RANKS), 1)
    b_gate = ffn_b_mine[: wt // 2].reshape(-1, RANKS)
    b_up = ffn_b_mine[wt // 2 :].reshape(-1, RANKS)
    down_a_mine = my_piece(down_a.reshape(wt // 2, n, units, RANKS), 1).reshape(-1, RANKS)

    came = swap(sent)
    resid, normed2, hid_out = token_forward(
        mine_ref, came, x_rows, out_a, out_b, mask_own, gain_ffn, wout_blocks
    )

    normed2_near = gather_near(normed2)
    ffn_args = (ffn_pieces, down_pieces)
    ffn_rest = (ffn_a, b_gate, b_up, down_a_mine, down_b, fold_ffn, wide, wt)
    sides = []
    for blocks, cots, masks in (
        (other_core(normed2_near), cot_other, mask[half:]),
        (normed2_near, cot_near, mask[:half]),
    ):
        sides.append(feed_forward(mine_ref, place_ref, blocks, cots, *ffn_args, masks, *ffn_rest))
    back_far, down_far, small_far, *rest_far = sides[0]
    back, down, small, *rest = sides[1]
    parts = scatter_near(back, across(back_far, 1))
    d_sent, d_resid, d_hid_out, out_b_part = token_backward(
        mine_ref, came, cot_rows, resid, out_a, out_b, mask_own, gain_ffn, hid_out, parts, wout_blocks
    )

    g_proj, gated_heads, small_in, in_b_rows = mixer_backward(
        ends, mine_ref, order_mine, swap(d_sent), kept, gap_mine, gain_mine, hid_in, in_b_wide, mask, fold_in
    )
    back_in_far = across(mm(g_proj[half:], win).astype(bf16), 1)
    back_in = mm(g_proj[:half], win).astype(bf16)
    parts_in = scatter_near(back_in, back_in_far)
    small_in = jnp.sum(swap(from_order(small_in.reshape(n, rows, RANKS), mine)).astype(f32), axis=0).astype(bf16)
    small_in = swap(jnp.broadcast_to(small_in, (n, rows, RANKS)))
    small_in = to_order(small_in, mine).reshape(total, RANKS)
    d_hid_in = (mm(small_in, fold_in, NT) * jnp.tile(mask, (1, PROJECTIONS))).astype(bf16)
    tokens_grad = token_end(x_rows, d_resid, d_hid_in, in_a, gain_mix, parts_in)

    near, other, from_x, from_y = scatter_near(down, across(down_far, 1))
    block_out = resid + near[:rows].astype(f32) + other[:rows].astype(f32)
    for pieces in (from_x, from_y):
        if pieces:
            block_out = block_out + jnp.concatenate(pieces).astype(f32)
    block_out = block_out.astype(bf16)

    small_ffn = jnp.concatenate([small, small_far]).reshape(n, rows, RANKS)
    small_ffn = jnp.sum(swap(from_order(small_ffn, mine)).astype(f32), axis=0).astype(bf16)
    small_ffn = to_order(lax.all_gather(small_ffn, "seq", axis=0), mine).reshape(total, RANKS)
    spread = (mm(small_ffn, fold_ffn, NT) * jnp.tile(mask, (1, 3))).astype(bf16)
    hid_down, d_hid_ffn = spread[:, :RANKS], spread[:, RANKS:]
    normed2_mine, cot_mine = [jnp.concatenate([rest[i], rest_far[i]]) for i in range(2)]
    down_a_rows, gate_rows, up_rows = [rest[i] + rest_far[i] for i in range(2, 5)]
    down_b_rows = mm(cot_mine, hid_down, TN)
    ffn_a_rows = mm(normed2_mine, d_hid_ffn, TN)
    ffn_b_rows = jnp.concatenate([gate_rows, up_rows])
    d_hid_out_all = to_order(lax.all_gather(d_hid_out, "seq", axis=0), mine).reshape(total, RANKS)
    out_a_rows = mm(gated_heads, d_hid_out_all, TN)
    out_b_rows = lax.psum_scatter(out_b_part, "seq", scatter_dimension=0, tiled=True)
    in_a_rows = mm(normed_mine, d_hid_in, TN)

    def reduced(arrays, how):
        packed = [
            jnp.concatenate(
                [
                    array[:, c * RANKS : (c + 1) * RANKS].reshape(wt, -1, RANKS)
                    for c in range(array.shape[1] // RANKS)
                ],
                axis=1,
            )
            for array in arrays
        ]
        summed = how(jnp.concatenate(packed, axis=1))
        results, start = [], 0
        for array in arrays:
            height = array.shape[0] // wt
            count = array.shape[1] // RANKS
            results.append(
                jnp.concatenate(
                    [summed[start + c * height : start + (c + 1) * height] for c in range(count)], axis=1
                )
            )
            start += count * height
        return results

    def by_offload(values):
        return lax.psum_scatter(values, "wt", scatter_dimension=0, tiled=False)

    def by_swap(values):
        return jnp.sum(swap(values, "wt"), axis=0)

    ffn_b_grad, down_a_grad, down_b_grad, ffn_a_grad = reduced(
        [ffn_b_rows, down_a_rows, down_b_rows, ffn_a_rows], by_offload
    )
    out_a_grad, out_b_grad, in_a_grad, in_b_grad = reduced(
        [out_a_rows, out_b_rows, in_a_rows, in_b_rows], by_swap
    )
    return (
        block_out[None],
        tokens_grad[None],
        in_a_grad,
        to_owner(in_b_grad, PROJECTIONS),
        out_a_grad,
        out_b_grad,
        ffn_a_grad,
        to_owner(ffn_b_grad, wt),
        to_owner(down_a_grad, wt // 2),
        down_b_grad,
    )


def solution(mesh):
    placed = (
        P("wt", "seq", None),
        P("wt", "seq", None),
        P(None, "wt"),
        P(None, "wt"),
        P(None, "wt"),
        P(None, "wt"),
        P(),
        P(),
        P(),
        P(),
        P(),
        P(),
        P(),
        P(),
        P(),
        P(),
        P(),
        P(),
        P("wt", None),
        P("wt", None),
        P("wt", None),
    )
    return jax.shard_map(
        local,
        mesh=mesh,
        in_specs=placed,
        out_specs=(
            P("wt", "seq", None),
            P("wt", "seq", None),
            P(("seq", "wt"), None),
            P(("seq", "wt"), None),
            P(("seq", "wt"), None),
            P(("seq", "wt"), None),
            P(("seq", "wt"), None),
            P(("seq", "wt"), None),
            P(("seq", "wt"), None),
            P(("seq", "wt"), None),
        ),
        check_vma=False,
    )
```

```python
import jax
import jax.numpy as jnp
from jax import lax
from jax.sharding import PartitionSpec as P
from jax.experimental import pallas as pl
from jax.experimental.pallas import tpu as pltpu

HEAD = 128
CHUNK = 128
TILE = 512
NN = (((1,), (0,)), ((), ()))
NT = (((1,), (1,)), ((), ()))
TN = (((0,), (0,)), ((), ()))


def mm(left, right, dims=NN):
    return lax.dot_general(left, right, dims, preferred_element_type=jnp.float32)


def halves(values):
    high = values.astype(jnp.bfloat16)
    return high, (values - high.astype(jnp.float32)).astype(jnp.bfloat16)


def mm3(left, right, dims=NN):
    return mm(left[0], right[0], dims) + (mm(left[0], right[1], dims) + mm(left[1], right[0], dims))


def mm2(left, right, dims=NN):
    return mm(left[0], right, dims) + mm(left[1], right, dims)


def mm2r(left, right, dims=NN):
    return mm(left, right[0], dims) + mm(left, right[1], dims)


def sum_with(ones, values):
    high, rest = halves(values)
    mid = (values - high.astype(jnp.float32) - rest.astype(jnp.float32)).astype(jnp.bfloat16)
    return mm(ones, high) + (mm(ones, rest) + mm(ones, mid))


def move_rows(picks, pairs):
    total = pairs[0][0].shape[0]

    @pl.loop(0, total // TILE)
    def _(tile):
        start = pl.multiple_of(tile * TILE, TILE)
        chosen = picks(start, total)
        for source, target in pairs:
            target[pl.ds(start, TILE), :] = mm(chosen, source[...]).astype(jnp.bfloat16)


def picks_natural(order_row_ref):
    def picks(start, total):
        places = lax.broadcasted_iota(jnp.int32, (TILE, total), 0) + start
        return jnp.where(order_row_ref[...] == places, 1.0, 0.0).astype(jnp.bfloat16)

    return picks


def picks_packed(order_column_ref):
    def picks(start, total):
        places = lax.broadcasted_iota(jnp.int32, (TILE, total), 1)
        return jnp.where(order_column_ref[pl.ds(start, TILE), :] == places, 1.0, 0.0).astype(jnp.bfloat16)

    return picks


def segment_terms(ends_ref, start):
    count = ends_ref.shape[0] - 1

    def seg_of(positions):
        return sum((positions >= ends_ref[j]).astype(jnp.int32) for j in range(count))

    rows = lax.broadcasted_iota(jnp.int32, (CHUNK, CHUNK), 0)
    cols = lax.broadcasted_iota(jnp.int32, (CHUNK, CHUNK), 1)
    same = seg_of(rows + start) == seg_of(cols + start)
    wide = seg_of(lax.broadcasted_iota(jnp.int32, (CHUNK, HEAD), 0) + start)
    before = jnp.where(start == 0, -1, seg_of(start - 1))
    last = seg_of(start + CHUNK - 1)
    carry_ok = (wide == before).astype(jnp.float32)
    tail_ok = (wide == last).astype(jnp.float32)
    keep = (last == before).astype(jnp.float32)
    return (rows >= cols) & same, (rows <= cols) & same, carry_ok, tail_ok, keep


def chunk_decays(forget, gap, lower):
    sigma = jax.nn.sigmoid(forget)
    keys = gap * (1.0 - sigma)
    cumulative = sum_with(lower, jnp.log1p(-keys))
    middle = cumulative[CHUNK // 2 - 1 : CHUNK // 2]
    total = cumulative[CHUNK - 1 : CHUNK]
    return sigma, keys, cumulative, middle, total


def lower_ones():
    rows = lax.broadcasted_iota(jnp.int32, (CHUNK, CHUNK), 0)
    cols = lax.broadcasted_iota(jnp.int32, (CHUNK, CHUNK), 1)
    return jnp.where(rows >= cols, 1.0, 0.0).astype(jnp.bfloat16)


VMEM = pl.BlockSpec(memory_space=pltpu.VMEM)
SMEM = pl.BlockSpec(memory_space=pltpu.SMEM)
ANY = pl.BlockSpec(memory_space=pl.ANY)


def params(mebibytes):
    return pltpu.CompilerParams(vmem_limit_bytes=mebibytes * 2**20)


def cost(tera_ops):
    return pl.CostEstimate(flops=int(tera_ops * 1e9), bytes_accessed=0, transcendentals=0)


def block_order(count):
    return list(range(0, count, 2)) + list(range(1, count, 2))


def tile_spec(rows, columns):
    return pl.BlockSpec((rows, columns), lambda i: (i, 0))


def row_to_column(row):
    size = row.shape[1]
    eye = lax.broadcasted_iota(jnp.int32, (size, size), 0) == lax.broadcasted_iota(jnp.int32, (size, size), 1)
    return jnp.sum(jnp.where(eye, row, 0.0), axis=1, keepdims=True)


def column_to_row(column):
    size = column.shape[0]
    eye = lax.broadcasted_iota(jnp.int32, (size, size), 0) == lax.broadcasted_iota(jnp.int32, (size, size), 1)
    return jnp.sum(jnp.where(eye, column, 0.0), axis=0, keepdims=True)


def packed_lines(rows_of, width):
    lines = []
    for row in rows_of:
        high, rest = halves(row)
        last = row - high.astype(jnp.float32) - rest.astype(jnp.float32)
        for part in (high.astype(jnp.float32), rest.astype(jnp.float32), last):
            lines += [part[:, i : i + width] for i in range(0, row.shape[1], width)]
    lines.append(jnp.zeros((16 - len(lines), width), jnp.float32))
    return jnp.concatenate(lines, axis=0).astype(jnp.bfloat16)


def unpacked_row(lines, which, each):
    first = 3 * each * which
    return [
        lines[first + i : first + i + 1]
        + lines[first + each + i : first + each + i + 1]
        + lines[first + 2 * each + i : first + 2 * each + i + 1]
        for i in range(each)
    ]


def window(ref, start, size):
    return ref.at[pl.ds(start, size)]


def windows(pieces, refs):
    return [window(ref, start, size) for ref, (_, start, size) in zip(refs, pieces)]


def arrays_of(pieces):
    return [array for array, _, _ in pieces]


def line_copies(refs, place, target, sem):
    if len(refs) == 1:
        return [(None, pltpu.make_async_copy(refs[0], target(None), sem))]
    own, up, down, a, b, c = refs
    held = ((own, down, b, c), (up, own, down, a), (a, up, own, down), (c, b, up, own))
    return [
        (place == p, pltpu.make_async_copy(ref, target(w), sem))
        for p, entries in enumerate(held)
        for w, ref in enumerate(entries)
    ]


def go(copies, what):
    for condition, copy in copies:
        if condition is None:
            getattr(copy, what)()
        else:
            pl.when(condition)(getattr(copy, what))


class Stream:
    def __init__(self, blocks):
        self.pieces = [piece for block in blocks for piece in block]
        self.arrays = arrays_of(self.pieces)
        self.blocks = [len(block) for block in blocks]
        self.rows = sum(size for _, _, size in blocks[0])

    def bind(self, refs, slots, sems):
        self.refs, self.slots, self.sems = windows(self.pieces, refs), slots, sems

    def copies(self, block, slot):
        first = sum(self.blocks[:block])
        result, start = [], 0
        for i in range(self.blocks[block]):
            size = self.pieces[first + i][2]
            result.append(
                pltpu.make_async_copy(
                    self.refs[first + i], self.slots.at[slot, pl.ds(start, size)], self.sems.at[slot, i]
                )
            )
            start += size
        return result

    def fetch(self, step):
        count = len(self.blocks)

        @pl.when(step == 0)
        def _():
            for copy in self.copies(0, 0):
                copy.start()

        for block in range(count):

            @pl.when(step == block)
            def _(block=block):
                if block + 1 < count:
                    for copy in self.copies(block + 1, (block + 1) % 2):
                        copy.start()
                for copy in self.copies(block, block % 2):
                    copy.wait()

        return self.slots[lax.rem(step, 2)]


def stream_scratch(rows, columns):
    return [pltpu.VMEM((2, rows, columns), jnp.bfloat16), pltpu.SemaphoreType.DMA((2, 2))]


def projection_copies(refs, place, target, sem):
    def at(w):
        rows = refs[0].shape[0] if w is None else refs[0].shape[0] * w
        return target.at[pl.ds(0, rows)] if w is None else target.at[pl.ds(rows, refs[0].shape[0])]

    return line_copies(refs, place, at, sem)


def forward_kernel(stream, win_pieces, *refs):
    ends_ref, mine_ref, place_ref, refs = refs[0], refs[1], refs[2], refs[3:]
    pieces, refs = refs[: len(stream.pieces)], refs[len(stream.pieces) :]
    win_refs, refs = refs[: len(win_pieces)], refs[len(win_pieces) :]
    (
        order_row_ref, order_column_ref, a_ref, b_ref, mask_ref, gap_ref, gain_ref,
        sent_ref, hid_ref, normed_mine_ref, zq_ref, zg_ref, mixed_ref, query_nat, forget_nat, value_nat, states_ref,
        query_ref, forget_ref, value_ref, out_nat, state_now, win_ref, slots, sems, win_sem,
    ) = refs
    total, width = mixed_ref.shape
    heads = width // HEAD
    devices = sent_ref.shape[0]
    rows_each = total // devices
    stream.bind(pieces, slots, sems)
    win_copies = projection_copies(windows(win_pieces, win_refs), place_ref[0], win_ref, win_sem)
    go(win_copies, "start")
    win_ref[4 * width :, :] = a_ref[...]
    columns = pl.ds(pl.multiple_of(mine_ref[0] * width, 128), width)
    ranks = mask_ref.shape[1]
    go(win_copies, "wait")

    @pl.loop(0, devices)
    def _(step):
        block = stream.fetch(step)
        rows = pl.ds(pl.multiple_of(step * rows_each, rows_each), rows_each)
        normed_mine_ref[rows, :] = slots[lax.rem(step, 2), :, columns]
        main = mm(block, win_ref[...], NT)
        mask = mask_ref[rows, :].astype(jnp.float32)
        for j in range(4):
            lowered = main[:, 4 * width + j * ranks : 4 * width + (j + 1) * ranks] * mask
            hid_ref[rows, j * ranks : (j + 1) * ranks] = lowered.astype(jnp.bfloat16)
        main = main[:, : 4 * width] + mm(hid_ref[rows, :], b_ref[...], NT)
        zq = main[:, 0:width]
        zq_ref[rows, :] = zq
        query_ref[rows, :] = (zq * jax.nn.sigmoid(zq)).astype(jnp.bfloat16)
        forget_ref[rows, :] = main[:, width : 2 * width].astype(jnp.bfloat16)
        value_ref[rows, :] = main[:, 2 * width : 3 * width].astype(jnp.bfloat16)
        zg_ref[rows, :] = main[:, 3 * width : 4 * width]

    move_rows(
        picks_natural(order_row_ref),
        ((query_ref, query_nat), (forget_ref, forget_nat), (value_ref, value_nat)),
    )
    state_now[...] = jnp.zeros_like(state_now)
    lower = lower_ones()

    @pl.loop(0, total // CHUNK, unroll=2)
    def _(chunk):
        start = pl.multiple_of(chunk * CHUNK, CHUNK)
        rows = pl.ds(start, CHUNK)
        allowed, _, carry_ok, tail_ok, keep = segment_terms(ends_ref, start)
        for head in range(heads):
            lanes = slice(head * HEAD, (head + 1) * HEAD)
            query = query_nat[rows, lanes].astype(jnp.float32)
            value = value_nat[rows, lanes]
            _, keys, cumulative, middle, final = chunk_decays(
                forget_nat[rows, lanes].astype(jnp.float32), gap_ref[:, lanes], lower
            )
            grown = jnp.exp(cumulative - middle)
            shrunk = jnp.exp(middle - cumulative)
            scores = mm3(halves(query * grown), halves(keys * shrunk), NT)
            scores = jnp.where(allowed, scores, 0.0)
            state = state_now[head]
            states_ref[chunk, head] = state
            inter = mm3(halves(query * jnp.exp(cumulative) * carry_ok), halves(state), NT)
            out_nat[rows, lanes] = (mm2(halves(scores), value) + inter).astype(jnp.bfloat16)
            tail = keys * jnp.exp(final - cumulative) * tail_ok
            state_now[head] = state * (jnp.exp(final) * keep) + mm2r(value, halves(tail), TN)

    states_ref[total // CHUNK] = state_now[...]
    move_rows(picks_packed(order_column_ref), ((out_nat, mixed_ref),))

    for place, bits in enumerate(block_order(devices)):
        rows = slice(place * rows_each, (place + 1) * rows_each)
        target = mine_ref[0] ^ bits
        mixed = mixed_ref[rows, :].astype(jnp.float32)
        zg = zg_ref[rows, :]
        raw = mixed * gain_ref[...] * (zg * jax.nn.sigmoid(zg))
        sent_ref[target, 0:rows_each, :] = raw.astype(jnp.bfloat16)
        squares = halves(mixed * mixed)
        ones = jnp.ones((8, width), jnp.bfloat16)
        squares = (mm(ones, squares[0], NT) + mm(ones, squares[1], NT))[0:1]
        sent_ref[target, rows_each : rows_each + 16, :] = packed_lines([squares], width)


def mixer_forward(ends, mine, place, order, blocks, win_pieces, in_a_t, in_b_wide, mask, gap, gain):
    stream = Stream(blocks)
    devices = len(blocks)
    model = in_a_t.shape[1]
    total, width = stream.rows * devices, gap.shape[0]
    heads = width // HEAD
    ranks = mask.shape[1]
    rows = jax.ShapeDtypeStruct((total, width), jnp.bfloat16)
    wide_rows = jax.ShapeDtypeStruct((total, width), jnp.float32)
    states = jax.ShapeDtypeStruct((total // CHUNK + 1, heads, HEAD, HEAD), jnp.float32)
    sent = jax.ShapeDtypeStruct((devices, stream.rows + 16, width), jnp.bfloat16)
    hid = jax.ShapeDtypeStruct((total, 4 * ranks), jnp.bfloat16)
    return pl.pallas_call(
        lambda *refs: forward_kernel(stream, win_pieces, *refs),
        out_shape=(sent, hid, rows, wide_rows, wide_rows, rows, rows, rows, rows, states),
        in_specs=[SMEM] * 3 + [ANY] * (len(stream.pieces) + len(win_pieces)) + [VMEM] * 7,
        out_specs=(VMEM,) * 10,
        scratch_shapes=[pltpu.VMEM((total, width), jnp.bfloat16)] * 4
        + [pltpu.VMEM((heads, HEAD, HEAD), jnp.float32), pltpu.VMEM((4 * (width + ranks), model), jnp.bfloat16)]
        + stream_scratch(stream.rows, model)
        + [pltpu.SemaphoreType.DMA(())],
        compiler_params=params(62),
        cost_estimate=cost(57),
    )(
        ends, mine, place, *stream.arrays, *arrays_of(win_pieces), *order,
        in_a_t, in_b_wide, mask, gap.reshape(1, width), gain.reshape(1, width),
    )


def backward_kernel(
    ends_ref, mine_ref, order_row_ref, order_column_ref, came_ref, zq_ref, zg_ref, mixed_ref,
    query_nat, forget_nat, value_nat, states_ref, gap_ref, gain_ref, hid_ref, b_ref, mask_ref, fold_ref,
    g_proj_ref, gated_ref, small_ref, b_rows_ref,
    grad_ref, grad_nat, d_query_nat, d_forget_nat, d_value_nat, slope_now,
):
    total, width = mixed_ref.shape
    heads = width // HEAD
    devices = came_ref.shape[0]
    rows_each = total // devices

    for place, bits in enumerate(block_order(devices)):
        rows = slice(place * rows_each, (place + 1) * rows_each)
        source = mine_ref[0] ^ bits
        d_gated = came_ref[source, 0:rows_each, :].astype(jnp.float32)
        scalars = came_ref[source, rows_each : rows_each + 16, :].astype(jnp.float32)
        factor, mean = [
            jnp.concatenate([row_to_column(row) for row in unpacked_row(scalars, i, rows_each // width)])
            for i in range(2)
        ]
        mixed = mixed_ref[rows, :].astype(jnp.float32)
        zg = zg_ref[rows, :]
        sigma = jax.nn.sigmoid(zg)
        silu = zg * sigma
        gained = mixed * gain_ref[...]
        gated_ref[rows, :] = ((gained * silu).astype(jnp.bfloat16).astype(jnp.float32) * factor).astype(jnp.bfloat16)
        d_zg = d_gated * (gained * factor) * (sigma * (1.0 + zg * (1.0 - sigma)))
        g_proj_ref[rows, 3 * width : 4 * width] = d_zg.astype(jnp.bfloat16)
        scaled = d_gated * gain_ref[...] * silu
        cube = factor * factor * factor
        grad_ref[rows, :] = (factor * scaled - mixed * (cube * mean)).astype(jnp.bfloat16)

    move_rows(picks_natural(order_row_ref), ((grad_ref, grad_nat),))
    slope_now[...] = jnp.zeros_like(slope_now)
    lower = lower_ones()

    @pl.loop(0, total // CHUNK, unroll=2)
    def _(step):
        chunk = total // CHUNK - 1 - step
        start = pl.multiple_of(chunk * CHUNK, CHUNK)
        rows = pl.ds(start, CHUNK)
        allowed, later, carry_ok, tail_ok, keep = segment_terms(ends_ref, start)
        later = jnp.where(later, 1.0, 0.0).astype(jnp.bfloat16)
        for head in range(heads):
            lanes = slice(head * HEAD, (head + 1) * HEAD)
            query = query_nat[rows, lanes].astype(jnp.float32)
            value = value_nat[rows, lanes]
            grad = grad_nat[rows, lanes]
            sigma, keys, cumulative, middle, final = chunk_decays(
                forget_nat[rows, lanes].astype(jnp.float32), gap_ref[:, lanes], lower
            )
            grown = jnp.exp(cumulative - middle)
            shrunk = jnp.exp(middle - cumulative)
            query_grown = halves(query * grown)
            keys_shrunk = halves(keys * shrunk)
            scores = halves(jnp.where(allowed, mm3(query_grown, keys_shrunk, NT), 0.0))
            d_scores = halves(jnp.where(allowed, mm(grad, value, NT), 0.0))
            state = halves(states_ref[chunk, head])
            slope = slope_now[head]
            slope_parts = halves(slope)
            from_start = jnp.exp(cumulative) * carry_ok
            to_end = jnp.exp(final - cumulative) * tail_ok
            d_query = mm3(d_scores, keys_shrunk) * grown + mm2r(grad, state) * from_start
            d_keys = mm3(d_scores, query_grown, TN) * shrunk + mm2r(value, slope_parts) * to_end
            d_value = mm2(scores, grad, TN) + mm3(halves(keys * to_end), slope_parts, NT)
            past = jnp.sum(states_ref[chunk + 1, head] * slope, axis=0, keepdims=True)
            d_logf = sum_with(later, query * d_query - keys * d_keys) + tail_ok * past
            d_keys = d_keys - d_logf / (1.0 - keys)
            slope_now[head] = slope * (jnp.exp(final) * keep) + mm2r(grad, halves(query * from_start), TN)
            d_query_nat[rows, lanes] = d_query.astype(jnp.bfloat16)
            d_forget_nat[rows, lanes] = (-d_keys * keys * sigma).astype(jnp.bfloat16)
            d_value_nat[rows, lanes] = d_value.astype(jnp.bfloat16)

    picks = picks_packed(order_column_ref)

    @pl.loop(0, total // TILE)
    def _(tile):
        start = pl.multiple_of(tile * TILE, TILE)
        rows = pl.ds(start, TILE)
        chosen = picks(start, total)
        zq = zq_ref[rows, :]
        sigma = jax.nn.sigmoid(zq)
        d_query = mm(chosen, d_query_nat[...])
        g_proj_ref[rows, 0:width] = (d_query * (sigma * (1.0 + zq * (1.0 - sigma)))).astype(jnp.bfloat16)
        g_proj_ref[rows, width : 2 * width] = mm(chosen, d_forget_nat[...]).astype(jnp.bfloat16)
        g_proj_ref[rows, 2 * width : 3 * width] = mm(chosen, d_value_nat[...]).astype(jnp.bfloat16)
        mask = mask_ref[rows, :].astype(jnp.float32)
        through = mm(g_proj_ref[rows, :], b_ref[...])
        ranks = mask.shape[1]
        parts = [(through[:, j * ranks : (j + 1) * ranks] * mask).astype(jnp.bfloat16) for j in range(4)]
        small_ref[rows, :] = mm(jnp.concatenate(parts, axis=1), fold_ref[...]).astype(jnp.bfloat16)

    ranks = mask_ref.shape[1]
    for j in range(4):
        b_rows_ref[j * width : (j + 1) * width, :] = mm(
            g_proj_ref[:, j * width : (j + 1) * width], hid_ref[:, j * ranks : (j + 1) * ranks], TN
        )


def mixer_backward(ends, mine, order, came, kept, gap, gain, hid_in, in_b_wide, mask, fold):
    total, width = kept[0].shape
    ranks = mask.shape[1]
    heads = width // HEAD
    rows = jax.ShapeDtypeStruct((total, width), jnp.bfloat16)
    return pl.pallas_call(
        backward_kernel,
        out_shape=(
            jax.ShapeDtypeStruct((total, 4 * width), jnp.bfloat16),
            rows,
            jax.ShapeDtypeStruct((total, ranks), jnp.bfloat16),
            jax.ShapeDtypeStruct((4 * width, ranks), jnp.float32),
        ),
        in_specs=[SMEM] * 2 + [VMEM] * 16,
        out_specs=(VMEM,) * 4,
        scratch_shapes=[pltpu.VMEM((total, width), jnp.bfloat16)] * 5
        + [pltpu.VMEM((heads, HEAD, HEAD), jnp.float32)],
        compiler_params=params(62),
        cost_estimate=cost(51),
    )(
        ends, mine, *order, came, *kept,
        gap.reshape(1, width), gain.reshape(1, width), hid_in, in_b_wide, mask, fold,
    )


def spans(blocks):
    result = []
    for index, block in enumerate(blocks):
        start = 0
        for piece in block:
            result.append((index, start, piece.shape[0]))
            start += piece.shape[0]
    return result


def token_forward_kernel(where, count, *refs):
    mine_ref, came_ref, x_ref, a_ref, b_ref, mask_ref, gain_ref = refs[:7]
    weights, refs = refs[7 : 7 + count], refs[7 + count :]
    resid_ref, normed_ref, hid_ref, all_ref, gated_ref, a_mine, sems = refs
    devices = came_ref.shape[0]
    rows, model = x_ref.shape
    width = came_ref.shape[2]
    bits = block_order(devices)
    copies = [
        pltpu.make_async_copy(weights[i], all_ref.at[pl.ds(block * width + start, size)], sems.at[i])
        for i, (block, start, size) in enumerate(where)
    ]
    for copy in copies:
        copy.start()
    squares = jnp.zeros((1, rows), jnp.float32)
    for d in range(devices):
        lines = came_ref[d, rows : rows + 16, :].astype(jnp.float32)
        squares = squares + jnp.concatenate(unpacked_row(lines, 0, rows // width), axis=1)
    factor = lax.rsqrt(row_to_column(squares) / model + eps_norm)
    for place, bit in enumerate(bits):
        source = mine_ref[0] ^ bit
        lanes = slice(place * width, (place + 1) * width)
        raw = came_ref[source, 0:rows, :].astype(jnp.float32)
        gated_ref[:, lanes] = (raw * factor).astype(jnp.bfloat16)
        a_mine[lanes, :] = a_ref[pl.ds(pl.multiple_of(source * width, 128), width), :]
    gated = gated_ref[...]
    hid = (mm(gated, a_mine[...]) * mask_ref[...].astype(jnp.float32)).astype(jnp.bfloat16)
    hid_ref[...] = hid
    extra = mm(hid, b_ref[...], NT)
    for copy in copies:
        copy.wait()
    resid = x_ref[...].astype(jnp.float32) + mm(gated, all_ref[...]) + extra
    resid_ref[...] = resid
    factor = lax.rsqrt(jnp.mean(resid * resid, axis=-1, keepdims=True) + eps_norm)
    normed_ref[...] = (resid * factor * gain_ref[...]).astype(jnp.bfloat16)


def token_forward(mine, came, x, out_a, out_b, mask_own, gain, weights):
    rows, model = x.shape
    where = spans(weights)
    pieces = [piece for block in weights for piece in block]
    ranks = out_a.shape[1]
    return pl.pallas_call(
        lambda *refs: token_forward_kernel(where, len(pieces), *refs),
        out_shape=(
            jax.ShapeDtypeStruct((rows, model), jnp.float32),
            jax.ShapeDtypeStruct((rows, model), jnp.bfloat16),
            jax.ShapeDtypeStruct((rows, ranks), jnp.bfloat16),
        ),
        in_specs=[SMEM] + [VMEM] * 6 + [ANY] * len(pieces),
        out_specs=(VMEM,) * 3,
        scratch_shapes=[
            pltpu.VMEM((model, model), jnp.bfloat16),
            pltpu.VMEM((rows, model), jnp.bfloat16),
            pltpu.VMEM((model, ranks), jnp.bfloat16),
            pltpu.SemaphoreType.DMA((len(pieces),)),
        ],
        compiler_params=params(62),
        cost_estimate=cost(8),
    )(mine, came, x, out_a, out_b, mask_own, gain.reshape(1, model), *pieces)


def summed(refs):
    own, other, from_x, from_y = refs
    total = own[...].astype(jnp.float32) + other[...].astype(jnp.float32)
    for pieces in (from_x, from_y):
        if pieces:
            total = total + jnp.concatenate([piece[...] for piece in pieces]).astype(jnp.float32)
    return total


def first_block(rows, columns):
    return pl.BlockSpec((rows, columns), lambda i: (0, 0))


def whole(array):
    return pl.BlockSpec(array.shape, lambda i: (0,) * array.ndim)


def token_backward_kernel(where, count, near, nears, *refs):
    mine_ref, came_ref, cot_ref, resid_ref, a_ref, b_ref, mask_ref, gain_ref, hid_ref, own, other = refs[:11]
    refs = refs[11:]
    from_x, from_y, refs = refs[:near], refs[near:nears], refs[nears:]
    weights, refs = refs[:count], refs[count:]
    sent_ref, d_resid_ref, d_hid_ref, b_rows_ref, all_ref, sems = refs
    devices = came_ref.shape[0]
    rows, model = resid_ref.shape
    width = came_ref.shape[2]
    copies = [
        pltpu.make_async_copy(weights[i], all_ref.at[pl.ds(block * width + start, size)], sems.at[i])
        for i, (block, start, size) in enumerate(where)
    ]
    for copy in copies:
        copy.start()
    squares = jnp.zeros((1, rows), jnp.float32)
    for d in range(devices):
        lines = came_ref[d, rows : rows + 16, :].astype(jnp.float32)
        squares = squares + jnp.concatenate(unpacked_row(lines, 0, rows // width), axis=1)
    factor_two = lax.rsqrt(squares / model + eps_norm)

    resid = resid_ref[...]
    factor = lax.rsqrt(jnp.mean(resid * resid, axis=-1, keepdims=True) + eps_norm)
    scaled = summed((own, other, from_x, from_y)) * gain_ref[...]
    mean = jnp.mean(resid * scaled, axis=-1, keepdims=True)
    d_resid = cot_ref[...].astype(jnp.float32) + factor * scaled - resid * (factor * factor * factor * mean)
    d_resid_ref[...] = d_resid
    g_attn = d_resid.astype(jnp.bfloat16)
    d_hid = (mm(g_attn, b_ref[...]) * mask_ref[...].astype(jnp.float32)).astype(jnp.bfloat16)
    d_hid_ref[...] = d_hid
    b_rows_ref[...] = mm(g_attn, hid_ref[...], TN)
    for copy in copies:
        copy.wait()
    total = jnp.zeros((rows, 1), jnp.float32)
    for place, bit in enumerate(block_order(devices)):
        target = mine_ref[0] ^ bit
        block = slice(place * width, (place + 1) * width)
        a_block = a_ref[pl.ds(pl.multiple_of(target * width, 128), width), :]
        d_gated = mm(g_attn, all_ref[block, :], NT) + mm(d_hid, a_block, NT)
        raw = came_ref[target, 0:rows, :].astype(jnp.float32)
        total = total + jnp.sum(raw * d_gated, axis=-1, keepdims=True)
        sent_ref[target, 0:rows, :] = d_gated.astype(jnp.bfloat16)
    lines = packed_lines([factor_two, column_to_row(total / model)], width)
    for d in range(devices):
        sent_ref[d, rows : rows + 16, :] = lines


def token_backward(mine, came, cot, resid, out_a, out_b, mask_own, gain, hid, parts, weights):
    rows, model = resid.shape
    own, other, from_x, from_y = parts
    where = spans(weights)
    pieces = [piece for block in weights for piece in block]
    ranks = out_a.shape[1]
    fixed = [came, cot, resid, out_a, out_b, mask_own, gain.reshape(1, model), hid]
    return pl.pallas_call(
        lambda *refs: token_backward_kernel(where, len(pieces), len(from_x), len(from_x + from_y), *refs),
        grid=(1,),
        out_shape=(
            jax.ShapeDtypeStruct(came.shape, jnp.bfloat16),
            jax.ShapeDtypeStruct((rows, model), jnp.float32),
            jax.ShapeDtypeStruct((rows, ranks), jnp.bfloat16),
            jax.ShapeDtypeStruct((model, ranks), jnp.float32),
        ),
        in_specs=[SMEM] + [whole(array) for array in fixed] + [first_block(rows, model)] * 2
        + [whole(piece) for piece in from_x + from_y] + [ANY] * len(pieces),
        out_specs=(
            pl.BlockSpec(came.shape, lambda i: (0, 0, 0)),
            first_block(rows, model),
            first_block(rows, ranks),
            first_block(model, ranks),
        ),
        scratch_shapes=[
            pltpu.VMEM((model, model), jnp.bfloat16),
            pltpu.SemaphoreType.DMA((len(pieces),)),
        ],
        compiler_params=params(62),
        cost_estimate=cost(12),
    )(mine, *fixed, own, other, *from_x, *from_y, *pieces)


def token_end_kernel(near, nears, *refs):
    x_ref, d_resid_ref, d_hid_ref, a_ref, gain_ref, own, other = refs[:7]
    refs = refs[7:]
    from_x, from_y, out_ref = refs[:near], refs[near:nears], refs[nears]
    x = x_ref[...].astype(jnp.float32)
    factor = lax.rsqrt(jnp.mean(x * x, axis=-1, keepdims=True) + eps_norm)
    d_normed = summed((own, other, from_x, from_y)) + mm(d_hid_ref[...], a_ref[...], NT)
    scaled = d_normed * gain_ref[...]
    mean = jnp.mean(x * scaled, axis=-1, keepdims=True)
    out = d_resid_ref[...] + factor * scaled - x * (factor * factor * factor * mean)
    out_ref[...] = out.astype(jnp.bfloat16)


def token_end(x, d_resid, d_hid, in_a, gain, parts):
    rows, model = x.shape
    own, other, from_x, from_y = parts
    fixed = [x, d_resid]
    return pl.pallas_call(
        lambda *refs: token_end_kernel(len(from_x), len(from_x + from_y), *refs),
        grid=(1,),
        out_shape=jax.ShapeDtypeStruct((rows, model), jnp.bfloat16),
        in_specs=[whole(x), whole(d_resid), first_block(rows, d_hid.shape[1]), whole(in_a), first_block(1, model)]
        + [first_block(rows, model)] * 2 + [whole(piece) for piece in from_x + from_y],
        out_specs=first_block(rows, model),
        compiler_params=params(62),
        cost_estimate=cost(4),
    )(x, d_resid, d_hid, in_a, gain.reshape(1, model), own, other, *from_x, *from_y)


def both_copies(refs, place, target, padded, sem):
    if len(refs) == 2:
        size = refs[0].shape[0]
        return [(None, pltpu.make_async_copy(refs[i], window(target, i * padded, size), sem)) for i in range(2)]
    groups = [refs[i : i + 6] for i in range(0, len(refs), 6)]
    units = sum(group[0].shape[0] for group in groups)
    copies, first = [], 0
    for group in groups:
        size = group[0].shape[0]

        def at(w, first=first, size=size):
            return window(target, w // 2 * padded + w % 2 * units + first, size)

        copies += line_copies(group, place, at, sem)
        first += size
    return copies


def hidden_of(refs):
    if len(refs) == 2:
        return refs[0].shape[0]
    return 2 * sum(refs[i].shape[0] for i in range(0, len(refs), 6))


def load_both(refs, place, w_all, ffn_a_ref, padded, sem):
    copies = both_copies(refs, place, w_all, padded, sem)
    go(copies, "start")
    hidden_units = hidden_of(refs)
    if padded > hidden_units:
        blank = jnp.zeros((padded - hidden_units, w_all.shape[1]), jnp.bfloat16)
        w_all[hidden_units:padded, :] = blank
        w_all[padded + hidden_units : 2 * padded, :] = blank
    w_all[2 * padded :, :] = ffn_a_ref[...]
    return copies


def ffn_up_kernel(stream, ffn_pieces, *refs):
    mine_ref, place_ref, refs = refs[0], refs[1], refs[2:]
    pieces, refs = refs[: len(stream.pieces)], refs[len(stream.pieces) :]
    weights, refs = windows(ffn_pieces, refs), refs[len(ffn_pieces) :]
    mask_ref, ffn_a_ref, both_b_ref, both_ref, hid_ref, mine_out_ref, w_all, slots, sems, ffn_sem = refs
    step = pl.program_id(0)
    stream.bind(pieces, slots, sems)
    padded = both_b_ref.shape[0] // 2
    wide = mine_out_ref.shape[1]

    @pl.when(step == 0)
    def _():
        go(load_both(weights, place_ref[0], w_all, ffn_a_ref, padded, ffn_sem), "wait")

    normed = stream.fetch(step)
    columns = pl.ds(pl.multiple_of(mine_ref[0] * wide, 128), wide)
    mine_out_ref[...] = slots[lax.rem(step, 2), :, columns]
    mask = mask_ref[...].astype(jnp.float32)
    main = mm(normed, w_all[...], NT)
    hid = (main[:, 2 * padded :] * jnp.concatenate([mask, mask], axis=1)).astype(jnp.bfloat16)
    hid_ref[...] = hid
    both_ref[...] = main[:, : 2 * padded] + mm(hid, both_b_ref[...], NT)


def ffn_up(mine, place, normed, weights, mask, ffn_a_t, both_b, wide):
    stream = Stream(normed)
    rows, model = stream.rows, ffn_a_t.shape[1]
    total = rows * len(normed)
    ranks = mask.shape[1]
    padded = both_b.shape[0] // 2
    return pl.pallas_call(
        lambda *refs: ffn_up_kernel(stream, weights, *refs),
        grid=(len(normed),),
        out_shape=(
            jax.ShapeDtypeStruct((total, 2 * padded), jnp.float32),
            jax.ShapeDtypeStruct((total, 2 * ranks), jnp.bfloat16),
            jax.ShapeDtypeStruct((total, wide), jnp.bfloat16),
        ),
        in_specs=[SMEM] * 2
        + [ANY] * (len(stream.pieces) + len(weights))
        + [tile_spec(rows, ranks), whole(ffn_a_t), whole(both_b)],
        out_specs=(tile_spec(rows, 2 * padded), tile_spec(rows, 2 * ranks), tile_spec(rows, wide)),
        scratch_shapes=[pltpu.VMEM((2 * padded + 2 * ranks, model), jnp.bfloat16)]
        + stream_scratch(rows, model)
        + [pltpu.SemaphoreType.DMA(())],
        compiler_params=params(62),
        cost_estimate=cost(28),
    )(mine, place, *stream.arrays, *arrays_of(weights), mask, ffn_a_t, both_b)


def ffn_back_kernel(stream, ffn_pieces, down_pieces, *refs):
    mine_ref, place_ref, refs = refs[0], refs[1], refs[2:]
    pieces, refs = refs[: len(stream.pieces)], refs[len(stream.pieces) :]
    weights, refs = windows(ffn_pieces, refs), refs[len(ffn_pieces) :]
    downs, refs = windows(down_pieces, refs), refs[len(down_pieces) :]
    (
        both_ref, hid_ref, mask_ref, ffn_a_ref, both_b_ref, down_a_ref, down_b_ref, fold_ref,
        back_ref, down_ref, small_ref, cot_mine_ref, down_rows, both_rows,
        w_all, w_down, left_both, left_down, slots, sems, ffn_sem, down_sem,
    ) = refs
    step = pl.program_id(0)
    stream.bind(pieces, slots, sems)
    padded = down_a_ref.shape[0]
    model = w_down.shape[1]
    wide = cot_mine_ref.shape[1]

    @pl.when(step == 0)
    def _():
        hidden_units = hidden_of(weights)
        if len(downs) == 1:
            down = line_copies(downs, place_ref[0], lambda w: window(w_down, 0, hidden_units), down_sem)
        else:
            strip = downs[0].shape[0]
            narrow = model * strip // hidden_units
            down = []
            for part in range(hidden_units // strip):
                down += line_copies(
                    [ref.at[:, pl.ds(part * narrow, narrow)] for ref in downs],
                    place_ref[0],
                    lambda w, part=part: w_down.at[pl.ds(part * strip, strip), pl.ds(w * narrow, narrow)],
                    down_sem,
                )
        go(down, "start")
        if padded > hidden_units:
            w_down[hidden_units:padded, :] = jnp.zeros((padded - hidden_units, model), jnp.bfloat16)
        w_down[padded:, :] = down_b_ref[...]
        both = load_both(weights, place_ref[0], w_all, ffn_a_ref, padded, ffn_sem)
        go(down, "wait")
        go(both, "wait")
        down_rows[...] = jnp.zeros_like(down_rows)
        both_rows[...] = jnp.zeros_like(both_rows)

    cot = stream.fetch(step)
    columns = pl.ds(pl.multiple_of(mine_ref[0] * wide, 128), wide)
    cot_mine_ref[...] = slots[lax.rem(step, 2), :, columns]
    mask = mask_ref[...].astype(jnp.float32)
    hid = hid_ref[...]
    main = mm(cot, w_down[...], NT)
    d_hid = (main[:, padded:] * mask).astype(jnp.bfloat16)
    d_hidden = main[:, :padded] + mm(d_hid, down_a_ref[...], NT)
    gate, upper = both_ref[:, :padded], both_ref[:, padded:]
    sigma = jax.nn.sigmoid(gate)
    silu = gate * sigma
    left_down[:, :padded] = (silu * upper).astype(jnp.bfloat16)
    left_both[:, :padded] = (d_hidden * upper * (sigma * (1.0 + gate * (1.0 - sigma)))).astype(jnp.bfloat16)
    left_both[:, padded : 2 * padded] = (d_hidden * silu).astype(jnp.bfloat16)
    mask_two = jnp.concatenate([mask, mask], axis=1)
    through = (mm(left_both[:, : 2 * padded], both_b_ref[...]) * mask_two).astype(jnp.bfloat16)
    left_both[:, 2 * padded :] = through
    back_ref[...] = mm(left_both[...], w_all[...]).astype(jnp.bfloat16)
    low = (mm(left_down[:, :padded], down_a_ref[...]) * mask).astype(jnp.bfloat16)
    left_down[:, padded:] = low
    down_ref[...] = mm(left_down[...], w_down[...]).astype(jnp.bfloat16)
    small_ref[...] = mm(jnp.concatenate([low, through], axis=1), fold_ref[...]).astype(jnp.bfloat16)
    down_rows[...] += mm(d_hid, left_down[:, :padded], TN)
    both_rows[...] += mm(hid, left_both[:, : 2 * padded], TN)


def ffn_back(mine, place, cot, weights, downs, both, hid, mask, first, ffn_a_t, both_b, down_a, down_b_t, fold, wide):
    stream = Stream(cot)
    rows, model = stream.rows, ffn_a_t.shape[1]
    blocks = len(cot)
    total = rows * blocks
    padded, ranks = down_a.shape
    fixed = [ffn_a_t, both_b, down_a, down_b_t, fold]
    grown = jax.ShapeDtypeStruct((total, model), jnp.bfloat16)

    def from_first(columns):
        return pl.BlockSpec((rows, columns), lambda i: (i + first, 0))

    return pl.pallas_call(
        lambda *refs: ffn_back_kernel(stream, weights, downs, *refs),
        grid=(blocks,),
        out_shape=(
            grown, grown, jax.ShapeDtypeStruct((total, ranks), jnp.bfloat16),
            jax.ShapeDtypeStruct((total, wide), jnp.bfloat16),
            jax.ShapeDtypeStruct((ranks, padded), jnp.float32),
            jax.ShapeDtypeStruct((2 * ranks, 2 * padded), jnp.float32),
        ),
        in_specs=[SMEM] * 2
        + [ANY] * (len(stream.pieces) + len(weights) + len(downs))
        + [from_first(2 * padded), from_first(2 * ranks), from_first(ranks)]
        + [whole(array) for array in fixed],
        out_specs=(
            tile_spec(rows, model), tile_spec(rows, model), tile_spec(rows, ranks), tile_spec(rows, wide),
            first_block(ranks, padded), first_block(2 * ranks, 2 * padded),
        ),
        scratch_shapes=[
            pltpu.VMEM((2 * padded + 2 * ranks, model), jnp.bfloat16),
            pltpu.VMEM((padded + ranks, model), jnp.bfloat16),
            pltpu.VMEM((rows, 2 * padded + 2 * ranks), jnp.bfloat16),
            pltpu.VMEM((rows, padded + ranks), jnp.bfloat16),
        ]
        + stream_scratch(rows, model)
        + [pltpu.SemaphoreType.DMA(()), pltpu.SemaphoreType.DMA(())],
        compiler_params=params(62),
        cost_estimate=cost(33),
    )(mine, place, *stream.arrays, *arrays_of(weights), *arrays_of(downs), both, hid, mask, *fixed)


def spread_kernel(win_pieces, *refs):
    place_ref, refs = refs[0], refs[1:]
    pieces, refs = windows(win_pieces, refs), refs[len(win_pieces) :]
    x_ref, out_ref, win_ref, sem = refs
    copies = projection_copies(pieces, place_ref[0], win_ref, sem)

    @pl.when(pl.program_id(0) == 0)
    def _():
        go(copies, "start")
        go(copies, "wait")

    out_ref[...] = mm(x_ref[...], win_ref[...]).astype(jnp.bfloat16)


def spread(place, values, win_pieces, first, blocks, rows):
    inner = values.shape[1]
    model = win_pieces[0][0].shape[1]
    return pl.pallas_call(
        lambda *refs: spread_kernel(win_pieces, *refs),
        grid=(blocks,),
        out_shape=jax.ShapeDtypeStruct((rows * blocks, model), jnp.bfloat16),
        in_specs=[SMEM] + [ANY] * len(win_pieces) + [pl.BlockSpec((rows, inner), lambda i: (i + first, 0))],
        out_specs=tile_spec(rows, model),
        scratch_shapes=[pltpu.VMEM((inner, model), jnp.bfloat16), pltpu.SemaphoreType.DMA(())],
        compiler_params=params(62),
        cost_estimate=cost(8),
    )(place, *arrays_of(win_pieces), values)


def pack_in_kernel(mine_ref, win_ref, wout_ref, out_ref, window, sems):
    wide, model = window.shape[1], window.shape[0]
    narrow = wout_ref.shape[1]
    strips = model // narrow
    strip = wide // strips
    start = pl.multiple_of(mine_ref[0] * wide, 128)
    copies = [pltpu.make_async_copy(win_ref.at[:, pl.ds(start, wide)], window, sems.at[0])]
    for part in range(strips):
        copies.append(
            pltpu.make_async_copy(
                wout_ref.at[pl.ds(pl.multiple_of(start + part * strip, 16), strip)],
                out_ref.at[pl.ds(wide, strip), pl.ds(part * narrow, narrow)],
                sems.at[1 + part],
            )
        )
    for copy in copies:
        copy.start()
    eye = lax.broadcasted_iota(jnp.int32, (wide, wide), 0) == lax.broadcasted_iota(jnp.int32, (wide, wide), 1)
    eye = jnp.where(eye, 1.0, 0.0).astype(jnp.bfloat16)
    for copy in copies:
        copy.wait()
    out_ref[0:wide, :] = mm(eye, window[...], NT).astype(jnp.bfloat16)


def pack_in(mine, w_in, w_out, wide):
    model, narrow = w_in.shape[0], w_out.shape[1]
    strips = model // narrow
    return pl.pallas_call(
        pack_in_kernel,
        out_shape=jax.ShapeDtypeStruct((wide + wide // strips, model), jnp.bfloat16),
        in_specs=[SMEM, ANY, ANY],
        out_specs=VMEM,
        scratch_shapes=[pltpu.VMEM((model, wide), jnp.bfloat16), pltpu.SemaphoreType.DMA((1 + strips,))],
        compiler_params=params(62),
        cost_estimate=cost(3),
    )(mine, w_in, w_out)


def pack_ffn_kernel(units, mine_ref, wffn_ref, wdown_ref, out_ref, held, sems):
    model, columns = wffn_ref.shape
    span = held.shape[1]
    narrow = wdown_ref.shape[1]
    parts = model // narrow
    shards = wdown_ref.shape[0] // (units * 8)
    strip = units * shards // parts
    wanted = mine_ref[0] * units
    start = jnp.minimum(wanted // 128 * 128, columns - span)
    copies = [pltpu.make_async_copy(wffn_ref.at[:, pl.ds(pl.multiple_of(start, 128), span)], held, sems.at[0])]
    for part in range(parts):
        shard, inside = part * strip // units, part * strip % units
        source = shard * units * 8 + wanted + inside
        copies.append(
            pltpu.make_async_copy(
                wdown_ref.at[pl.ds(pl.multiple_of(source, 16), strip)],
                out_ref.at[pl.ds(units, strip), pl.ds(part * narrow, narrow)],
                sems.at[1 + part],
            )
        )
    for copy in copies:
        copy.start()
    rows = lax.broadcasted_iota(jnp.int32, (units, span), 0) + (wanted - start)
    chosen = jnp.where(rows == lax.broadcasted_iota(jnp.int32, (units, span), 1), 1.0, 0.0).astype(jnp.bfloat16)
    for copy in copies:
        copy.wait()
    out_ref[0:units, :] = mm(chosen, held[...], NT).astype(jnp.bfloat16)


def pack_ffn(mine, w_ffn, w_down, units):
    model, columns = w_ffn.shape
    span = min(columns, (units + 127) // 128 * 128 + 128)
    parts = model // w_down.shape[1]
    return pl.pallas_call(
        lambda *refs: pack_ffn_kernel(units, *refs),
        out_shape=jax.ShapeDtypeStruct((units + 2 * units // parts, model), jnp.bfloat16),
        in_specs=[SMEM, ANY, ANY],
        out_specs=VMEM,
        scratch_shapes=[pltpu.VMEM((model, span), jnp.bfloat16), pltpu.SemaphoreType.DMA((1 + parts,))],
        compiler_params=params(62),
        cost_estimate=cost(3),
    )(mine, w_ffn, w_down)


def unpack_out_kernel(pieces, *refs):
    place_ref, out, sem = refs[0], refs[-2], refs[-1]
    refs = windows(pieces, refs[1:-2])
    strip = refs[0].shape[0]
    strips = out.shape[0] // strip
    narrow = out.shape[1] // strips
    copies = []
    for part in range(strips):
        copies += line_copies(
            [ref.at[:, pl.ds(part * narrow, narrow)] for ref in refs],
            place_ref[0],
            lambda w, part=part: out.at[pl.ds(part * strip, strip), pl.ds(w * narrow, narrow)],
            sem,
        )
    go(copies, "start")
    go(copies, "wait")


def unpack_out(place, pieces, wide):
    model = pieces[0][0].shape[1]
    return pl.pallas_call(
        lambda *refs: unpack_out_kernel(pieces, *refs),
        out_shape=jax.ShapeDtypeStruct((wide, model), pieces[0][0].dtype),
        in_specs=[SMEM] + [ANY] * len(pieces),
        out_specs=VMEM,
        scratch_shapes=[pltpu.SemaphoreType.DMA(())],
        compiler_params=params(62),
        cost_estimate=cost(2),
    )(place, *arrays_of(pieces))


ADAPTERS = 8
RANK = 16
RANKS = ADAPTERS * RANK
PROJECTIONS = 4
eps_norm = 1e-06
f32 = jnp.float32
bf16 = jnp.bfloat16


def sequence_of(positions, seq_lengths):
    bounds = jnp.cumsum(seq_lengths)[:-1]
    return jnp.sum((positions[:, None] >= bounds[None, :]).astype(jnp.int32), axis=1)


def adapter_of(seq_numbers, seq_ids):
    numbers = jnp.arange(seq_ids.shape[0], dtype=jnp.int32)
    return jnp.sum(
        (seq_numbers[:, None] == numbers[None, :]).astype(jnp.int32) * seq_ids[None, :], axis=1
    )


def adapter_mask(adapter, count=1):
    columns = jnp.arange(count * RANKS, dtype=jnp.int32) % RANKS // RANK
    return (columns[None, :] == adapter[:, None]).astype(bf16)


def norm_factor(values):
    return lax.rsqrt(jnp.mean(values * values, axis=-1, keepdims=True) + eps_norm)


def norm_back(values, factor, gain, grad):
    scaled = grad * gain
    return factor * scaled - values * factor**3 * jnp.mean(values * scaled, axis=-1, keepdims=True)


def silu_slope(values, sigma):
    return sigma * (1.0 + values * (1.0 - sigma))


def relative(blocks, index):
    count, rest = blocks.shape[0], blocks.shape[1:]
    bit = 1
    while bit < count:
        pairs = blocks.reshape((count // (2 * bit), 2, bit) + rest)
        blocks = jnp.where((index & bit) != 0, pairs[:, ::-1], pairs).reshape((count,) + rest)
        bit *= 2
    return blocks


def to_order(blocks, index):
    count = blocks.shape[0]
    blocks = relative(blocks, index)
    pairs = blocks.reshape((count // 2, 2) + blocks.shape[1:])
    return jnp.concatenate([pairs[:, 0], pairs[:, 1]])


def from_order(blocks, index):
    count = blocks.shape[0]
    pairs = jnp.stack([blocks[: count // 2], blocks[count // 2 :]], axis=1)
    return relative(pairs.reshape(blocks.shape), index)


def across(values, bits, axis="seq"):
    size = lax.axis_size(axis)
    return lax.ppermute(values, axis, [(i, i ^ bits) for i in range(size)])


def first_near(block):
    size = lax.axis_size("seq")
    return [across(block, k) for k in ((2, 4) if size == 8 else range(2, size, 2))]


def more_near(block, first):
    if len(first) != 2:
        return [[block]] + [[other] for other in first]
    by_x, by_y = first
    half = block.shape[0] // 2
    return [[block], [by_x], [by_y], [across(by_x[:half], 4), across(by_y[half:], 2)]]


def other_core(blocks):
    return [[across(piece, 1) for piece in block] for block in blocks]


def with_rows(blocks):
    return [[(piece, 0, piece.shape[0]) for piece in block] for block in blocks]


def two_blocks(blocks):
    upper, lower = [], []
    for block in blocks:
        if len(block) == 1:
            half = block[0].shape[0] // 2
            upper.append([(block[0], 0, half)])
            lower.append([(block[0], half, half)])
        else:
            upper.append([(block[0], 0, block[0].shape[0])])
            lower.append([(block[1], 0, block[1].shape[0])])
    return upper, lower


def scatter_parts(near, other):
    size = lax.axis_size("seq")
    rows = near.shape[0] // (size // 2)
    half = rows // 2

    def part(block, start, stop):
        at = slice(block * rows + start, block * rows + stop)
        return near[at].astype(f32) + other[at].astype(f32)

    if size != 8:
        return [part(i, 0, rows).astype(bf16) for i in range(1, size // 2)], []
    sent = [part(3, 0, half), part(3, half, rows), part(1, 0, half), part(2, half, rows)]
    return [piece.astype(bf16) for piece in sent], [part(1, half, rows), part(2, 0, half)]


def scatter_first(sent):
    bits = (2, 4, 2, 4) if lax.axis_size("seq") == 8 else [2 * i + 2 for i in range(len(sent))]
    return [across(piece, bit) for piece, bit in zip(sent, bits)]


def scatter_second(came, rest):
    if not rest:
        total = sum(piece.astype(f32) for piece in came).astype(bf16)
        return [total], []
    far_x, far_y, by_x, by_y = came
    by_x_more = across((rest[0] + far_y.astype(f32)).astype(bf16), 2)
    by_y_more = across((rest[1] + far_x.astype(f32)).astype(bf16), 4)
    return [by_x, by_x_more], [by_y_more, by_y]


def swap(values, axis="seq"):
    return lax.all_to_all(values, axis, split_axis=0, concat_axis=0, tiled=False)


def along(values, pairs):
    return lax.ppermute(values, "wt", pairs)


def first_pieces(block):
    return along(block, [(0, 1), (1, 2), (2, 3)]), along(block, [(1, 0), (2, 1), (3, 2)])


def more_pieces(first, start, size):
    place = lax.axis_index("wt")
    up, down = [piece[start : start + size] for piece in first]
    inner, outer = jnp.where(place == 1, up, down), jnp.where(place == 2, up, down)
    return [along(inner, [(1, 2), (2, 1)]), along(outer, [(2, 3), (1, 0)]), along(inner, [(1, 3), (2, 0)])]


def line_rows(block, first, more, start, size, more_start=0):
    return [(piece, start, size) for piece in (block,) + tuple(first)] + [(piece, more_start, size) for piece in more]


def after(values, *others):
    return lax.optimization_barrier((values,) + others)[0]


def to_owner(piece, count):
    size, lines = lax.axis_size("seq"), lax.axis_size("wt")
    each = lines // count
    moves = []
    for s in range(size):
        for q in range(lines):
            whole = (q // each) * size * each + s * each + q % each
            moves.append((s * lines + q, whole))
    return lax.ppermute(piece, ("seq", "wt"), moves)


def fold_columns(count, first):
    source = jnp.arange(count * RANKS)
    target = jnp.arange(RANKS)
    wanted = (first + source // RANKS) * RANK + source % RANK
    return (wanted[:, None] == target[None, :]).astype(bf16)


def local(
    tokens,
    cotangent,
    w_in,
    w_out,
    w_ffn,
    w_down,
    gain_mix,
    gain_gate,
    gain_ffn,
    forget_gap,
    in_a,
    in_b,
    out_a,
    out_b,
    ffn_a,
    ffn_b,
    down_a,
    down_b,
    order,
    lengths,
    adapter_ids,
):
    n, wt = lax.axis_size("seq"), lax.axis_size("wt")
    mine = lax.axis_index("seq")
    mine_ref = mine.astype(jnp.int32).reshape(1)
    place_ref = lax.axis_index("wt").astype(jnp.int32).reshape(1)
    x_rows = tokens[0]
    cot_rows = cotangent[0]
    rows, model = x_rows.shape
    total = n * rows
    wide = model // n
    units = w_ffn.shape[1] // n
    hidden_units = wt // 2 * units
    padded = (hidden_units + 127) // 128 * 128
    blocks = n // 2
    on_line = wt == PROJECTIONS and n == 8

    def my_columns(values, extent, axis):
        return lax.dynamic_slice_in_dim(values, mine * extent, extent, axis)

    def my_piece(values, axis):
        return lax.dynamic_index_in_dim(values, mine, axis, False)

    def pad_rows(values):
        return jnp.pad(values, ((0, padded - hidden_units), (0, 0)))

    if on_line:
        win_mine = pack_in(mine_ref, w_in, w_out, wide)
        win_first = lax.optimization_barrier(first_pieces(win_mine))
        win_more = more_pieces(win_first, 0, win_mine.shape[0])
        ffn_mine = pack_ffn(mine_ref, w_ffn, w_down, units)
    else:
        spread_in = lax.all_gather(w_in, "wt", axis=1, tiled=True)
        spread_in = my_piece(spread_in.reshape(model, PROJECTIONS, n, wide), 2)
        win_pieces = [jnp.transpose(spread_in, (1, 2, 0)).reshape(PROJECTIONS * wide, model)]
        win_pieces = [(win_pieces[0], 0, PROJECTIONS * wide)]
        wout_mine = lax.all_gather(my_columns(w_out, wide, 0), "wt", axis=1, tiled=True)
        down_mine = my_piece(w_down.reshape(wt // 2, n, units, -1), 1).reshape(hidden_units, -1)
        down_pieces = [(lax.all_gather(down_mine, "wt", axis=1, tiled=True), 0, hidden_units)]
        spread_ffn = lax.all_gather(my_columns(w_ffn, units, 1).T, "wt", axis=0)
        spread_ffn = [spread_ffn[: wt // 2].reshape(-1, model), spread_ffn[wt // 2 :].reshape(-1, model)]
        ffn_pieces = [(piece, 0, hidden_units) for piece in spread_ffn]

    inputs = x_rows.astype(f32)
    normed = (inputs * norm_factor(inputs) * gain_mix).astype(bf16)
    pair = jnp.concatenate([normed, cot_rows])
    pair_first = first_near(pair)
    order_mine = to_order(order[0].reshape(n, rows), mine).reshape(total)
    ends = jnp.cumsum(lengths[0])
    adapter = adapter_of(sequence_of(order_mine, lengths[0]), adapter_ids[0])
    mask = adapter_mask(adapter)
    mask_own = mask[:rows]
    gap_mine = my_columns(forget_gap, wide, 0)
    gain_mine = my_columns(gain_gate, wide, 0)
    in_b_mine = my_piece(in_b.reshape(PROJECTIONS, n, wide, RANKS), 1)
    in_b_wide = jnp.concatenate(
        [jnp.pad(in_b_mine[j], ((0, 0), (j * RANKS, (PROJECTIONS - 1 - j) * RANKS))) for j in range(PROJECTIONS)]
    )
    fold_in, fold_ffn, fold_out = fold_columns(PROJECTIONS, 0), fold_columns(3, PROJECTIONS), fold_columns(1, PROJECTIONS + 3)
    ffn_b_mine = my_piece(ffn_b.reshape(wt, n, units, RANKS), 1)
    b_gate = pad_rows(ffn_b_mine[: wt // 2].reshape(-1, RANKS))
    b_up = pad_rows(ffn_b_mine[wt // 2 :].reshape(-1, RANKS))
    both_b = jnp.concatenate([jnp.pad(b_gate, ((0, 0), (0, RANKS))), jnp.pad(b_up, ((0, 0), (RANKS, 0)))])
    down_a_mine = pad_rows(my_piece(down_a.reshape(wt // 2, n, units, RANKS), 1).reshape(-1, RANKS))
    ready = lax.optimization_barrier(
        (
            pair_first, (order_mine.reshape(1, total), order_mine.reshape(total, 1)), mask, gap_mine, gain_mine,
            in_b_wide, both_b, down_a_mine, down_b.T, ffn_a.T, in_a.T,
        )
    )
    pair_first, order_both, mask, gap_mine, gain_mine, in_b_wide, both_b, down_a_mine, down_b_t, ffn_a_t, in_a_t = ready
    pair_near = more_near(pair, pair_first)
    pair_other = other_core(pair_near)
    normed_near, cot_near = two_blocks(pair_near)
    normed_other, cot_other = two_blocks(pair_other)

    if on_line:
        win_more, ffn_mine = lax.optimization_barrier((win_more, ffn_mine))
        win_pieces = line_rows(win_mine, win_first, win_more, 0, wide)
        wout_mine = line_rows(win_mine, win_first, win_more, wide, win_mine.shape[0] - wide, wide)
        wout_mine = unpack_out(place_ref, wout_mine, wide)
    sent, hid_in, normed_mine, *kept = mixer_forward(
        ends, mine_ref, place_ref, order_both, normed_near + normed_other, win_pieces,
        after(in_a_t, wout_mine), in_b_wide, mask, gap_mine, gain_mine,
    )
    wout_first = [across(wout_mine, k) for k in range(2, n, 2)]
    if on_line:
        sent, wout_first, ffn_first = lax.optimization_barrier((sent, wout_first, first_pieces(ffn_mine)))
        early = units // 48 * 16
        early_more = more_pieces(ffn_first, 0, early)
        strip = ffn_mine.shape[0] - units
    else:
        sent, wout_first = lax.optimization_barrier((sent, wout_first))
    wout_near = [[wout_mine]] + [[block] for block in wout_first]
    wout_blocks = wout_near + other_core(wout_near)

    came = swap(sent)
    resid, normed2, hid_out = token_forward(
        mine_ref, came, x_rows, out_a, out_b, mask_own, gain_ffn, wout_blocks
    )

    if on_line:
        normed2, early_more = lax.optimization_barrier((normed2, early_more))
        late_more = more_pieces(after(ffn_first, *early_more), early, units - early)
        ffn_pieces = line_rows(ffn_mine, ffn_first, early_more, 0, early)
        ffn_pieces += line_rows(ffn_mine, ffn_first, late_more, early, units - early)
        down_more = more_pieces(after(ffn_first, *late_more), units, strip)

    normed2_near = more_near(normed2, first_near(normed2))
    both, hid_ffn, normed2_mine = ffn_up(
        mine_ref, place_ref, with_rows(normed2_near + other_core(normed2_near)), ffn_pieces, mask, ffn_a_t, both_b, wide
    )
    if on_line:
        both, down_more = lax.optimization_barrier((both, down_more))
        down_pieces = line_rows(ffn_mine, ffn_first, down_more, units, strip)
    sides = []
    for cots, first in ((cot_other, blocks), (cot_near, 0)):
        sides.append(
            ffn_back(
                mine_ref, place_ref, cots, ffn_pieces, down_pieces, both, hid_ffn, mask, first,
                ffn_a_t, both_b, down_a_mine, down_b_t, fold_ffn, wide,
            )
        )
    back_far, down_far, small_far, *rest_far = sides[0]
    back, down, small, *rest = sides[1]
    back_far, down_far = across(back_far, 1), across(down_far, 1)
    back, down, back_far, down_far = lax.optimization_barrier((back, down, back_far, down_far))
    back_parts, back_rest = scatter_parts(back, back_far)
    from_x, from_y = scatter_second(scatter_first(back_parts), back_rest)
    d_sent, d_resid, d_hid_out, out_b_part = token_backward(
        mine_ref, came, cot_rows, resid, out_a, out_b, mask_own, gain_ffn, hid_out,
        (back, back_far, from_x, from_y), wout_blocks,
    )
    cot_mine = jnp.concatenate([rest[0], rest_far[0]])
    down_rows, both_rows = [rest[i] + rest_far[i] for i in (1, 2)]
    down_a_rows = down_rows[:, :hidden_units].T
    ffn_b_rows = jnp.concatenate(
        [both_rows[:RANKS, :hidden_units], both_rows[RANKS:, padded : padded + hidden_units]], axis=1
    ).T

    def packed_rows(arrays):
        return jnp.concatenate(
            [
                array[:, c * RANKS : (c + 1) * RANKS].reshape(wt, -1, RANKS)
                for array in arrays
                for c in range(array.shape[1] // RANKS)
            ],
            axis=1,
        )

    def unpacked_rows(summed, arrays):
        results, start = [], 0
        for array in arrays:
            height = array.shape[0] // wt
            parts = []
            for _ in range(array.shape[1] // RANKS):
                parts.append(summed[start : start + height])
                start += height
            results.append(jnp.concatenate(parts, axis=1))
        return results

    early = [ffn_b_rows, down_a_rows]
    early_sum = lax.psum_scatter(packed_rows(early), "wt", scatter_dimension=0, tiled=False)

    out_parts = [
        (down[i * rows : (i + 1) * rows].astype(f32) + down_far[i * rows : (i + 1) * rows].astype(f32)).astype(bf16)
        for i in range(1, blocks)
    ]
    out_came = [across(part, 2 * i + 2) for i, part in enumerate(after(out_parts, d_sent))]
    d_came = swap(d_sent)
    g_proj, gated_heads, small_in, in_b_rows = mixer_backward(
        ends, mine_ref, order_both, d_came, kept, gap_mine, gain_mine, hid_in, in_b_wide, mask, fold_in
    )
    g_proj, small_in, out_came, early_sum = lax.optimization_barrier((g_proj, small_in, out_came, early_sum))
    ffn_b_grad, down_a_grad = unpacked_rows(early_sum, early)

    small = (small_in + jnp.concatenate([small, small_far])).reshape(n, rows, RANKS)
    small = jnp.concatenate([from_order(small, mine), out_b_part.astype(bf16).reshape(n, rows, -1)], axis=2)
    small, g_proj = lax.optimization_barrier((small, g_proj))
    small = swap(small)
    back_in_far = across(spread(place_ref, g_proj, win_pieces, blocks, blocks, rows), 1)
    back_in = spread(place_ref, g_proj, win_pieces, 0, blocks, rows)
    in_parts, in_rest = scatter_parts(back_in, back_in_far)
    in_came = scatter_first(in_parts)
    small = jnp.sum(after(small, *in_parts, *in_rest).astype(f32), axis=0)
    out_b_rows = small[:, RANKS:].reshape(wide, RANKS)
    small = small[:, :RANKS].astype(bf16)
    d_hid_in_own = (mm(small, fold_in, NT) * adapter_mask(adapter[:rows], PROJECTIONS)).astype(bf16)
    small = small + mm(d_hid_out, fold_out).astype(bf16)
    small = swap(jnp.broadcast_to(small, (n,) + small.shape))
    block_out = resid + down[:rows].astype(f32) + down_far[:rows].astype(f32)
    block_out = (block_out + sum(piece.astype(f32) for piece in out_came)).astype(bf16)
    in_came, block_out = lax.optimization_barrier((in_came, block_out))
    if in_rest:
        in_rest = [in_rest[0] + in_came[1].astype(f32), in_rest[1] + in_came[0].astype(f32)]
        in_rest = [part.astype(bf16) for part in in_rest]
        small, in_rest = lax.optimization_barrier((small, in_rest))
        from_x, from_y = [in_came[2], across(in_rest[0], 2)], [across(in_rest[1], 4), in_came[3]]
    else:
        from_x, from_y = scatter_second(in_came, in_rest)
    small = to_order(small, mine).reshape(total, RANKS)
    d_hid_in = (mm(small, fold_in, NT) * adapter_mask(adapter, PROJECTIONS)).astype(bf16)

    wide_ffn = (mm(small, fold_ffn, NT) * adapter_mask(adapter, 3)).astype(bf16)
    late = [
        mm(cot_mine, wide_ffn[:, :RANKS], TN),
        mm(normed2_mine, wide_ffn[:, RANKS:], TN),
        mm(gated_heads, (mm(small, fold_out, NT) * mask).astype(bf16), TN),
        out_b_rows,
        mm(normed_mine, d_hid_in, TN),
        in_b_rows,
    ]
    late_sum = jnp.sum(swap(packed_rows(late).astype(bf16), "wt").astype(f32), axis=0)
    down_b_grad, ffn_a_grad, out_a_grad, out_b_grad, in_a_grad, in_b_grad = unpacked_rows(late_sum, late)
    tokens_grad = token_end(
        x_rows, d_resid, d_hid_in_own, in_a, gain_mix, (back_in, back_in_far, from_x, from_y)
    )
    return (
        block_out[None],
        tokens_grad[None],
        in_a_grad,
        to_owner(in_b_grad, PROJECTIONS),
        out_a_grad,
        out_b_grad,
        ffn_a_grad,
        to_owner(ffn_b_grad, wt),
        to_owner(down_a_grad, wt // 2),
        down_b_grad,
    )


def solution(mesh):
    placed = (
        P("wt", "seq", None),
        P("wt", "seq", None),
        P(None, "wt"),
        P(None, "wt"),
        P(None, "wt"),
        P(None, "wt"),
        P(),
        P(),
        P(),
        P(),
        P(),
        P(),
        P(),
        P(),
        P(),
        P(),
        P(),
        P(),
        P("wt", None),
        P("wt", None),
        P("wt", None),
    )
    return jax.shard_map(
        local,
        mesh=mesh,
        in_specs=placed,
        out_specs=(
            P("wt", "seq", None),
            P("wt", "seq", None),
            P(("seq", "wt"), None),
            P(("seq", "wt"), None),
            P(("seq", "wt"), None),
            P(("seq", "wt"), None),
            P(("seq", "wt"), None),
            P(("seq", "wt"), None),
            P(("seq", "wt"), None),
            P(("seq", "wt"), None),
        ),
        check_vma=False,
    )
```

```python
import jax
import jax.numpy as jnp
from jax import lax
from jax.sharding import PartitionSpec as P
from jax.experimental import pallas as pl
from jax.experimental.pallas import tpu as pltpu

HEAD = 128
CHUNK = 128
TILE = 512
NN = (((1,), (0,)), ((), ()))
NT = (((1,), (1,)), ((), ()))
TN = (((0,), (0,)), ((), ()))


def mm(left, right, dims=NN):
    return lax.dot_general(left, right, dims, preferred_element_type=jnp.float32)


def halves(values):
    high = values.astype(jnp.bfloat16)
    return high, (values - high.astype(jnp.float32)).astype(jnp.bfloat16)


def mm3(left, right, dims=NN):
    return mm(left[0], right[0], dims) + (mm(left[0], right[1], dims) + mm(left[1], right[0], dims))


def mm2(left, right, dims=NN):
    return mm(left[0], right, dims) + mm(left[1], right, dims)


def mm2r(left, right, dims=NN):
    return mm(left, right[0], dims) + mm(left, right[1], dims)


def sum_with(ones, values):
    high, rest = halves(values)
    mid = (values - high.astype(jnp.float32) - rest.astype(jnp.float32)).astype(jnp.bfloat16)
    return mm(ones, high) + (mm(ones, rest) + mm(ones, mid))


def move_rows(picks, pairs):
    total = pairs[0][0].shape[0]

    @pl.loop(0, total // TILE)
    def _(tile):
        start = pl.multiple_of(tile * TILE, TILE)
        chosen = picks(start, total)
        for source, target in pairs:
            target[pl.ds(start, TILE), :] = mm(chosen, source[...]).astype(jnp.bfloat16)


def picks_natural(order_row_ref):
    def picks(start, total):
        places = lax.broadcasted_iota(jnp.int32, (TILE, total), 0) + start
        return jnp.where(order_row_ref[...] == places, 1.0, 0.0).astype(jnp.bfloat16)

    return picks


def picks_packed(order_column_ref):
    def picks(start, total):
        places = lax.broadcasted_iota(jnp.int32, (TILE, total), 1)
        return jnp.where(order_column_ref[pl.ds(start, TILE), :] == places, 1.0, 0.0).astype(jnp.bfloat16)

    return picks


def segment_terms(ends_ref, start):
    count = ends_ref.shape[0] - 1

    def seg_of(positions):
        return sum((positions >= ends_ref[j]).astype(jnp.int32) for j in range(count))

    rows = lax.broadcasted_iota(jnp.int32, (CHUNK, CHUNK), 0)
    cols = lax.broadcasted_iota(jnp.int32, (CHUNK, CHUNK), 1)
    same = seg_of(rows + start) == seg_of(cols + start)
    wide = seg_of(lax.broadcasted_iota(jnp.int32, (CHUNK, HEAD), 0) + start)
    before = jnp.where(start == 0, -1, seg_of(start - 1))
    last = seg_of(start + CHUNK - 1)
    carry_ok = (wide == before).astype(jnp.float32)
    tail_ok = (wide == last).astype(jnp.float32)
    keep = (last == before).astype(jnp.float32)
    return (rows >= cols) & same, (rows <= cols) & same, carry_ok, tail_ok, keep


def chunk_decays(forget, gap, lower):
    sigma = jax.nn.sigmoid(forget)
    keys = gap * (1.0 - sigma)
    cumulative = sum_with(lower, jnp.log1p(-keys))
    middle = cumulative[CHUNK // 2 - 1 : CHUNK // 2]
    total = cumulative[CHUNK - 1 : CHUNK]
    return sigma, keys, cumulative, middle, total


def lower_ones():
    rows = lax.broadcasted_iota(jnp.int32, (CHUNK, CHUNK), 0)
    cols = lax.broadcasted_iota(jnp.int32, (CHUNK, CHUNK), 1)
    return jnp.where(rows >= cols, 1.0, 0.0).astype(jnp.bfloat16)


VMEM = pl.BlockSpec(memory_space=pltpu.VMEM)
SMEM = pl.BlockSpec(memory_space=pltpu.SMEM)
ANY = pl.BlockSpec(memory_space=pl.ANY)


def params(mebibytes):
    return pltpu.CompilerParams(vmem_limit_bytes=mebibytes * 2**20)


def cost(tera_ops):
    return pl.CostEstimate(flops=int(tera_ops * 1e9), bytes_accessed=0, transcendentals=0)


def block_order(count):
    return list(range(0, count, 2)) + list(range(1, count, 2))


def tile_spec(rows, columns):
    return pl.BlockSpec((rows, columns), lambda i: (i, 0))


def row_to_column(row):
    size = row.shape[1]
    eye = lax.broadcasted_iota(jnp.int32, (size, size), 0) == lax.broadcasted_iota(jnp.int32, (size, size), 1)
    return jnp.sum(jnp.where(eye, row, 0.0), axis=1, keepdims=True)


def column_to_row(column):
    size = column.shape[0]
    eye = lax.broadcasted_iota(jnp.int32, (size, size), 0) == lax.broadcasted_iota(jnp.int32, (size, size), 1)
    return jnp.sum(jnp.where(eye, column, 0.0), axis=0, keepdims=True)


def packed_lines(rows_of, width):
    lines = []
    for row in rows_of:
        high, rest = halves(row)
        last = row - high.astype(jnp.float32) - rest.astype(jnp.float32)
        for part in (high.astype(jnp.float32), rest.astype(jnp.float32), last):
            lines += [part[:, i : i + width] for i in range(0, row.shape[1], width)]
    lines.append(jnp.zeros((16 - len(lines), width), jnp.float32))
    return jnp.concatenate(lines, axis=0).astype(jnp.bfloat16)


def unpacked_row(lines, which, each):
    first = 3 * each * which
    return [
        lines[first + i : first + i + 1]
        + lines[first + each + i : first + each + i + 1]
        + lines[first + 2 * each + i : first + 2 * each + i + 1]
        for i in range(each)
    ]


def window(ref, start, size):
    return ref.at[pl.ds(start, size)]


def windows(pieces, refs):
    return [window(ref, start, size) for ref, (_, start, size) in zip(refs, pieces)]


def arrays_of(pieces):
    return [array for array, _, _ in pieces]


def line_copies(refs, place, target, sem):
    if len(refs) == 1:
        return [(None, pltpu.make_async_copy(refs[0], target(None), sem))]
    own, up, down, a, b, c = refs
    held = ((own, down, b, c), (up, own, down, a), (a, up, own, down), (c, b, up, own))
    return [
        (place == p, pltpu.make_async_copy(ref, target(w), sem))
        for p, entries in enumerate(held)
        for w, ref in enumerate(entries)
    ]


def go(copies, what):
    for condition, copy in copies:
        if condition is None:
            getattr(copy, what)()
        else:
            pl.when(condition)(getattr(copy, what))


class Stream:
    def __init__(self, blocks):
        self.pieces = [piece for block in blocks for piece in block]
        self.arrays = arrays_of(self.pieces)
        self.blocks = [len(block) for block in blocks]
        self.rows = sum(size for _, _, size in blocks[0])

    def bind(self, refs, slots, sems):
        self.refs, self.slots, self.sems = windows(self.pieces, refs), slots, sems

    def copies(self, block, slot):
        first = sum(self.blocks[:block])
        result, start = [], 0
        for i in range(self.blocks[block]):
            size = self.pieces[first + i][2]
            result.append(
                pltpu.make_async_copy(
                    self.refs[first + i], self.slots.at[slot, pl.ds(start, size)], self.sems.at[slot, i]
                )
            )
            start += size
        return result

    def fetch(self, step):
        count = len(self.blocks)

        @pl.when(step == 0)
        def _():
            for copy in self.copies(0, 0):
                copy.start()

        for block in range(count):

            @pl.when(step == block)
            def _(block=block):
                if block + 1 < count:
                    for copy in self.copies(block + 1, (block + 1) % 2):
                        copy.start()
                for copy in self.copies(block, block % 2):
                    copy.wait()

        return self.slots[lax.rem(step, 2)]


def stream_scratch(rows, columns):
    return [pltpu.VMEM((2, rows, columns), jnp.bfloat16), pltpu.SemaphoreType.DMA((2, 2))]


def projection_copies(refs, place, target, sem):
    def at(w):
        rows = refs[0].shape[0] if w is None else refs[0].shape[0] * w
        return target.at[pl.ds(0, rows)] if w is None else target.at[pl.ds(rows, refs[0].shape[0])]

    return line_copies(refs, place, at, sem)


def forward_kernel(stream, win_pieces, *refs):
    ends_ref, mine_ref, place_ref, refs = refs[0], refs[1], refs[2], refs[3:]
    pieces, refs = refs[: len(stream.pieces)], refs[len(stream.pieces) :]
    win_refs, refs = refs[: len(win_pieces)], refs[len(win_pieces) :]
    (
        order_row_ref, order_column_ref, a_ref, b_ref, mask_ref, gap_ref, gain_ref,
        sent_ref, hid_out, normed_mine_out, zq_out, zg_out, mixed_ref, query_out, forget_out, value_out, states_ref,
        query_ref, forget_ref, value_ref, out_nat, state_now, win_ref, slots, sems, win_sem,
        hid_ref, normed_mine_ref, zq_ref, zg_ref, query_nat, forget_nat, value_nat, out_sems,
    ) = refs
    early = [(hid_ref, hid_out), (normed_mine_ref, normed_mine_out), (zq_ref, zq_out), (zg_ref, zg_out)]
    early += [(query_nat, query_out), (forget_nat, forget_out), (value_nat, value_out)]
    early = [pltpu.make_async_copy(here, there, out_sems.at[i]) for i, (here, there) in enumerate(early)]
    total, width = mixed_ref.shape
    heads = width // HEAD
    devices = sent_ref.shape[0]
    rows_each = total // devices
    stream.bind(pieces, slots, sems)
    win_copies = projection_copies(windows(win_pieces, win_refs), place_ref[0], win_ref, win_sem)
    go(win_copies, "start")
    win_ref[4 * width :, :] = a_ref[...]
    columns = pl.ds(pl.multiple_of(mine_ref[0] * width, 128), width)
    ranks = mask_ref.shape[1]
    go(win_copies, "wait")

    @pl.loop(0, devices)
    def _(step):
        block = stream.fetch(step)
        rows = pl.ds(pl.multiple_of(step * rows_each, rows_each), rows_each)
        normed_mine_ref[rows, :] = slots[lax.rem(step, 2), :, columns]
        main = mm(block, win_ref[...], NT)
        mask = mask_ref[rows, :].astype(jnp.float32)
        for j in range(4):
            lowered = main[:, 4 * width + j * ranks : 4 * width + (j + 1) * ranks] * mask
            hid_ref[rows, j * ranks : (j + 1) * ranks] = lowered.astype(jnp.bfloat16)
        main = main[:, : 4 * width] + mm(hid_ref[rows, :], b_ref[...], NT)
        zq = main[:, 0:width]
        zq_ref[rows, :] = zq
        query_ref[rows, :] = (zq * jax.nn.sigmoid(zq)).astype(jnp.bfloat16)
        forget_ref[rows, :] = main[:, width : 2 * width].astype(jnp.bfloat16)
        value_ref[rows, :] = main[:, 2 * width : 3 * width].astype(jnp.bfloat16)
        zg_ref[rows, :] = main[:, 3 * width : 4 * width]

    for copy in early[:4]:
        copy.start()
    move_rows(
        picks_natural(order_row_ref),
        ((query_ref, query_nat), (forget_ref, forget_nat), (value_ref, value_nat)),
    )
    for copy in early[4:]:
        copy.start()
    state_now[...] = jnp.zeros_like(state_now)
    lower = lower_ones()

    @pl.loop(0, total // CHUNK, unroll=2)
    def _(chunk):
        start = pl.multiple_of(chunk * CHUNK, CHUNK)
        rows = pl.ds(start, CHUNK)
        allowed, _, carry_ok, tail_ok, keep = segment_terms(ends_ref, start)
        for head in range(heads):
            lanes = slice(head * HEAD, (head + 1) * HEAD)
            query = query_nat[rows, lanes].astype(jnp.float32)
            value = value_nat[rows, lanes]
            _, keys, cumulative, middle, final = chunk_decays(
                forget_nat[rows, lanes].astype(jnp.float32), gap_ref[:, lanes], lower
            )
            grown = jnp.exp(cumulative - middle)
            shrunk = jnp.exp(middle - cumulative)
            scores = mm3(halves(query * grown), halves(keys * shrunk), NT)
            scores = jnp.where(allowed, scores, 0.0)
            state = state_now[head]
            states_ref[chunk, head] = state
            inter = mm3(halves(query * jnp.exp(cumulative) * carry_ok), halves(state), NT)
            out_nat[rows, lanes] = (mm2(halves(scores), value) + inter).astype(jnp.bfloat16)
            tail = keys * jnp.exp(final - cumulative) * tail_ok
            state_now[head] = state * (jnp.exp(final) * keep) + mm2r(value, halves(tail), TN)

    states_ref[total // CHUNK] = state_now[...]
    move_rows(picks_packed(order_column_ref), ((out_nat, mixed_ref),))

    for place, bits in enumerate(block_order(devices)):
        rows = slice(place * rows_each, (place + 1) * rows_each)
        target = mine_ref[0] ^ bits
        mixed = mixed_ref[rows, :].astype(jnp.float32)
        zg = zg_ref[rows, :]
        raw = mixed * gain_ref[...] * (zg * jax.nn.sigmoid(zg))
        sent_ref[target, 0:rows_each, :] = raw.astype(jnp.bfloat16)
        squares = halves(mixed * mixed)
        ones = jnp.ones((8, width), jnp.bfloat16)
        squares = (mm(ones, squares[0], NT) + mm(ones, squares[1], NT))[0:1]
        sent_ref[target, rows_each : rows_each + 16, :] = packed_lines([squares], width)
    for copy in early:
        copy.wait()


def mixer_forward(ends, mine, place, order, blocks, win_pieces, in_a_t, in_b_wide, mask, gap, gain):
    stream = Stream(blocks)
    devices = len(blocks)
    model = in_a_t.shape[1]
    total, width = stream.rows * devices, gap.shape[0]
    heads = width // HEAD
    ranks = mask.shape[1]
    rows = jax.ShapeDtypeStruct((total, width), jnp.bfloat16)
    wide_rows = jax.ShapeDtypeStruct((total, width), jnp.float32)
    states = jax.ShapeDtypeStruct((total // CHUNK + 1, heads, HEAD, HEAD), jnp.float32)
    sent = jax.ShapeDtypeStruct((devices, stream.rows + 16, width), jnp.bfloat16)
    hid = jax.ShapeDtypeStruct((total, 4 * ranks), jnp.bfloat16)
    return pl.pallas_call(
        lambda *refs: forward_kernel(stream, win_pieces, *refs),
        out_shape=(sent, hid, rows, wide_rows, wide_rows, rows, rows, rows, rows, states),
        in_specs=[SMEM] * 3 + [ANY] * (len(stream.pieces) + len(win_pieces)) + [VMEM] * 7,
        out_specs=(VMEM, ANY, ANY, ANY, ANY, VMEM, ANY, ANY, ANY, VMEM),
        scratch_shapes=[pltpu.VMEM((total, width), jnp.bfloat16)] * 4
        + [pltpu.VMEM((heads, HEAD, HEAD), jnp.float32), pltpu.VMEM((4 * (width + ranks), model), jnp.bfloat16)]
        + stream_scratch(stream.rows, model)
        + [pltpu.SemaphoreType.DMA(())]
        + [pltpu.VMEM(array.shape, array.dtype) for array in (hid, rows, wide_rows, wide_rows, rows, rows, rows)]
        + [pltpu.SemaphoreType.DMA((7,))],
        compiler_params=params(62),
        cost_estimate=cost(57),
    )(
        ends, mine, place, *stream.arrays, *arrays_of(win_pieces), *order,
        in_a_t, in_b_wide, mask, gap.reshape(1, width), gain.reshape(1, width),
    )


def backward_kernel(win_pieces, *refs):
    ends_ref, mine_ref, place_ref, refs = refs[0], refs[1], refs[2], refs[3:]
    win_refs, refs = windows(win_pieces, refs), refs[len(win_pieces) :]
    late, refs = refs[:7], refs[7:]
    (
        order_row_ref, order_column_ref, came_ref, zg_ref, mixed_ref, gap_ref, gain_ref, mask_ref, fold_ref,
        g_proj_ref, gated_ref, small_ref, b_rows_ref, spread_out,
        grad_ref, grad_nat, d_query_nat, d_forget_nat, d_value_nat, slope_now,
        query_nat, forget_nat, value_nat, states_ref, zq_ref, hid_ref, b_ref, late_sems,
        win_ref, win_sem, spread_ref, spread_sems,
    ) = refs
    late = [
        pltpu.make_async_copy(there, here, late_sems.at[i])
        for i, (there, here) in enumerate(
            zip(late, (query_nat, forget_nat, value_nat, states_ref, zq_ref, hid_ref, b_ref))
        )
    ]
    for copy in late:
        copy.start()
    win_copies = projection_copies(win_refs, place_ref[0], win_ref, win_sem)
    go(win_copies, "start")
    total, width = mixed_ref.shape
    heads = width // HEAD
    devices = came_ref.shape[0]
    rows_each = total // devices

    for place, bits in enumerate(block_order(devices)):
        rows = slice(place * rows_each, (place + 1) * rows_each)
        source = mine_ref[0] ^ bits
        d_gated = came_ref[source, 0:rows_each, :].astype(jnp.float32)
        scalars = came_ref[source, rows_each : rows_each + 16, :].astype(jnp.float32)
        factor, mean = [
            jnp.concatenate([row_to_column(row) for row in unpacked_row(scalars, i, rows_each // width)])
            for i in range(2)
        ]
        mixed = mixed_ref[rows, :].astype(jnp.float32)
        zg = zg_ref[rows, :]
        sigma = jax.nn.sigmoid(zg)
        silu = zg * sigma
        gained = mixed * gain_ref[...]
        gated_ref[rows, :] = ((gained * silu).astype(jnp.bfloat16).astype(jnp.float32) * factor).astype(jnp.bfloat16)
        d_zg = d_gated * (gained * factor) * (sigma * (1.0 + zg * (1.0 - sigma)))
        g_proj_ref[rows, 3 * width : 4 * width] = d_zg.astype(jnp.bfloat16)
        scaled = d_gated * gain_ref[...] * silu
        cube = factor * factor * factor
        grad_ref[rows, :] = (factor * scaled - mixed * (cube * mean)).astype(jnp.bfloat16)

    move_rows(picks_natural(order_row_ref), ((grad_ref, grad_nat),))
    for copy in late[:4]:
        copy.wait()
    slope_now[...] = jnp.zeros_like(slope_now)
    lower = lower_ones()

    @pl.loop(0, total // CHUNK, unroll=2)
    def _(step):
        chunk = total // CHUNK - 1 - step
        start = pl.multiple_of(chunk * CHUNK, CHUNK)
        rows = pl.ds(start, CHUNK)
        allowed, later, carry_ok, tail_ok, keep = segment_terms(ends_ref, start)
        later = jnp.where(later, 1.0, 0.0).astype(jnp.bfloat16)
        for head in range(heads):
            lanes = slice(head * HEAD, (head + 1) * HEAD)
            query = query_nat[rows, lanes].astype(jnp.float32)
            value = value_nat[rows, lanes]
            grad = grad_nat[rows, lanes]
            sigma, keys, cumulative, middle, final = chunk_decays(
                forget_nat[rows, lanes].astype(jnp.float32), gap_ref[:, lanes], lower
            )
            grown = jnp.exp(cumulative - middle)
            shrunk = jnp.exp(middle - cumulative)
            query_grown = halves(query * grown)
            keys_shrunk = halves(keys * shrunk)
            scores = halves(jnp.where(allowed, mm3(query_grown, keys_shrunk, NT), 0.0))
            d_scores = halves(jnp.where(allowed, mm(grad, value, NT), 0.0))
            state = halves(states_ref[chunk, head])
            slope = slope_now[head]
            slope_parts = halves(slope)
            from_start = jnp.exp(cumulative) * carry_ok
            to_end = jnp.exp(final - cumulative) * tail_ok
            d_query = mm3(d_scores, keys_shrunk) * grown + mm2r(grad, state) * from_start
            d_keys = mm3(d_scores, query_grown, TN) * shrunk + mm2r(value, slope_parts) * to_end
            d_value = mm2(scores, grad, TN) + mm3(halves(keys * to_end), slope_parts, NT)
            past = jnp.sum(states_ref[chunk + 1, head] * slope, axis=0, keepdims=True)
            d_logf = sum_with(later, query * d_query - keys * d_keys) + tail_ok * past
            d_keys = d_keys - d_logf / (1.0 - keys)
            slope_now[head] = slope * (jnp.exp(final) * keep) + mm2r(grad, halves(query * from_start), TN)
            d_query_nat[rows, lanes] = d_query.astype(jnp.bfloat16)
            d_forget_nat[rows, lanes] = (-d_keys * keys * sigma).astype(jnp.bfloat16)
            d_value_nat[rows, lanes] = d_value.astype(jnp.bfloat16)

    picks = picks_packed(order_column_ref)
    for copy in late[4:]:
        copy.wait()

    @pl.loop(0, total // TILE)
    def _(tile):
        start = pl.multiple_of(tile * TILE, TILE)
        rows = pl.ds(start, TILE)
        chosen = picks(start, total)
        zq = zq_ref[rows, :]
        sigma = jax.nn.sigmoid(zq)
        d_query = mm(chosen, d_query_nat[...])
        g_proj_ref[rows, 0:width] = (d_query * (sigma * (1.0 + zq * (1.0 - sigma)))).astype(jnp.bfloat16)
        g_proj_ref[rows, width : 2 * width] = mm(chosen, d_forget_nat[...]).astype(jnp.bfloat16)
        g_proj_ref[rows, 2 * width : 3 * width] = mm(chosen, d_value_nat[...]).astype(jnp.bfloat16)
        mask = mask_ref[rows, :].astype(jnp.float32)
        through = mm(g_proj_ref[rows, :], b_ref[...])
        ranks = mask.shape[1]
        parts = [(through[:, j * ranks : (j + 1) * ranks] * mask).astype(jnp.bfloat16) for j in range(4)]
        small_ref[rows, :] = mm(jnp.concatenate(parts, axis=1), fold_ref[...]).astype(jnp.bfloat16)

    go(win_copies, "wait")
    half = devices // 2

    def spread_copy(block, slot):
        rows = pl.ds(pl.multiple_of(block * rows_each, rows_each), rows_each)
        return pltpu.make_async_copy(spread_ref.at[slot], spread_out.at[rows], spread_sems.at[slot])

    @pl.loop(0, half)
    def _(block):
        slot = lax.rem(block, 2)

        @pl.when(block >= 2)
        def _():
            spread_copy(block - 2, slot).wait()

        rows = pl.ds(pl.multiple_of((block + half) * rows_each, rows_each), rows_each)
        spread_ref[slot] = mm(g_proj_ref[rows, :], win_ref[...]).astype(jnp.bfloat16)
        spread_copy(block, slot).start()

    ranks = mask_ref.shape[1]
    for j in range(4):
        b_rows_ref[:, j * width : (j + 1) * width] = mm(
            hid_ref[:, j * ranks : (j + 1) * ranks], g_proj_ref[:, j * width : (j + 1) * width], TN
        )
    for block in range(half - 2, half):
        spread_copy(block, block % 2).wait()


def mixer_backward(ends, mine, place, order, came, kept, win_pieces, gap, gain, hid_in, in_b_wide, mask, fold):
    zq, zg, mixed, query, forget, value, states = kept
    total, width = zq.shape
    ranks = mask.shape[1]
    heads = width // HEAD
    devices = came.shape[0]
    rows_each = total // devices
    model = win_pieces[0][0].shape[1]
    rows = jax.ShapeDtypeStruct((total, width), jnp.bfloat16)
    late = (query, forget, value, states, zq, hid_in, in_b_wide)
    return pl.pallas_call(
        lambda *refs: backward_kernel(win_pieces, *refs),
        out_shape=(
            jax.ShapeDtypeStruct((total, 4 * width), jnp.bfloat16),
            rows,
            jax.ShapeDtypeStruct((total, ranks), jnp.bfloat16),
            jax.ShapeDtypeStruct((ranks, 4 * width), jnp.float32),
            jax.ShapeDtypeStruct((total // 2, model), jnp.bfloat16),
        ),
        in_specs=[SMEM] * 3 + [ANY] * (len(win_pieces) + len(late)) + [VMEM] * 9,
        out_specs=(VMEM,) * 4 + (ANY,),
        scratch_shapes=[pltpu.VMEM((total, width), jnp.bfloat16)] * 5
        + [pltpu.VMEM((heads, HEAD, HEAD), jnp.float32)]
        + [pltpu.VMEM(array.shape, array.dtype) for array in late]
        + [pltpu.SemaphoreType.DMA((len(late),))]
        + [pltpu.VMEM((4 * width, model), jnp.bfloat16), pltpu.SemaphoreType.DMA(())]
        + [pltpu.VMEM((2, rows_each, model), jnp.bfloat16), pltpu.SemaphoreType.DMA((2,))],
        compiler_params=params(62),
        cost_estimate=cost(51),
    )(
        ends, mine, place, *arrays_of(win_pieces), *late, *order, came, zg, mixed,
        gap.reshape(1, width), gain.reshape(1, width), mask, fold,
    )


def spans(blocks):
    result = []
    for index, block in enumerate(blocks):
        start = 0
        for piece in block:
            result.append((index, start, piece.shape[0]))
            start += piece.shape[0]
    return result


def token_forward_kernel(where, count, *refs):
    mine_ref, came_ref, x_ref, a_ref, b_ref, mask_ref, gain_ref = refs[:7]
    weights, refs = refs[7 : 7 + count], refs[7 + count :]
    resid_ref, normed_ref, hid_ref, all_ref, gated_ref, a_mine, sems = refs
    devices = came_ref.shape[0]
    rows, model = x_ref.shape
    width = came_ref.shape[2]
    bits = block_order(devices)
    copies = [
        pltpu.make_async_copy(weights[i], all_ref.at[pl.ds(block * width + start, size)], sems.at[i])
        for i, (block, start, size) in enumerate(where)
    ]
    for copy in copies:
        copy.start()
    squares = jnp.zeros((1, rows), jnp.float32)
    for d in range(devices):
        lines = came_ref[d, rows : rows + 16, :].astype(jnp.float32)
        squares = squares + jnp.concatenate(unpacked_row(lines, 0, rows // width), axis=1)
    factor = lax.rsqrt(row_to_column(squares) / model + eps_norm)
    for place, bit in enumerate(bits):
        source = mine_ref[0] ^ bit
        lanes = slice(place * width, (place + 1) * width)
        raw = came_ref[source, 0:rows, :].astype(jnp.float32)
        gated_ref[:, lanes] = (raw * factor).astype(jnp.bfloat16)
        a_mine[lanes, :] = a_ref[pl.ds(pl.multiple_of(source * width, 128), width), :]
    gated = gated_ref[...]
    hid = (mm(gated, a_mine[...]) * mask_ref[...].astype(jnp.float32)).astype(jnp.bfloat16)
    hid_ref[...] = hid
    extra = mm(hid, b_ref[...], NT)
    for copy in copies:
        copy.wait()
    resid = x_ref[...].astype(jnp.float32) + mm(gated, all_ref[...]) + extra
    resid_ref[...] = resid
    factor = lax.rsqrt(jnp.mean(resid * resid, axis=-1, keepdims=True) + eps_norm)
    normed_ref[...] = (resid * factor * gain_ref[...]).astype(jnp.bfloat16)


def token_forward(mine, came, x, out_a, out_b, mask_own, gain, weights):
    rows, model = x.shape
    where = spans(weights)
    pieces = [piece for block in weights for piece in block]
    ranks = out_a.shape[1]
    return pl.pallas_call(
        lambda *refs: token_forward_kernel(where, len(pieces), *refs),
        out_shape=(
            jax.ShapeDtypeStruct((rows, model), jnp.float32),
            jax.ShapeDtypeStruct((rows, model), jnp.bfloat16),
            jax.ShapeDtypeStruct((rows, ranks), jnp.bfloat16),
        ),
        in_specs=[SMEM] + [VMEM] * 6 + [ANY] * len(pieces),
        out_specs=(VMEM,) * 3,
        scratch_shapes=[
            pltpu.VMEM((model, model), jnp.bfloat16),
            pltpu.VMEM((rows, model), jnp.bfloat16),
            pltpu.VMEM((model, ranks), jnp.bfloat16),
            pltpu.SemaphoreType.DMA((len(pieces),)),
        ],
        compiler_params=params(62),
        cost_estimate=cost(8),
    )(mine, came, x, out_a, out_b, mask_own, gain.reshape(1, model), *pieces)


def summed(refs):
    own, other, from_x, from_y = refs
    total = own[...].astype(jnp.float32) + other[...].astype(jnp.float32)
    for pieces in (from_x, from_y):
        if pieces:
            total = total + jnp.concatenate([piece[...] for piece in pieces]).astype(jnp.float32)
    return total


def first_block(rows, columns):
    return pl.BlockSpec((rows, columns), lambda i: (0, 0))


def whole(array):
    return pl.BlockSpec(array.shape, lambda i: (0,) * array.ndim)


def token_backward_kernel(where, count, near, nears, *refs):
    mine_ref, came_ref, cot_ref, resid_ref, a_ref, b_ref, mask_ref, gain_ref, hid_ref, own, other = refs[:11]
    refs = refs[11:]
    from_x, from_y, refs = refs[:near], refs[near:nears], refs[nears:]
    weights, refs = refs[:count], refs[count:]
    sent_ref, d_resid_ref, d_hid_ref, b_rows_ref, all_ref, sems = refs
    devices = came_ref.shape[0]
    rows, model = resid_ref.shape
    width = came_ref.shape[2]
    copies = [
        pltpu.make_async_copy(weights[i], all_ref.at[pl.ds(block * width + start, size)], sems.at[i])
        for i, (block, start, size) in enumerate(where)
    ]
    for copy in copies:
        copy.start()
    squares = jnp.zeros((1, rows), jnp.float32)
    for d in range(devices):
        lines = came_ref[d, rows : rows + 16, :].astype(jnp.float32)
        squares = squares + jnp.concatenate(unpacked_row(lines, 0, rows // width), axis=1)
    factor_two = lax.rsqrt(squares / model + eps_norm)

    resid = resid_ref[...]
    factor = lax.rsqrt(jnp.mean(resid * resid, axis=-1, keepdims=True) + eps_norm)
    scaled = summed((own, other, from_x, from_y)) * gain_ref[...]
    mean = jnp.mean(resid * scaled, axis=-1, keepdims=True)
    d_resid = cot_ref[...].astype(jnp.float32) + factor * scaled - resid * (factor * factor * factor * mean)
    d_resid_ref[...] = d_resid
    g_attn = d_resid.astype(jnp.bfloat16)
    d_hid = (mm(g_attn, b_ref[...]) * mask_ref[...].astype(jnp.float32)).astype(jnp.bfloat16)
    d_hid_ref[...] = d_hid
    b_rows_ref[...] = mm(g_attn, hid_ref[...], TN)
    for copy in copies:
        copy.wait()
    total = jnp.zeros((rows, 1), jnp.float32)
    for place, bit in enumerate(block_order(devices)):
        target = mine_ref[0] ^ bit
        block = slice(place * width, (place + 1) * width)
        a_block = a_ref[pl.ds(pl.multiple_of(target * width, 128), width), :]
        d_gated = mm(g_attn, all_ref[block, :], NT) + mm(d_hid, a_block, NT)
        raw = came_ref[target, 0:rows, :].astype(jnp.float32)
        total = total + jnp.sum(raw * d_gated, axis=-1, keepdims=True)
        sent_ref[target, 0:rows, :] = d_gated.astype(jnp.bfloat16)
    lines = packed_lines([factor_two, column_to_row(total / model)], width)
    for d in range(devices):
        sent_ref[d, rows : rows + 16, :] = lines


def token_backward(mine, came, cot, resid, out_a, out_b, mask_own, gain, hid, parts, weights):
    rows, model = resid.shape
    own, other, from_x, from_y = parts
    where = spans(weights)
    pieces = [piece for block in weights for piece in block]
    ranks = out_a.shape[1]
    fixed = [came, cot, resid, out_a, out_b, mask_own, gain.reshape(1, model), hid]
    return pl.pallas_call(
        lambda *refs: token_backward_kernel(where, len(pieces), len(from_x), len(from_x + from_y), *refs),
        grid=(1,),
        out_shape=(
            jax.ShapeDtypeStruct(came.shape, jnp.bfloat16),
            jax.ShapeDtypeStruct((rows, model), jnp.float32),
            jax.ShapeDtypeStruct((rows, ranks), jnp.bfloat16),
            jax.ShapeDtypeStruct((model, ranks), jnp.float32),
        ),
        in_specs=[SMEM] + [whole(array) for array in fixed] + [first_block(rows, model)] * 2
        + [whole(piece) for piece in from_x + from_y] + [ANY] * len(pieces),
        out_specs=(
            pl.BlockSpec(came.shape, lambda i: (0, 0, 0)),
            first_block(rows, model),
            first_block(rows, ranks),
            first_block(model, ranks),
        ),
        scratch_shapes=[
            pltpu.VMEM((model, model), jnp.bfloat16),
            pltpu.SemaphoreType.DMA((len(pieces),)),
        ],
        compiler_params=params(62),
        cost_estimate=cost(12),
    )(mine, *fixed, own, other, *from_x, *from_y, *pieces)


def token_end_kernel(near, nears, *refs):
    x_ref, d_resid_ref, d_hid_ref, a_ref, gain_ref, own, other = refs[:7]
    refs = refs[7:]
    from_x, from_y, out_ref = refs[:near], refs[near:nears], refs[nears]
    x = x_ref[...].astype(jnp.float32)
    factor = lax.rsqrt(jnp.mean(x * x, axis=-1, keepdims=True) + eps_norm)
    d_normed = summed((own, other, from_x, from_y)) + mm(d_hid_ref[...], a_ref[...], NT)
    scaled = d_normed * gain_ref[...]
    mean = jnp.mean(x * scaled, axis=-1, keepdims=True)
    out = d_resid_ref[...] + factor * scaled - x * (factor * factor * factor * mean)
    out_ref[...] = out.astype(jnp.bfloat16)


def token_end(x, d_resid, d_hid, in_a, gain, parts):
    rows, model = x.shape
    own, other, from_x, from_y = parts
    fixed = [x, d_resid]
    return pl.pallas_call(
        lambda *refs: token_end_kernel(len(from_x), len(from_x + from_y), *refs),
        grid=(1,),
        out_shape=jax.ShapeDtypeStruct((rows, model), jnp.bfloat16),
        in_specs=[whole(x), whole(d_resid), first_block(rows, d_hid.shape[1]), whole(in_a), first_block(1, model)]
        + [first_block(rows, model)] * 2 + [whole(piece) for piece in from_x + from_y],
        out_specs=first_block(rows, model),
        compiler_params=params(62),
        cost_estimate=cost(4),
    )(x, d_resid, d_hid, in_a, gain.reshape(1, model), own, other, *from_x, *from_y)


def both_copies(refs, place, target, padded, sem):
    if len(refs) == 2:
        size = refs[0].shape[0]
        return [(None, pltpu.make_async_copy(refs[i], window(target, i * padded, size), sem)) for i in range(2)]
    groups = [refs[i : i + 6] for i in range(0, len(refs), 6)]
    units = sum(group[0].shape[0] for group in groups)
    copies, first = [], 0
    for group in groups:
        size = group[0].shape[0]

        def at(w, first=first, size=size):
            return window(target, w // 2 * padded + w % 2 * units + first, size)

        copies += line_copies(group, place, at, sem)
        first += size
    return copies


def hidden_of(refs):
    if len(refs) == 2:
        return refs[0].shape[0]
    return 2 * sum(refs[i].shape[0] for i in range(0, len(refs), 6))


def load_both(refs, place, w_all, ffn_a_ref, padded, sem):
    copies = both_copies(refs, place, w_all, padded, sem)
    go(copies, "start")
    hidden_units = hidden_of(refs)
    if padded > hidden_units:
        blank = jnp.zeros((padded - hidden_units, w_all.shape[1]), jnp.bfloat16)
        w_all[hidden_units:padded, :] = blank
        w_all[padded + hidden_units : 2 * padded, :] = blank
    w_all[2 * padded :, :] = ffn_a_ref[...]
    return copies


def ffn_up_kernel(stream, ffn_pieces, *refs):
    mine_ref, place_ref, refs = refs[0], refs[1], refs[2:]
    pieces, refs = refs[: len(stream.pieces)], refs[len(stream.pieces) :]
    weights, refs = windows(ffn_pieces, refs), refs[len(ffn_pieces) :]
    mask_ref, ffn_a_ref, both_b_ref, both_ref, hid_ref, mine_out_ref, w_all, slots, sems, ffn_sem = refs
    step = pl.program_id(0)
    stream.bind(pieces, slots, sems)
    padded = both_b_ref.shape[0] // 2
    wide = mine_out_ref.shape[1]

    @pl.when(step == 0)
    def _():
        go(load_both(weights, place_ref[0], w_all, ffn_a_ref, padded, ffn_sem), "wait")

    normed = stream.fetch(step)
    columns = pl.ds(pl.multiple_of(mine_ref[0] * wide, 128), wide)
    mine_out_ref[...] = slots[lax.rem(step, 2), :, columns]
    mask = mask_ref[...].astype(jnp.float32)
    main = mm(normed, w_all[...], NT)
    hid = (main[:, 2 * padded :] * jnp.concatenate([mask, mask], axis=1)).astype(jnp.bfloat16)
    hid_ref[...] = hid
    both_ref[...] = main[:, : 2 * padded] + mm(hid, both_b_ref[...], NT)


def ffn_up(mine, place, normed, weights, mask, ffn_a_t, both_b, wide):
    stream = Stream(normed)
    rows, model = stream.rows, ffn_a_t.shape[1]
    total = rows * len(normed)
    ranks = mask.shape[1]
    padded = both_b.shape[0] // 2
    return pl.pallas_call(
        lambda *refs: ffn_up_kernel(stream, weights, *refs),
        grid=(len(normed),),
        out_shape=(
            jax.ShapeDtypeStruct((total, 2 * padded), jnp.float32),
            jax.ShapeDtypeStruct((total, 2 * ranks), jnp.bfloat16),
            jax.ShapeDtypeStruct((total, wide), jnp.bfloat16),
        ),
        in_specs=[SMEM] * 2
        + [ANY] * (len(stream.pieces) + len(weights))
        + [tile_spec(rows, ranks), whole(ffn_a_t), whole(both_b)],
        out_specs=(tile_spec(rows, 2 * padded), tile_spec(rows, 2 * ranks), tile_spec(rows, wide)),
        scratch_shapes=[pltpu.VMEM((2 * padded + 2 * ranks, model), jnp.bfloat16)]
        + stream_scratch(rows, model)
        + [pltpu.SemaphoreType.DMA(())],
        compiler_params=params(62),
        cost_estimate=cost(28),
    )(mine, place, *stream.arrays, *arrays_of(weights), mask, ffn_a_t, both_b)


def ffn_back_kernel(stream, ffn_pieces, down_pieces, *refs):
    mine_ref, place_ref, refs = refs[0], refs[1], refs[2:]
    pieces, refs = refs[: len(stream.pieces)], refs[len(stream.pieces) :]
    weights, refs = windows(ffn_pieces, refs), refs[len(ffn_pieces) :]
    downs, refs = windows(down_pieces, refs), refs[len(down_pieces) :]
    (
        both_ref, hid_ref, mask_ref, ffn_a_ref, both_b_ref, down_a_ref, down_b_ref, fold_ref,
        back_ref, down_ref, small_ref, cot_mine_ref, down_rows, both_rows,
        w_all, w_down, left_both, left_down, slots, sems, ffn_sem, down_sem,
    ) = refs
    step = pl.program_id(0)
    stream.bind(pieces, slots, sems)
    padded = down_a_ref.shape[0]
    model = w_down.shape[1]
    wide = cot_mine_ref.shape[1]

    @pl.when(step == 0)
    def _():
        hidden_units = hidden_of(weights)
        if len(downs) == 1:
            down = line_copies(downs, place_ref[0], lambda w: window(w_down, 0, hidden_units), down_sem)
        else:
            strip = downs[0].shape[0]
            narrow = model * strip // hidden_units
            down = []
            for part in range(hidden_units // strip):
                down += line_copies(
                    [ref.at[:, pl.ds(part * narrow, narrow)] for ref in downs],
                    place_ref[0],
                    lambda w, part=part: w_down.at[pl.ds(part * strip, strip), pl.ds(w * narrow, narrow)],
                    down_sem,
                )
        go(down, "start")
        if padded > hidden_units:
            w_down[hidden_units:padded, :] = jnp.zeros((padded - hidden_units, model), jnp.bfloat16)
        w_down[padded:, :] = down_b_ref[...]
        load_both(weights, place_ref[0], w_all, ffn_a_ref, padded, ffn_sem)
        go(down, "wait")
        down_rows[...] = jnp.zeros_like(down_rows)
        both_rows[...] = jnp.zeros_like(both_rows)

    cot = stream.fetch(step)
    columns = pl.ds(pl.multiple_of(mine_ref[0] * wide, 128), wide)
    cot_mine_ref[...] = slots[lax.rem(step, 2), :, columns]
    mask = mask_ref[...].astype(jnp.float32)
    hid = hid_ref[...]
    main = mm(cot, w_down[...], NT)
    d_hid = (main[:, padded:] * mask).astype(jnp.bfloat16)
    d_hidden = main[:, :padded] + mm(d_hid, down_a_ref[...], NT)
    gate, upper = both_ref[:, :padded], both_ref[:, padded:]
    sigma = jax.nn.sigmoid(gate)
    silu = gate * sigma
    left_down[:, :padded] = (silu * upper).astype(jnp.bfloat16)
    left_both[:, :padded] = (d_hidden * upper * (sigma * (1.0 + gate * (1.0 - sigma)))).astype(jnp.bfloat16)
    left_both[:, padded : 2 * padded] = (d_hidden * silu).astype(jnp.bfloat16)
    mask_two = jnp.concatenate([mask, mask], axis=1)

    @pl.when(step == 0)
    def _():
        go(both_copies(weights, place_ref[0], w_all, padded, ffn_sem), "wait")

    through = (mm(left_both[:, : 2 * padded], both_b_ref[...]) * mask_two).astype(jnp.bfloat16)
    left_both[:, 2 * padded :] = through
    back_ref[...] = mm(left_both[...], w_all[...]).astype(jnp.bfloat16)
    low = (mm(left_down[:, :padded], down_a_ref[...]) * mask).astype(jnp.bfloat16)
    left_down[:, padded:] = low
    down_ref[...] = mm(left_down[...], w_down[...]).astype(jnp.bfloat16)
    small_ref[...] = mm(jnp.concatenate([low, through], axis=1), fold_ref[...]).astype(jnp.bfloat16)
    down_rows[...] += mm(d_hid, left_down[:, :padded], TN)
    both_rows[...] += mm(hid, left_both[:, : 2 * padded], TN)


def ffn_back(mine, place, cot, weights, downs, both, hid, mask, first, ffn_a_t, both_b, down_a, down_b_t, fold, wide):
    stream = Stream(cot)
    rows, model = stream.rows, ffn_a_t.shape[1]
    blocks = len(cot)
    total = rows * blocks
    padded, ranks = down_a.shape
    fixed = [ffn_a_t, both_b, down_a, down_b_t, fold]
    grown = jax.ShapeDtypeStruct((total, model), jnp.bfloat16)

    def from_first(columns):
        return pl.BlockSpec((rows, columns), lambda i: (i + first, 0))

    return pl.pallas_call(
        lambda *refs: ffn_back_kernel(stream, weights, downs, *refs),
        grid=(blocks,),
        out_shape=(
            grown, grown, jax.ShapeDtypeStruct((total, ranks), jnp.bfloat16),
            jax.ShapeDtypeStruct((total, wide), jnp.bfloat16),
            jax.ShapeDtypeStruct((ranks, padded), jnp.float32),
            jax.ShapeDtypeStruct((2 * ranks, 2 * padded), jnp.float32),
        ),
        in_specs=[SMEM] * 2
        + [ANY] * (len(stream.pieces) + len(weights) + len(downs))
        + [from_first(2 * padded), from_first(2 * ranks), from_first(ranks)]
        + [whole(array) for array in fixed],
        out_specs=(
            tile_spec(rows, model), tile_spec(rows, model), tile_spec(rows, ranks), tile_spec(rows, wide),
            first_block(ranks, padded), first_block(2 * ranks, 2 * padded),
        ),
        scratch_shapes=[
            pltpu.VMEM((2 * padded + 2 * ranks, model), jnp.bfloat16),
            pltpu.VMEM((padded + ranks, model), jnp.bfloat16),
            pltpu.VMEM((rows, 2 * padded + 2 * ranks), jnp.bfloat16),
            pltpu.VMEM((rows, padded + ranks), jnp.bfloat16),
        ]
        + stream_scratch(rows, model)
        + [pltpu.SemaphoreType.DMA(()), pltpu.SemaphoreType.DMA(())],
        compiler_params=params(62),
        cost_estimate=cost(33),
    )(mine, place, *stream.arrays, *arrays_of(weights), *arrays_of(downs), both, hid, mask, *fixed)


def spread_kernel(win_pieces, *refs):
    place_ref, refs = refs[0], refs[1:]
    pieces, refs = windows(win_pieces, refs), refs[len(win_pieces) :]
    x_ref, out_ref, win_ref, sem = refs
    copies = projection_copies(pieces, place_ref[0], win_ref, sem)

    @pl.when(pl.program_id(0) == 0)
    def _():
        go(copies, "start")
        go(copies, "wait")

    out_ref[...] = mm(x_ref[...], win_ref[...]).astype(jnp.bfloat16)


def spread(place, values, win_pieces, first, blocks, rows):
    inner = values.shape[1]
    model = win_pieces[0][0].shape[1]
    return pl.pallas_call(
        lambda *refs: spread_kernel(win_pieces, *refs),
        grid=(blocks,),
        out_shape=jax.ShapeDtypeStruct((rows * blocks, model), jnp.bfloat16),
        in_specs=[SMEM] + [ANY] * len(win_pieces) + [pl.BlockSpec((rows, inner), lambda i: (i + first, 0))],
        out_specs=tile_spec(rows, model),
        scratch_shapes=[pltpu.VMEM((inner, model), jnp.bfloat16), pltpu.SemaphoreType.DMA(())],
        compiler_params=params(62),
        cost_estimate=cost(8),
    )(place, *arrays_of(win_pieces), values)


def pack_in_kernel(mine_ref, win_ref, wout_ref, out_ref, window, sems):
    wide, model = window.shape[1], window.shape[0]
    narrow = wout_ref.shape[1]
    strips = model // narrow
    strip = wide // strips
    start = pl.multiple_of(mine_ref[0] * wide, 128)
    copies = [pltpu.make_async_copy(win_ref.at[:, pl.ds(start, wide)], window, sems.at[0])]
    for part in range(strips):
        copies.append(
            pltpu.make_async_copy(
                wout_ref.at[pl.ds(pl.multiple_of(start + part * strip, 16), strip)],
                out_ref.at[pl.ds(wide, strip), pl.ds(part * narrow, narrow)],
                sems.at[1 + part],
            )
        )
    for copy in copies:
        copy.start()
    eye = lax.broadcasted_iota(jnp.int32, (wide, wide), 0) == lax.broadcasted_iota(jnp.int32, (wide, wide), 1)
    eye = jnp.where(eye, 1.0, 0.0).astype(jnp.bfloat16)
    for copy in copies:
        copy.wait()
    out_ref[0:wide, :] = mm(eye, window[...], NT).astype(jnp.bfloat16)


def pack_in(mine, w_in, w_out, wide):
    model, narrow = w_in.shape[0], w_out.shape[1]
    strips = model // narrow
    return pl.pallas_call(
        pack_in_kernel,
        out_shape=jax.ShapeDtypeStruct((wide + wide // strips, model), jnp.bfloat16),
        in_specs=[SMEM, ANY, ANY],
        out_specs=VMEM,
        scratch_shapes=[pltpu.VMEM((model, wide), jnp.bfloat16), pltpu.SemaphoreType.DMA((1 + strips,))],
        compiler_params=params(62),
        cost_estimate=cost(3),
    )(mine, w_in, w_out)


def pack_ffn_kernel(units, mine_ref, wffn_ref, wdown_ref, out_ref, held, sems):
    model, columns = wffn_ref.shape
    span = held.shape[1]
    narrow = wdown_ref.shape[1]
    parts = model // narrow
    shards = wdown_ref.shape[0] // (units * 8)
    strip = units * shards // parts
    wanted = mine_ref[0] * units
    start = jnp.minimum(wanted // 128 * 128, columns - span)
    copies = [pltpu.make_async_copy(wffn_ref.at[:, pl.ds(pl.multiple_of(start, 128), span)], held, sems.at[0])]
    for part in range(parts):
        shard, inside = part * strip // units, part * strip % units
        source = shard * units * 8 + wanted + inside
        copies.append(
            pltpu.make_async_copy(
                wdown_ref.at[pl.ds(pl.multiple_of(source, 16), strip)],
                out_ref.at[pl.ds(units, strip), pl.ds(part * narrow, narrow)],
                sems.at[1 + part],
            )
        )
    for copy in copies:
        copy.start()
    rows = lax.broadcasted_iota(jnp.int32, (units, span), 0) + (wanted - start)
    chosen = jnp.where(rows == lax.broadcasted_iota(jnp.int32, (units, span), 1), 1.0, 0.0).astype(jnp.bfloat16)
    for copy in copies:
        copy.wait()
    out_ref[0:units, :] = mm(chosen, held[...], NT).astype(jnp.bfloat16)


def pack_ffn(mine, w_ffn, w_down, units):
    model, columns = w_ffn.shape
    span = min(columns, (units + 127) // 128 * 128 + 128)
    parts = model // w_down.shape[1]
    return pl.pallas_call(
        lambda *refs: pack_ffn_kernel(units, *refs),
        out_shape=jax.ShapeDtypeStruct((units + 2 * units // parts, model), jnp.bfloat16),
        in_specs=[SMEM, ANY, ANY],
        out_specs=VMEM,
        scratch_shapes=[pltpu.VMEM((model, span), jnp.bfloat16), pltpu.SemaphoreType.DMA((1 + parts,))],
        compiler_params=params(62),
        cost_estimate=cost(3),
    )(mine, w_ffn, w_down)


def unpack_out_kernel(pieces, *refs):
    place_ref, out, sem = refs[0], refs[-2], refs[-1]
    refs = windows(pieces, refs[1:-2])
    strip = refs[0].shape[0]
    strips = out.shape[0] // strip
    narrow = out.shape[1] // strips
    copies = []
    for part in range(strips):
        copies += line_copies(
            [ref.at[:, pl.ds(part * narrow, narrow)] for ref in refs],
            place_ref[0],
            lambda w, part=part: out.at[pl.ds(part * strip, strip), pl.ds(w * narrow, narrow)],
            sem,
        )
    go(copies, "start")
    go(copies, "wait")


def unpack_out(place, pieces, wide):
    model = pieces[0][0].shape[1]
    return pl.pallas_call(
        lambda *refs: unpack_out_kernel(pieces, *refs),
        out_shape=jax.ShapeDtypeStruct((wide, model), pieces[0][0].dtype),
        in_specs=[SMEM] + [ANY] * len(pieces),
        out_specs=VMEM,
        scratch_shapes=[pltpu.SemaphoreType.DMA(())],
        compiler_params=params(62),
        cost_estimate=cost(2),
    )(place, *arrays_of(pieces))


ADAPTERS = 8
RANK = 16
RANKS = ADAPTERS * RANK
PROJECTIONS = 4
eps_norm = 1e-06
f32 = jnp.float32
bf16 = jnp.bfloat16


def sequence_of(positions, seq_lengths):
    bounds = jnp.cumsum(seq_lengths)[:-1]
    return jnp.sum((positions[:, None] >= bounds[None, :]).astype(jnp.int32), axis=1)


def adapter_of(seq_numbers, seq_ids):
    numbers = jnp.arange(seq_ids.shape[0], dtype=jnp.int32)
    return jnp.sum(
        (seq_numbers[:, None] == numbers[None, :]).astype(jnp.int32) * seq_ids[None, :], axis=1
    )


def adapter_mask(adapter, count=1):
    columns = jnp.arange(count * RANKS, dtype=jnp.int32) % RANKS // RANK
    return (columns[None, :] == adapter[:, None]).astype(bf16)


def norm_factor(values):
    return lax.rsqrt(jnp.mean(values * values, axis=-1, keepdims=True) + eps_norm)


def norm_back(values, factor, gain, grad):
    scaled = grad * gain
    return factor * scaled - values * factor**3 * jnp.mean(values * scaled, axis=-1, keepdims=True)


def silu_slope(values, sigma):
    return sigma * (1.0 + values * (1.0 - sigma))


def relative(blocks, index):
    count, rest = blocks.shape[0], blocks.shape[1:]
    bit = 1
    while bit < count:
        pairs = blocks.reshape((count // (2 * bit), 2, bit) + rest)
        blocks = jnp.where((index & bit) != 0, pairs[:, ::-1], pairs).reshape((count,) + rest)
        bit *= 2
    return blocks


def to_order(blocks, index):
    count = blocks.shape[0]
    blocks = relative(blocks, index)
    pairs = blocks.reshape((count // 2, 2) + blocks.shape[1:])
    return jnp.concatenate([pairs[:, 0], pairs[:, 1]])


def from_order(blocks, index):
    count = blocks.shape[0]
    pairs = jnp.stack([blocks[: count // 2], blocks[count // 2 :]], axis=1)
    return relative(pairs.reshape(blocks.shape), index)


def across(values, bits, axis="seq"):
    size = lax.axis_size(axis)
    return lax.ppermute(values, axis, [(i, i ^ bits) for i in range(size)])


def first_near(block):
    size = lax.axis_size("seq")
    return [across(block, k) for k in ((2, 4) if size == 8 else range(2, size, 2))]


def more_near(block, first):
    if len(first) != 2:
        return [[block]] + [[other] for other in first]
    by_x, by_y = first
    half = block.shape[0] // 2
    return [[block], [by_x], [by_y], [across(by_x[:half], 4), across(by_y[half:], 2)]]


def other_core(blocks):
    return [[across(piece, 1) for piece in block] for block in blocks]


def with_rows(blocks):
    return [[(piece, 0, piece.shape[0]) for piece in block] for block in blocks]


def two_blocks(blocks):
    half = blocks[0][0].shape[0] // 2
    upper = [[(block[0], 0, half)] for block in blocks]
    return upper, [[(block[0], half, half)] for block in blocks if block[0].shape[0] == 2 * half]


def scatter_parts(near, other):
    size = lax.axis_size("seq")
    rows = near.shape[0] // (size // 2)
    half = rows // 2

    def part(block, start, stop):
        at = slice(block * rows + start, block * rows + stop)
        return near[at].astype(f32) + other[at].astype(f32)

    if size != 8:
        return [part(i, 0, rows).astype(bf16) for i in range(1, size // 2)], []
    sent = [part(3, 0, half), part(3, half, rows), part(1, 0, half), part(2, half, rows)]
    return [piece.astype(bf16) for piece in sent], [part(1, half, rows), part(2, 0, half)]


def scatter_first(sent):
    bits = (2, 4, 2, 4) if lax.axis_size("seq") == 8 else [2 * i + 2 for i in range(len(sent))]
    return [across(piece, bit) for piece, bit in zip(sent, bits)]


def scatter_second(came, rest):
    if not rest:
        total = sum(piece.astype(f32) for piece in came).astype(bf16)
        return [total], []
    far_x, far_y, by_x, by_y = came
    by_x_more = across((rest[0] + far_y.astype(f32)).astype(bf16), 2)
    by_y_more = across((rest[1] + far_x.astype(f32)).astype(bf16), 4)
    return [by_x, by_x_more], [by_y_more, by_y]


def swap(values, axis="seq"):
    return lax.all_to_all(values, axis, split_axis=0, concat_axis=0, tiled=False)


def along(values, pairs):
    return lax.ppermute(values, "wt", pairs)


def first_pieces(block):
    return along(block, [(0, 1), (1, 2), (2, 3)]), along(block, [(1, 0), (2, 1), (3, 2)])


def more_pieces(first, start, size):
    place = lax.axis_index("wt")
    up, down = [piece[start : start + size] for piece in first]
    inner, outer = jnp.where(place == 1, up, down), jnp.where(place == 2, up, down)
    return [along(inner, [(1, 2), (2, 1)]), along(outer, [(2, 3), (1, 0)]), along(inner, [(1, 3), (2, 0)])]


def line_rows(block, first, more, start, size, more_start=0):
    return [(piece, start, size) for piece in (block,) + tuple(first)] + [(piece, more_start, size) for piece in more]


def after(values, *others):
    return lax.optimization_barrier((values,) + others)[0]


def to_owner(piece, count):
    size, lines = lax.axis_size("seq"), lax.axis_size("wt")
    each = lines // count
    moves = []
    for s in range(size):
        for q in range(lines):
            whole = (q // each) * size * each + s * each + q % each
            moves.append((s * lines + q, whole))
    return lax.ppermute(piece, ("seq", "wt"), moves)


def fold_columns(count, first):
    source = jnp.arange(count * RANKS)
    target = jnp.arange(RANKS)
    wanted = (first + source // RANKS) * RANK + source % RANK
    return (wanted[:, None] == target[None, :]).astype(bf16)


def local(
    tokens,
    cotangent,
    w_in,
    w_out,
    w_ffn,
    w_down,
    gain_mix,
    gain_gate,
    gain_ffn,
    forget_gap,
    in_a,
    in_b,
    out_a,
    out_b,
    ffn_a,
    ffn_b,
    down_a,
    down_b,
    order,
    lengths,
    adapter_ids,
):
    n, wt = lax.axis_size("seq"), lax.axis_size("wt")
    mine = lax.axis_index("seq")
    mine_ref = mine.astype(jnp.int32).reshape(1)
    place_ref = lax.axis_index("wt").astype(jnp.int32).reshape(1)
    x_rows = tokens[0]
    cot_rows = cotangent[0]
    rows, model = x_rows.shape
    total = n * rows
    wide = model // n
    units = w_ffn.shape[1] // n
    hidden_units = wt // 2 * units
    padded = (hidden_units + 127) // 128 * 128
    blocks = n // 2
    on_line = wt == PROJECTIONS and n == 8

    def my_columns(values, extent, axis):
        return lax.dynamic_slice_in_dim(values, mine * extent, extent, axis)

    def my_piece(values, axis):
        return lax.dynamic_index_in_dim(values, mine, axis, False)

    def pad_rows(values):
        return jnp.pad(values, ((0, padded - hidden_units), (0, 0)))

    if on_line:
        win_mine = pack_in(mine_ref, w_in, w_out, wide)
        win_first = lax.optimization_barrier(first_pieces(win_mine))
        win_more = more_pieces(win_first, 0, win_mine.shape[0])
        ffn_mine = pack_ffn(mine_ref, w_ffn, w_down, units)
    else:
        spread_in = lax.all_gather(w_in, "wt", axis=1, tiled=True)
        spread_in = my_piece(spread_in.reshape(model, PROJECTIONS, n, wide), 2)
        win_pieces = [jnp.transpose(spread_in, (1, 2, 0)).reshape(PROJECTIONS * wide, model)]
        win_pieces = [(win_pieces[0], 0, PROJECTIONS * wide)]
        wout_mine = lax.all_gather(my_columns(w_out, wide, 0), "wt", axis=1, tiled=True)
        down_mine = my_piece(w_down.reshape(wt // 2, n, units, -1), 1).reshape(hidden_units, -1)
        down_pieces = [(lax.all_gather(down_mine, "wt", axis=1, tiled=True), 0, hidden_units)]
        spread_ffn = lax.all_gather(my_columns(w_ffn, units, 1).T, "wt", axis=0)
        spread_ffn = [spread_ffn[: wt // 2].reshape(-1, model), spread_ffn[wt // 2 :].reshape(-1, model)]
        ffn_pieces = [(piece, 0, hidden_units) for piece in spread_ffn]

    inputs = (after(x_rows, win_mine) if on_line else x_rows).astype(f32)
    normed = (inputs * norm_factor(inputs) * gain_mix).astype(bf16)
    pair = jnp.concatenate([normed, cot_rows])
    order_mine = to_order(order[0].reshape(n, rows), mine).reshape(total)
    ends = jnp.cumsum(lengths[0])
    adapter = adapter_of(sequence_of(order_mine, lengths[0]), adapter_ids[0])
    mask = adapter_mask(adapter)
    mask_own = mask[:rows]
    gap_mine = my_columns(forget_gap, wide, 0)
    gain_mine = my_columns(gain_gate, wide, 0)
    in_b_mine = my_piece(in_b.reshape(PROJECTIONS, n, wide, RANKS), 1)
    in_b_wide = jnp.concatenate(
        [jnp.pad(in_b_mine[j], ((0, 0), (j * RANKS, (PROJECTIONS - 1 - j) * RANKS))) for j in range(PROJECTIONS)]
    )
    fold_in, fold_ffn, fold_out = fold_columns(PROJECTIONS, 0), fold_columns(3, PROJECTIONS), fold_columns(1, PROJECTIONS + 3)
    ffn_b_mine = my_piece(ffn_b.reshape(wt, n, units, RANKS), 1)
    b_gate = pad_rows(ffn_b_mine[: wt // 2].reshape(-1, RANKS))
    b_up = pad_rows(ffn_b_mine[wt // 2 :].reshape(-1, RANKS))
    both_b = jnp.concatenate([jnp.pad(b_gate, ((0, 0), (0, RANKS))), jnp.pad(b_up, ((0, 0), (RANKS, 0)))])
    down_a_mine = pad_rows(my_piece(down_a.reshape(wt // 2, n, units, RANKS), 1).reshape(-1, RANKS))
    pair_first = first_near(after(pair, in_b_wide, both_b))
    ready = lax.optimization_barrier(
        (
            pair_first, (order_mine.reshape(1, total), order_mine.reshape(total, 1)), mask, gap_mine, gain_mine,
            in_b_wide, both_b, down_a_mine, down_b.T, ffn_a.T, in_a.T,
        )
    )
    pair_first, order_both, mask, gap_mine, gain_mine, in_b_wide, both_b, down_a_mine, down_b_t, ffn_a_t, in_a_t = ready
    pair_near = [[pair]] + [[block] for block in pair_first]
    if n == 8:
        pair_near.append([across(pair_first[1][:rows], 2)])
    pair_other = [[across(after(pair, *pair_first), 1)]] + other_core(pair_near[1:])
    normed_near, cot_near = two_blocks(pair_near)
    normed_other, cot_other = two_blocks(pair_other)

    if on_line:
        win_more, ffn_mine = lax.optimization_barrier((win_more, ffn_mine))
        win_pieces = line_rows(win_mine, win_first, win_more, 0, wide)
        wout_mine = line_rows(win_mine, win_first, win_more, wide, win_mine.shape[0] - wide, wide)
        wout_mine = unpack_out(place_ref, wout_mine, wide)
    sent, hid_in, normed_mine, *kept = mixer_forward(
        ends, mine_ref, place_ref, order_both, normed_near + normed_other, win_pieces,
        after(in_a_t, wout_mine), in_b_wide, mask, gap_mine, gain_mine,
    )
    wout_first = [across(wout_mine, k) for k in range(2, n, 2)]
    if on_line:
        sent, wout_first, ffn_first = lax.optimization_barrier((sent, wout_first, first_pieces(ffn_mine)))
        early = units // 64 * 16
        early_more = more_pieces(ffn_first, 0, early)
        strip = ffn_mine.shape[0] - units
    else:
        sent, wout_first = lax.optimization_barrier((sent, wout_first))
    wout_near = [[wout_mine]] + [[block] for block in wout_first]
    wout_blocks = wout_near + other_core(wout_near)

    came = swap(sent)
    resid, normed2, hid_out = token_forward(
        mine_ref, came, x_rows, out_a, out_b, mask_own, gain_ffn, wout_blocks
    )

    if on_line:
        normed2, early_more = lax.optimization_barrier((normed2, early_more))
        late_more = more_pieces(after(ffn_first, *early_more), early, units - early)

    normed2_near = more_near(normed2, first_near(normed2))
    if on_line:
        normed2_near, late_more = lax.optimization_barrier((normed2_near, late_more))
        ffn_pieces = line_rows(ffn_mine, ffn_first, early_more, 0, early)
        ffn_pieces += line_rows(ffn_mine, ffn_first, late_more, early, units - early)
        down_more = more_pieces(after(ffn_first, *late_more), units, strip)
    both, hid_ffn, normed2_mine = ffn_up(
        mine_ref, place_ref, with_rows(normed2_near + other_core(normed2_near)), ffn_pieces, mask, ffn_a_t, both_b, wide
    )
    if on_line:
        cot_far = across(after(cot_rows, normed2), 6)
        both, down_more, cot_far = lax.optimization_barrier((both, down_more, cot_far))
        cot_near.append([(cot_far, 0, rows)])
        cot_other.append([(across(cot_far, 1), 0, rows)])
        down_pieces = line_rows(ffn_mine, ffn_first, down_more, units, strip)
    sides = []
    for cots, first in ((cot_other, blocks), (cot_near, 0)):
        sides.append(
            ffn_back(
                mine_ref, place_ref, cots, ffn_pieces, down_pieces, both, hid_ffn, mask, first,
                ffn_a_t, both_b, down_a_mine, down_b_t, fold_ffn, wide,
            )
        )
    back_far, down_far, small_far, *rest_far = sides[0]
    back, down, small, *rest = sides[1]
    back_far, down_far = across(back_far, 1), across(down_far, 1)
    back, down, back_far, down_far = lax.optimization_barrier((back, down, back_far, down_far))
    back_parts, back_rest = scatter_parts(back, back_far)
    from_x, from_y = scatter_second(scatter_first(back_parts), back_rest)
    d_sent, d_resid, d_hid_out, out_b_part = token_backward(
        mine_ref, came, cot_rows, resid, out_a, out_b, mask_own, gain_ffn, hid_out,
        (back, back_far, from_x, from_y), wout_blocks,
    )
    cot_mine = jnp.concatenate([rest[0], rest_far[0]])
    down_rows, both_rows = [rest[i] + rest_far[i] for i in (1, 2)]
    down_a_rows = down_rows[:, :hidden_units].T
    ffn_b_rows = jnp.concatenate(
        [both_rows[:RANKS, :hidden_units], both_rows[RANKS:, padded : padded + hidden_units]], axis=1
    ).T

    def packed_rows(arrays):
        return jnp.concatenate(
            [
                array[:, c * RANKS : (c + 1) * RANKS].reshape(wt, -1, RANKS)
                for array in arrays
                for c in range(array.shape[1] // RANKS)
            ],
            axis=1,
        )

    def unpacked_rows(summed, arrays):
        results, start = [], 0
        for array in arrays:
            height = array.shape[0] // wt
            parts = []
            for _ in range(array.shape[1] // RANKS):
                parts.append(summed[start : start + height])
                start += height
            results.append(jnp.concatenate(parts, axis=1))
        return results

    early = [ffn_b_rows, down_a_rows]
    early_sum = lax.psum_scatter(packed_rows(early), "wt", scatter_dimension=0, tiled=False)

    out_parts = [
        (down[i * rows : (i + 1) * rows].astype(f32) + down_far[i * rows : (i + 1) * rows].astype(f32)).astype(bf16)
        for i in range(1, blocks)
    ]
    out_parts = after(out_parts, d_sent)
    d_came = after(swap(d_sent), *out_parts)
    out_came = [across(part, 2 * i + 2) for i, part in enumerate(out_parts)]
    g_proj, gated_heads, small_in, in_b_rows, back_in_far = mixer_backward(
        ends, mine_ref, place_ref, order_both, d_came, kept, win_pieces, gap_mine, gain_mine, hid_in, in_b_wide,
        mask, fold_in,
    )
    g_proj, gated_heads, small_in, in_b_rows, back_in_far, out_came, early_sum = lax.optimization_barrier(
        (g_proj, gated_heads, small_in, in_b_rows, back_in_far, out_came, early_sum)
    )
    in_b_early = [in_b_rows.T]
    in_b_sum = lax.psum_scatter(packed_rows(in_b_early), "wt", scatter_dimension=0, tiled=False)
    ffn_b_grad, down_a_grad = unpacked_rows(early_sum, early)

    small = (small_in + jnp.concatenate([small, small_far])).reshape(n, rows, RANKS)
    small, g_proj = lax.optimization_barrier((from_order(small, mine), g_proj))
    small = swap(small)
    back_in_far = across(back_in_far, 1)
    back_in = spread(place_ref, g_proj, win_pieces, 0, blocks, rows)
    in_parts, in_rest = scatter_parts(back_in, back_in_far)
    in_came = scatter_first(in_parts)
    small = jnp.sum(after(small, *in_parts, *in_rest).astype(f32), axis=0)
    small = small.astype(bf16)
    d_hid_in_own = (mm(small, fold_in, NT) * adapter_mask(adapter[:rows], PROJECTIONS)).astype(bf16)
    small = small + mm(d_hid_out, fold_out).astype(bf16)
    small = jnp.broadcast_to(small, (n,) + small.shape)
    small = swap(jnp.concatenate([small, out_b_part.astype(bf16).reshape(n, rows, -1)], axis=2))
    block_out = resid + down[:rows].astype(f32) + down_far[:rows].astype(f32)
    block_out = (block_out + sum(piece.astype(f32) for piece in out_came)).astype(bf16)
    if in_rest:
        in_came[0], in_came[1], small = lax.optimization_barrier((in_came[0], in_came[1], small))
        in_rest = [in_rest[0] + in_came[1].astype(f32), in_rest[1] + in_came[0].astype(f32)]
        in_rest = [part.astype(bf16) for part in in_rest]
        from_x, from_y = [in_came[2], across(in_rest[0], 2)], [across(in_rest[1], 4), in_came[3]]
    else:
        from_x, from_y = scatter_second(in_came, in_rest)
    out_b_rows = jnp.sum(small[:, :, RANKS:].astype(f32), axis=0).reshape(wide, RANKS)
    small = to_order(small[:, :, :RANKS], mine).reshape(total, RANKS)
    d_hid_in = (mm(small, fold_in, NT) * adapter_mask(adapter, PROJECTIONS)).astype(bf16)

    wide_ffn = (mm(small, fold_ffn, NT) * adapter_mask(adapter, 3)).astype(bf16)
    late = [
        mm(cot_mine, wide_ffn[:, :RANKS], TN),
        mm(normed2_mine, wide_ffn[:, RANKS:], TN),
        mm(gated_heads, (mm(small, fold_out, NT) * mask).astype(bf16), TN),
        out_b_rows,
        mm(normed_mine, d_hid_in, TN),
    ]
    in_b_sum, small = lax.optimization_barrier((in_b_sum, small))
    (in_b_grad,) = unpacked_rows(in_b_sum, in_b_early)
    packed, from_x, from_y = lax.optimization_barrier((packed_rows(late).astype(bf16), from_x, from_y))
    late_sum = jnp.sum(swap(packed, "wt").astype(f32), axis=0)
    down_b_grad, ffn_a_grad, out_a_grad, out_b_grad, in_a_grad = unpacked_rows(late_sum, late)
    tokens_grad = token_end(
        x_rows, d_resid, d_hid_in_own, in_a, gain_mix, (back_in, back_in_far, from_x, from_y)
    )
    return (
        block_out[None],
        tokens_grad[None],
        in_a_grad,
        to_owner(in_b_grad, PROJECTIONS),
        out_a_grad,
        out_b_grad,
        ffn_a_grad,
        to_owner(ffn_b_grad, wt),
        to_owner(down_a_grad, wt // 2),
        down_b_grad,
    )


def solution(mesh):
    placed = (
        P("wt", "seq", None),
        P("wt", "seq", None),
        P(None, "wt"),
        P(None, "wt"),
        P(None, "wt"),
        P(None, "wt"),
        P(),
        P(),
        P(),
        P(),
        P(),
        P(),
        P(),
        P(),
        P(),
        P(),
        P(),
        P(),
        P("wt", None),
        P("wt", None),
        P("wt", None),
    )
    return jax.shard_map(
        local,
        mesh=mesh,
        in_specs=placed,
        out_specs=(
            P("wt", "seq", None),
            P("wt", "seq", None),
            P(("seq", "wt"), None),
            P(("seq", "wt"), None),
            P(("seq", "wt"), None),
            P(("seq", "wt"), None),
            P(("seq", "wt"), None),
            P(("seq", "wt"), None),
            P(("seq", "wt"), None),
            P(("seq", "wt"), None),
        ),
        check_vma=False,
    )
```

```python
import jax
import jax.numpy as jnp
from jax import lax
from jax.sharding import PartitionSpec as P
from jax.experimental import pallas as pl
from jax.experimental.pallas import tpu as pltpu

HEAD = 128
CHUNK = 128
TILE = 512
NN = (((1,), (0,)), ((), ()))
NT = (((1,), (1,)), ((), ()))
TN = (((0,), (0,)), ((), ()))


def mm(left, right, dims=NN):
    return lax.dot_general(left, right, dims, preferred_element_type=jnp.float32)


def halves(values):
    high = values.astype(jnp.bfloat16)
    return high, (values - high.astype(jnp.float32)).astype(jnp.bfloat16)


def mm3(left, right, dims=NN):
    return mm(left[0], right[0], dims) + (mm(left[0], right[1], dims) + mm(left[1], right[0], dims))


def mm2(left, right, dims=NN):
    return mm(left[0], right, dims) + mm(left[1], right, dims)


def mm2r(left, right, dims=NN):
    return mm(left, right[0], dims) + mm(left, right[1], dims)


def sum_with(ones, values):
    high, rest = halves(values)
    mid = (values - high.astype(jnp.float32) - rest.astype(jnp.float32)).astype(jnp.bfloat16)
    return mm(ones, high) + (mm(ones, rest) + mm(ones, mid))


def move_rows(picks, pairs):
    total = pairs[0][0].shape[0]

    @pl.loop(0, total // TILE)
    def _(tile):
        start = pl.multiple_of(tile * TILE, TILE)
        chosen = picks(start, total)
        for source, target in pairs:
            target[pl.ds(start, TILE), :] = mm(chosen, source[...]).astype(jnp.bfloat16)


def picks_natural(order_row_ref):
    def picks(start, total):
        places = lax.broadcasted_iota(jnp.int32, (TILE, total), 0) + start
        return jnp.where(order_row_ref[...] == places, 1.0, 0.0).astype(jnp.bfloat16)

    return picks


def picks_packed(order_column_ref):
    def picks(start, total):
        places = lax.broadcasted_iota(jnp.int32, (TILE, total), 1)
        return jnp.where(order_column_ref[pl.ds(start, TILE), :] == places, 1.0, 0.0).astype(jnp.bfloat16)

    return picks


def segment_terms(ends_ref, start):
    count = ends_ref.shape[0] - 1

    def seg_of(positions):
        return sum((positions >= ends_ref[j]).astype(jnp.int32) for j in range(count))

    rows = lax.broadcasted_iota(jnp.int32, (CHUNK, CHUNK), 0)
    cols = lax.broadcasted_iota(jnp.int32, (CHUNK, CHUNK), 1)
    same = seg_of(rows + start) == seg_of(cols + start)
    wide = seg_of(lax.broadcasted_iota(jnp.int32, (CHUNK, HEAD), 0) + start)
    before = jnp.where(start == 0, -1, seg_of(start - 1))
    last = seg_of(start + CHUNK - 1)
    carry_ok = (wide == before).astype(jnp.float32)
    tail_ok = (wide == last).astype(jnp.float32)
    keep = (last == before).astype(jnp.float32)
    return (rows >= cols) & same, (rows <= cols) & same, carry_ok, tail_ok, keep


def chunk_decays(forget, gap, lower):
    sigma = jax.nn.sigmoid(forget)
    keys = gap * (1.0 - sigma)
    cumulative = sum_with(lower, jnp.log1p(-keys))
    middle = cumulative[CHUNK // 2 - 1 : CHUNK // 2]
    total = cumulative[CHUNK - 1 : CHUNK]
    return sigma, keys, cumulative, middle, total


def lower_ones():
    rows = lax.broadcasted_iota(jnp.int32, (CHUNK, CHUNK), 0)
    cols = lax.broadcasted_iota(jnp.int32, (CHUNK, CHUNK), 1)
    return jnp.where(rows >= cols, 1.0, 0.0).astype(jnp.bfloat16)


VMEM = pl.BlockSpec(memory_space=pltpu.VMEM)
SMEM = pl.BlockSpec(memory_space=pltpu.SMEM)
ANY = pl.BlockSpec(memory_space=pl.ANY)


def params(mebibytes):
    return pltpu.CompilerParams(vmem_limit_bytes=mebibytes * 2**20)


def cost(tera_ops):
    return pl.CostEstimate(flops=int(tera_ops * 1e9), bytes_accessed=0, transcendentals=0)


def block_order(count):
    return list(range(0, count, 2)) + list(range(1, count, 2))


def tile_spec(rows, columns):
    return pl.BlockSpec((rows, columns), lambda i: (i, 0))


def row_to_column(row):
    size = row.shape[1]
    eye = lax.broadcasted_iota(jnp.int32, (size, size), 0) == lax.broadcasted_iota(jnp.int32, (size, size), 1)
    return jnp.sum(jnp.where(eye, row, 0.0), axis=1, keepdims=True)


def column_to_row(column):
    size = column.shape[0]
    eye = lax.broadcasted_iota(jnp.int32, (size, size), 0) == lax.broadcasted_iota(jnp.int32, (size, size), 1)
    return jnp.sum(jnp.where(eye, column, 0.0), axis=0, keepdims=True)


def packed_lines(rows_of, width):
    lines = []
    for row in rows_of:
        high, rest = halves(row)
        last = row - high.astype(jnp.float32) - rest.astype(jnp.float32)
        for part in (high.astype(jnp.float32), rest.astype(jnp.float32), last):
            lines += [part[:, i : i + width] for i in range(0, row.shape[1], width)]
    lines.append(jnp.zeros((16 - len(lines), width), jnp.float32))
    return jnp.concatenate(lines, axis=0).astype(jnp.bfloat16)


def unpacked_row(lines, which, each):
    first = 3 * each * which
    return [
        lines[first + i : first + i + 1]
        + lines[first + each + i : first + each + i + 1]
        + lines[first + 2 * each + i : first + 2 * each + i + 1]
        for i in range(each)
    ]


def window(ref, start, size):
    return ref.at[pl.ds(start, size)]


def windows(pieces, refs):
    return [window(ref, start, size) for ref, (_, start, size) in zip(refs, pieces)]


def arrays_of(pieces):
    return [array for array, _, _ in pieces]


def line_copies(refs, place, target, sem):
    if len(refs) == 1:
        return [(None, pltpu.make_async_copy(refs[0], target(None), sem))]
    own, up, down, a, b, c = refs
    held = ((own, down, b, c), (up, own, down, a), (a, up, own, down), (c, b, up, own))
    return [
        (place == p, pltpu.make_async_copy(ref, target(w), sem))
        for p, entries in enumerate(held)
        for w, ref in enumerate(entries)
    ]


def go(copies, what):
    for condition, copy in copies:
        if condition is None:
            getattr(copy, what)()
        else:
            pl.when(condition)(getattr(copy, what))


class Stream:
    def __init__(self, blocks):
        self.pieces = [piece for block in blocks for piece in block]
        self.arrays = arrays_of(self.pieces)
        self.blocks = [len(block) for block in blocks]
        self.rows = sum(size for _, _, size in blocks[0])

    def bind(self, refs, slots, sems):
        self.refs, self.slots, self.sems = windows(self.pieces, refs), slots, sems

    def copies(self, block, slot):
        first = sum(self.blocks[:block])
        result, start = [], 0
        for i in range(self.blocks[block]):
            size = self.pieces[first + i][2]
            result.append(
                pltpu.make_async_copy(
                    self.refs[first + i], self.slots.at[slot, pl.ds(start, size)], self.sems.at[slot, i]
                )
            )
            start += size
        return result

    def fetch(self, step):
        count = len(self.blocks)

        @pl.when(step == 0)
        def _():
            for copy in self.copies(0, 0):
                copy.start()

        for block in range(count):

            @pl.when(step == block)
            def _(block=block):
                if block + 1 < count:
                    for copy in self.copies(block + 1, (block + 1) % 2):
                        copy.start()
                for copy in self.copies(block, block % 2):
                    copy.wait()

        return self.slots[lax.rem(step, 2)]


def stream_scratch(rows, columns):
    return [pltpu.VMEM((2, rows, columns), jnp.bfloat16), pltpu.SemaphoreType.DMA((2, 2))]


def projection_copies(refs, place, target, sem):
    def at(w):
        rows = refs[0].shape[0] if w is None else refs[0].shape[0] * w
        return target.at[pl.ds(0, rows)] if w is None else target.at[pl.ds(rows, refs[0].shape[0])]

    return line_copies(refs, place, at, sem)


def forward_kernel(stream, win_pieces, *refs):
    ends_ref, mine_ref, place_ref, refs = refs[0], refs[1], refs[2], refs[3:]
    pieces, refs = refs[: len(stream.pieces)], refs[len(stream.pieces) :]
    win_refs, refs = refs[: len(win_pieces)], refs[len(win_pieces) :]
    (
        order_row_ref, order_column_ref, a_ref, b_ref, mask_ref, gap_ref, gain_ref,
        sent_ref, hid_out, normed_mine_out, zq_out, zg_out, mixed_ref, query_out, forget_out, value_out, states_ref,
        query_ref, forget_ref, value_ref, out_nat, state_now, win_ref, slots, sems, win_sem,
        hid_ref, normed_mine_ref, zq_ref, zg_ref, query_nat, forget_nat, value_nat, out_sems,
    ) = refs
    early = [(hid_ref, hid_out), (normed_mine_ref, normed_mine_out), (zq_ref, zq_out), (zg_ref, zg_out)]
    early += [(query_nat, query_out), (forget_nat, forget_out), (value_nat, value_out)]
    early = [pltpu.make_async_copy(here, there, out_sems.at[i]) for i, (here, there) in enumerate(early)]
    total, width = mixed_ref.shape
    heads = width // HEAD
    devices = sent_ref.shape[0]
    rows_each = total // devices
    stream.bind(pieces, slots, sems)
    win_copies = projection_copies(windows(win_pieces, win_refs), place_ref[0], win_ref, win_sem)
    go(win_copies, "start")
    win_ref[4 * width :, :] = a_ref[...]
    columns = pl.ds(pl.multiple_of(mine_ref[0] * width, 128), width)
    ranks = mask_ref.shape[1]
    go(win_copies, "wait")

    @pl.loop(0, devices)
    def _(step):
        block = stream.fetch(step)
        rows = pl.ds(pl.multiple_of(step * rows_each, rows_each), rows_each)
        normed_mine_ref[rows, :] = slots[lax.rem(step, 2), :, columns]
        main = mm(block, win_ref[...], NT)
        mask = mask_ref[rows, :].astype(jnp.float32)
        for j in range(4):
            lowered = main[:, 4 * width + j * ranks : 4 * width + (j + 1) * ranks] * mask
            hid_ref[rows, j * ranks : (j + 1) * ranks] = lowered.astype(jnp.bfloat16)
        main = main[:, : 4 * width] + mm(hid_ref[rows, :], b_ref[...], NT)
        zq = main[:, 0:width]
        zq_ref[rows, :] = zq
        query_ref[rows, :] = (zq * jax.nn.sigmoid(zq)).astype(jnp.bfloat16)
        forget_ref[rows, :] = main[:, width : 2 * width].astype(jnp.bfloat16)
        value_ref[rows, :] = main[:, 2 * width : 3 * width].astype(jnp.bfloat16)
        zg_ref[rows, :] = main[:, 3 * width : 4 * width]

    for copy in early[:4]:
        copy.start()
    move_rows(
        picks_natural(order_row_ref),
        ((query_ref, query_nat), (forget_ref, forget_nat), (value_ref, value_nat)),
    )
    for copy in early[4:]:
        copy.start()
    state_now[...] = jnp.zeros_like(state_now)
    lower = lower_ones()

    @pl.loop(0, total // CHUNK, unroll=2)
    def _(chunk):
        start = pl.multiple_of(chunk * CHUNK, CHUNK)
        rows = pl.ds(start, CHUNK)
        allowed, _, carry_ok, tail_ok, keep = segment_terms(ends_ref, start)
        for head in range(heads):
            lanes = slice(head * HEAD, (head + 1) * HEAD)
            query = query_nat[rows, lanes].astype(jnp.float32)
            value = value_nat[rows, lanes]
            _, keys, cumulative, middle, final = chunk_decays(
                forget_nat[rows, lanes].astype(jnp.float32), gap_ref[:, lanes], lower
            )
            grown = jnp.exp(cumulative - middle)
            shrunk = jnp.exp(middle - cumulative)
            scores = mm3(halves(query * grown), halves(keys * shrunk), NT)
            scores = jnp.where(allowed, scores, 0.0)
            state = state_now[head]
            states_ref[chunk, head] = state
            inter = mm3(halves(query * jnp.exp(cumulative) * carry_ok), halves(state), NT)
            out_nat[rows, lanes] = (mm2(halves(scores), value) + inter).astype(jnp.bfloat16)
            tail = keys * jnp.exp(final - cumulative) * tail_ok
            state_now[head] = state * (jnp.exp(final) * keep) + mm2r(value, halves(tail), TN)

    states_ref[total // CHUNK] = state_now[...]
    move_rows(picks_packed(order_column_ref), ((out_nat, mixed_ref),))

    for place, bits in enumerate(block_order(devices)):
        rows = slice(place * rows_each, (place + 1) * rows_each)
        target = mine_ref[0] ^ bits
        mixed = mixed_ref[rows, :].astype(jnp.float32)
        zg = zg_ref[rows, :]
        raw = mixed * gain_ref[...] * (zg * jax.nn.sigmoid(zg))
        sent_ref[target, 0:rows_each, :] = raw.astype(jnp.bfloat16)
        squares = halves(mixed * mixed)
        ones = jnp.ones((8, width), jnp.bfloat16)
        squares = (mm(ones, squares[0], NT) + mm(ones, squares[1], NT))[0:1]
        sent_ref[target, rows_each : rows_each + 16, :] = packed_lines([squares], width)
    for copy in early:
        copy.wait()


def mixer_forward(ends, mine, place, order, blocks, win_pieces, in_a_t, in_b_wide, mask, gap, gain):
    stream = Stream(blocks)
    devices = len(blocks)
    model = in_a_t.shape[1]
    total, width = stream.rows * devices, gap.shape[0]
    heads = width // HEAD
    ranks = mask.shape[1]
    rows = jax.ShapeDtypeStruct((total, width), jnp.bfloat16)
    wide_rows = jax.ShapeDtypeStruct((total, width), jnp.float32)
    states = jax.ShapeDtypeStruct((total // CHUNK + 1, heads, HEAD, HEAD), jnp.float32)
    sent = jax.ShapeDtypeStruct((devices, stream.rows + 16, width), jnp.bfloat16)
    hid = jax.ShapeDtypeStruct((total, 4 * ranks), jnp.bfloat16)
    return pl.pallas_call(
        lambda *refs: forward_kernel(stream, win_pieces, *refs),
        out_shape=(sent, hid, rows, wide_rows, wide_rows, rows, rows, rows, rows, states),
        in_specs=[SMEM] * 3 + [ANY] * (len(stream.pieces) + len(win_pieces)) + [VMEM] * 7,
        out_specs=(VMEM, ANY, ANY, ANY, ANY, VMEM, ANY, ANY, ANY, VMEM),
        scratch_shapes=[pltpu.VMEM((total, width), jnp.bfloat16)] * 4
        + [pltpu.VMEM((heads, HEAD, HEAD), jnp.float32), pltpu.VMEM((4 * (width + ranks), model), jnp.bfloat16)]
        + stream_scratch(stream.rows, model)
        + [pltpu.SemaphoreType.DMA(())]
        + [pltpu.VMEM(array.shape, array.dtype) for array in (hid, rows, wide_rows, wide_rows, rows, rows, rows)]
        + [pltpu.SemaphoreType.DMA((7,))],
        compiler_params=params(62),
        cost_estimate=cost(57),
    )(
        ends, mine, place, *stream.arrays, *arrays_of(win_pieces), *order,
        in_a_t, in_b_wide, mask, gap.reshape(1, width), gain.reshape(1, width),
    )


def backward_kernel(win_pieces, *refs):
    ends_ref, mine_ref, place_ref, refs = refs[0], refs[1], refs[2], refs[3:]
    win_refs, refs = windows(win_pieces, refs), refs[len(win_pieces) :]
    late, refs = refs[:7], refs[7:]
    (
        order_row_ref, order_column_ref, came_ref, zg_ref, mixed_ref, gap_ref, gain_ref, mask_ref, fold_ref,
        gated_ref, small_ref, b_rows_ref, spread_far, spread_near, g_proj_ref,
        grad_ref, grad_nat, d_query_nat, d_forget_nat, d_value_nat, slope_now,
        query_nat, forget_nat, value_nat, states_ref, zq_ref, hid_ref, b_ref, late_sems,
        win_ref, win_sem, spread_ref, spread_sems,
    ) = refs
    late = [
        pltpu.make_async_copy(there, here, late_sems.at[i])
        for i, (there, here) in enumerate(
            zip(late, (query_nat, forget_nat, value_nat, states_ref, zq_ref, hid_ref, b_ref))
        )
    ]
    for copy in late:
        copy.start()
    win_copies = projection_copies(win_refs, place_ref[0], win_ref, win_sem)
    go(win_copies, "start")
    total, width = mixed_ref.shape
    heads = width // HEAD
    devices = came_ref.shape[0]
    rows_each = total // devices

    for place, bits in enumerate(block_order(devices)):
        rows = slice(place * rows_each, (place + 1) * rows_each)
        source = mine_ref[0] ^ bits
        d_gated = came_ref[source, 0:rows_each, :].astype(jnp.float32)
        scalars = came_ref[source, rows_each : rows_each + 16, :].astype(jnp.float32)
        factor, mean = [
            jnp.concatenate([row_to_column(row) for row in unpacked_row(scalars, i, rows_each // width)])
            for i in range(2)
        ]
        mixed = mixed_ref[rows, :].astype(jnp.float32)
        zg = zg_ref[rows, :]
        sigma = jax.nn.sigmoid(zg)
        silu = zg * sigma
        gained = mixed * gain_ref[...]
        gated_ref[rows, :] = ((gained * silu).astype(jnp.bfloat16).astype(jnp.float32) * factor).astype(jnp.bfloat16)
        d_zg = d_gated * (gained * factor) * (sigma * (1.0 + zg * (1.0 - sigma)))
        g_proj_ref[rows, 3 * width : 4 * width] = d_zg.astype(jnp.bfloat16)
        scaled = d_gated * gain_ref[...] * silu
        cube = factor * factor * factor
        grad_ref[rows, :] = (factor * scaled - mixed * (cube * mean)).astype(jnp.bfloat16)

    move_rows(picks_natural(order_row_ref), ((grad_ref, grad_nat),))
    for copy in late[:4]:
        copy.wait()
    slope_now[...] = jnp.zeros_like(slope_now)
    lower = lower_ones()

    @pl.loop(0, total // CHUNK, unroll=2)
    def _(step):
        chunk = total // CHUNK - 1 - step
        start = pl.multiple_of(chunk * CHUNK, CHUNK)
        rows = pl.ds(start, CHUNK)
        allowed, later, carry_ok, tail_ok, keep = segment_terms(ends_ref, start)
        later = jnp.where(later, 1.0, 0.0).astype(jnp.bfloat16)
        for head in range(heads):
            lanes = slice(head * HEAD, (head + 1) * HEAD)
            query = query_nat[rows, lanes].astype(jnp.float32)
            value = value_nat[rows, lanes]
            grad = grad_nat[rows, lanes]
            sigma, keys, cumulative, middle, final = chunk_decays(
                forget_nat[rows, lanes].astype(jnp.float32), gap_ref[:, lanes], lower
            )
            grown = jnp.exp(cumulative - middle)
            shrunk = jnp.exp(middle - cumulative)
            query_grown = halves(query * grown)
            keys_shrunk = halves(keys * shrunk)
            scores = halves(jnp.where(allowed, mm3(query_grown, keys_shrunk, NT), 0.0))
            d_scores = halves(jnp.where(allowed, mm(grad, value, NT), 0.0))
            state = halves(states_ref[chunk, head])
            slope = slope_now[head]
            slope_parts = halves(slope)
            from_start = jnp.exp(cumulative) * carry_ok
            to_end = jnp.exp(final - cumulative) * tail_ok
            d_query = mm3(d_scores, keys_shrunk) * grown + mm2r(grad, state) * from_start
            d_keys = mm3(d_scores, query_grown, TN) * shrunk + mm2r(value, slope_parts) * to_end
            d_value = mm2(scores, grad, TN) + mm3(halves(keys * to_end), slope_parts, NT)
            past = jnp.sum(states_ref[chunk + 1, head] * slope, axis=0, keepdims=True)
            d_logf = sum_with(later, query * d_query - keys * d_keys) + tail_ok * past
            d_keys = d_keys - d_logf / (1.0 - keys)
            slope_now[head] = slope * (jnp.exp(final) * keep) + mm2r(grad, halves(query * from_start), TN)
            d_query_nat[rows, lanes] = d_query.astype(jnp.bfloat16)
            d_forget_nat[rows, lanes] = (-d_keys * keys * sigma).astype(jnp.bfloat16)
            d_value_nat[rows, lanes] = d_value.astype(jnp.bfloat16)

    picks = picks_packed(order_column_ref)
    for copy in late[4:]:
        copy.wait()

    @pl.loop(0, total // TILE)
    def _(tile):
        start = pl.multiple_of(tile * TILE, TILE)
        rows = pl.ds(start, TILE)
        chosen = picks(start, total)
        zq = zq_ref[rows, :]
        sigma = jax.nn.sigmoid(zq)
        d_query = mm(chosen, d_query_nat[...])
        g_proj_ref[rows, 0:width] = (d_query * (sigma * (1.0 + zq * (1.0 - sigma)))).astype(jnp.bfloat16)
        g_proj_ref[rows, width : 2 * width] = mm(chosen, d_forget_nat[...]).astype(jnp.bfloat16)
        g_proj_ref[rows, 2 * width : 3 * width] = mm(chosen, d_value_nat[...]).astype(jnp.bfloat16)
        mask = mask_ref[rows, :].astype(jnp.float32)
        through = mm(g_proj_ref[rows, :], b_ref[...])
        ranks = mask.shape[1]
        parts = [(through[:, j * ranks : (j + 1) * ranks] * mask).astype(jnp.bfloat16) for j in range(4)]
        small_ref[rows, :] = mm(jnp.concatenate(parts, axis=1), fold_ref[...]).astype(jnp.bfloat16)

    go(win_copies, "wait")
    half = devices // 2

    def spread_copy(out, block, slot):
        rows = pl.ds(pl.multiple_of(block * rows_each, rows_each), rows_each)
        return pltpu.make_async_copy(spread_ref.at[slot], out.at[rows], spread_sems.at[slot])

    for out, first in ((spread_far, half), (spread_near, 0)):

        @pl.loop(0, half)
        def _(block, out=out, first=first):
            slot = lax.rem(block, 2)

            @pl.when((block >= 2) | (first == 0))
            def _():
                spread_copy(out, 0, slot).wait()

            rows = pl.ds(pl.multiple_of((block + first) * rows_each, rows_each), rows_each)
            spread_ref[slot] = mm(g_proj_ref[rows, :], win_ref[...]).astype(jnp.bfloat16)
            spread_copy(out, block, slot).start()

    ranks = mask_ref.shape[1]
    for j in range(4):
        b_rows_ref[:, j * width : (j + 1) * width] = mm(
            hid_ref[:, j * ranks : (j + 1) * ranks], g_proj_ref[:, j * width : (j + 1) * width], TN
        )
    for block in range(half - 2, half):
        spread_copy(spread_near, block, block % 2).wait()


def mixer_backward(ends, mine, place, order, came, kept, win_pieces, gap, gain, hid_in, in_b_wide, mask, fold):
    zq, zg, mixed, query, forget, value, states = kept
    total, width = zq.shape
    ranks = mask.shape[1]
    heads = width // HEAD
    devices = came.shape[0]
    rows_each = total // devices
    model = win_pieces[0][0].shape[1]
    rows = jax.ShapeDtypeStruct((total, width), jnp.bfloat16)
    late = (query, forget, value, states, zq, hid_in, in_b_wide)
    return pl.pallas_call(
        lambda *refs: backward_kernel(win_pieces, *refs),
        out_shape=(
            rows,
            jax.ShapeDtypeStruct((total, ranks), jnp.bfloat16),
            jax.ShapeDtypeStruct((ranks, 4 * width), jnp.float32),
            jax.ShapeDtypeStruct((total // 2, model), jnp.bfloat16),
            jax.ShapeDtypeStruct((total // 2, model), jnp.bfloat16),
        ),
        in_specs=[SMEM] * 3 + [ANY] * (len(win_pieces) + len(late)) + [VMEM] * 9,
        out_specs=(VMEM,) * 3 + (ANY,) * 2,
        scratch_shapes=[pltpu.VMEM((total, 4 * width), jnp.bfloat16)]
        + [pltpu.VMEM((total, width), jnp.bfloat16)] * 5
        + [pltpu.VMEM((heads, HEAD, HEAD), jnp.float32)]
        + [pltpu.VMEM(array.shape, array.dtype) for array in late]
        + [pltpu.SemaphoreType.DMA((len(late),))]
        + [pltpu.VMEM((4 * width, model), jnp.bfloat16), pltpu.SemaphoreType.DMA(())]
        + [pltpu.VMEM((2, rows_each, model), jnp.bfloat16), pltpu.SemaphoreType.DMA((2,))],
        compiler_params=params(62),
        cost_estimate=cost(51),
    )(
        ends, mine, place, *arrays_of(win_pieces), *late, *order, came, zg, mixed,
        gap.reshape(1, width), gain.reshape(1, width), mask, fold,
    )


def spans(blocks):
    result = []
    for index, block in enumerate(blocks):
        start = 0
        for piece in block:
            result.append((index, start, piece.shape[0]))
            start += piece.shape[0]
    return result


def token_forward_kernel(where, count, *refs):
    mine_ref, came_ref, x_ref, a_ref, b_ref, mask_ref, gain_ref = refs[:7]
    weights, refs = refs[7 : 7 + count], refs[7 + count :]
    resid_ref, normed_ref, hid_ref, all_ref, gated_ref, a_mine, sems = refs
    devices = came_ref.shape[0]
    rows, model = x_ref.shape
    width = came_ref.shape[2]
    bits = block_order(devices)
    copies = [
        pltpu.make_async_copy(weights[i], all_ref.at[pl.ds(block * width + start, size)], sems.at[i])
        for i, (block, start, size) in enumerate(where)
    ]
    for copy in copies:
        copy.start()
    squares = jnp.zeros((1, rows), jnp.float32)
    for d in range(devices):
        lines = came_ref[d, rows : rows + 16, :].astype(jnp.float32)
        squares = squares + jnp.concatenate(unpacked_row(lines, 0, rows // width), axis=1)
    factor = lax.rsqrt(row_to_column(squares) / model + eps_norm)
    for place, bit in enumerate(bits):
        source = mine_ref[0] ^ bit
        lanes = slice(place * width, (place + 1) * width)
        raw = came_ref[source, 0:rows, :].astype(jnp.float32)
        gated_ref[:, lanes] = (raw * factor).astype(jnp.bfloat16)
        a_mine[lanes, :] = a_ref[pl.ds(pl.multiple_of(source * width, 128), width), :]
    gated = gated_ref[...]
    hid = (mm(gated, a_mine[...]) * mask_ref[...].astype(jnp.float32)).astype(jnp.bfloat16)
    hid_ref[...] = hid
    extra = mm(hid, b_ref[...], NT)
    for copy in copies:
        copy.wait()
    resid = x_ref[...].astype(jnp.float32) + mm(gated, all_ref[...]) + extra
    resid_ref[...] = resid
    factor = lax.rsqrt(jnp.mean(resid * resid, axis=-1, keepdims=True) + eps_norm)
    normed_ref[...] = (resid * factor * gain_ref[...]).astype(jnp.bfloat16)


def token_forward(mine, came, x, out_a, out_b, mask_own, gain, weights):
    rows, model = x.shape
    where = spans(weights)
    pieces = [piece for block in weights for piece in block]
    ranks = out_a.shape[1]
    return pl.pallas_call(
        lambda *refs: token_forward_kernel(where, len(pieces), *refs),
        out_shape=(
            jax.ShapeDtypeStruct((rows, model), jnp.float32),
            jax.ShapeDtypeStruct((rows, model), jnp.bfloat16),
            jax.ShapeDtypeStruct((rows, ranks), jnp.bfloat16),
        ),
        in_specs=[SMEM] + [VMEM] * 6 + [ANY] * len(pieces),
        out_specs=(VMEM,) * 3,
        scratch_shapes=[
            pltpu.VMEM((model, model), jnp.bfloat16),
            pltpu.VMEM((rows, model), jnp.bfloat16),
            pltpu.VMEM((model, ranks), jnp.bfloat16),
            pltpu.SemaphoreType.DMA((len(pieces),)),
        ],
        compiler_params=params(62),
        cost_estimate=cost(8),
    )(mine, came, x, out_a, out_b, mask_own, gain.reshape(1, model), *pieces)


def summed(refs):
    own, other, from_x, from_y = refs
    total = own[...].astype(jnp.float32) + other[...].astype(jnp.float32)
    for pieces in (from_x, from_y):
        if pieces:
            total = total + jnp.concatenate([piece[...] for piece in pieces]).astype(jnp.float32)
    return total


def first_block(rows, columns):
    return pl.BlockSpec((rows, columns), lambda i: (0, 0))


def whole(array):
    return pl.BlockSpec(array.shape, lambda i: (0,) * array.ndim)


def token_backward_kernel(where, count, near, nears, *refs):
    mine_ref, came_ref, cot_ref, resid_ref, a_ref, b_ref, mask_ref, gain_ref, hid_ref, own, other = refs[:11]
    refs = refs[11:]
    from_x, from_y, refs = refs[:near], refs[near:nears], refs[nears:]
    weights, refs = refs[:count], refs[count:]
    sent_ref, d_resid_ref, d_hid_ref, b_rows_ref, all_ref, sems = refs
    devices = came_ref.shape[0]
    rows, model = resid_ref.shape
    width = came_ref.shape[2]
    copies = [
        pltpu.make_async_copy(weights[i], all_ref.at[pl.ds(block * width + start, size)], sems.at[i])
        for i, (block, start, size) in enumerate(where)
    ]
    for copy in copies:
        copy.start()
    squares = jnp.zeros((1, rows), jnp.float32)
    for d in range(devices):
        lines = came_ref[d, rows : rows + 16, :].astype(jnp.float32)
        squares = squares + jnp.concatenate(unpacked_row(lines, 0, rows // width), axis=1)
    factor_two = lax.rsqrt(squares / model + eps_norm)

    resid = resid_ref[...]
    factor = lax.rsqrt(jnp.mean(resid * resid, axis=-1, keepdims=True) + eps_norm)
    scaled = summed((own, other, from_x, from_y)) * gain_ref[...]
    mean = jnp.mean(resid * scaled, axis=-1, keepdims=True)
    d_resid = cot_ref[...].astype(jnp.float32) + factor * scaled - resid * (factor * factor * factor * mean)
    d_resid_ref[...] = d_resid
    g_attn = d_resid.astype(jnp.bfloat16)
    d_hid = (mm(g_attn, b_ref[...]) * mask_ref[...].astype(jnp.float32)).astype(jnp.bfloat16)
    d_hid_ref[...] = d_hid
    b_rows_ref[...] = mm(g_attn, hid_ref[...], TN)
    for copy in copies:
        copy.wait()
    total = jnp.zeros((rows, 1), jnp.float32)
    for place, bit in enumerate(block_order(devices)):
        target = mine_ref[0] ^ bit
        block = slice(place * width, (place + 1) * width)
        a_block = a_ref[pl.ds(pl.multiple_of(target * width, 128), width), :]
        d_gated = mm(g_attn, all_ref[block, :], NT) + mm(d_hid, a_block, NT)
        raw = came_ref[target, 0:rows, :].astype(jnp.float32)
        total = total + jnp.sum(raw * d_gated, axis=-1, keepdims=True)
        sent_ref[target, 0:rows, :] = d_gated.astype(jnp.bfloat16)
    lines = packed_lines([factor_two, column_to_row(total / model)], width)
    for d in range(devices):
        sent_ref[d, rows : rows + 16, :] = lines


def token_backward(mine, came, cot, resid, out_a, out_b, mask_own, gain, hid, parts, weights):
    rows, model = resid.shape
    own, other, from_x, from_y = parts
    where = spans(weights)
    pieces = [piece for block in weights for piece in block]
    ranks = out_a.shape[1]
    fixed = [came, cot, resid, out_a, out_b, mask_own, gain.reshape(1, model), hid]
    return pl.pallas_call(
        lambda *refs: token_backward_kernel(where, len(pieces), len(from_x), len(from_x + from_y), *refs),
        grid=(1,),
        out_shape=(
            jax.ShapeDtypeStruct(came.shape, jnp.bfloat16),
            jax.ShapeDtypeStruct((rows, model), jnp.float32),
            jax.ShapeDtypeStruct((rows, ranks), jnp.bfloat16),
            jax.ShapeDtypeStruct((model, ranks), jnp.float32),
        ),
        in_specs=[SMEM] + [whole(array) for array in fixed] + [first_block(rows, model)] * 2
        + [whole(piece) for piece in from_x + from_y] + [ANY] * len(pieces),
        out_specs=(
            pl.BlockSpec(came.shape, lambda i: (0, 0, 0)),
            first_block(rows, model),
            first_block(rows, ranks),
            first_block(model, ranks),
        ),
        scratch_shapes=[
            pltpu.VMEM((model, model), jnp.bfloat16),
            pltpu.SemaphoreType.DMA((len(pieces),)),
        ],
        compiler_params=params(62),
        cost_estimate=cost(12),
    )(mine, *fixed, own, other, *from_x, *from_y, *pieces)


def token_end_kernel(near, nears, *refs):
    x_ref, d_resid_ref, d_hid_ref, a_ref, gain_ref, own, other = refs[:7]
    refs = refs[7:]
    from_x, from_y, out_ref = refs[:near], refs[near:nears], refs[nears]
    x = x_ref[...].astype(jnp.float32)
    factor = lax.rsqrt(jnp.mean(x * x, axis=-1, keepdims=True) + eps_norm)
    d_normed = summed((own, other, from_x, from_y)) + mm(d_hid_ref[...], a_ref[...], NT)
    scaled = d_normed * gain_ref[...]
    mean = jnp.mean(x * scaled, axis=-1, keepdims=True)
    out = d_resid_ref[...] + factor * scaled - x * (factor * factor * factor * mean)
    out_ref[...] = out.astype(jnp.bfloat16)


def token_end(x, d_resid, d_hid, in_a, gain, parts):
    rows, model = x.shape
    own, other, from_x, from_y = parts
    fixed = [x, d_resid]
    return pl.pallas_call(
        lambda *refs: token_end_kernel(len(from_x), len(from_x + from_y), *refs),
        grid=(1,),
        out_shape=jax.ShapeDtypeStruct((rows, model), jnp.bfloat16),
        in_specs=[whole(x), whole(d_resid), first_block(rows, d_hid.shape[1]), whole(in_a), first_block(1, model)]
        + [first_block(rows, model)] * 2 + [whole(piece) for piece in from_x + from_y],
        out_specs=first_block(rows, model),
        compiler_params=params(62),
        cost_estimate=cost(4),
    )(x, d_resid, d_hid, in_a, gain.reshape(1, model), own, other, *from_x, *from_y)


def both_copies(refs, place, target, padded, sem):
    if len(refs) == 2:
        size = refs[0].shape[0]
        return [(None, pltpu.make_async_copy(refs[i], window(target, i * padded, size), sem)) for i in range(2)]
    groups = [refs[i : i + 6] for i in range(0, len(refs), 6)]
    units = sum(group[0].shape[0] for group in groups)
    copies, first = [], 0
    for group in groups:
        size = group[0].shape[0]

        def at(w, first=first, size=size):
            return window(target, w // 2 * padded + w % 2 * units + first, size)

        copies += line_copies(group, place, at, sem)
        first += size
    return copies


def hidden_of(refs):
    if len(refs) == 2:
        return refs[0].shape[0]
    return 2 * sum(refs[i].shape[0] for i in range(0, len(refs), 6))


def load_both(refs, place, w_all, ffn_a_ref, padded, sem):
    copies = both_copies(refs, place, w_all, padded, sem)
    go(copies, "start")
    hidden_units = hidden_of(refs)
    if padded > hidden_units:
        blank = jnp.zeros((padded - hidden_units, w_all.shape[1]), jnp.bfloat16)
        w_all[hidden_units:padded, :] = blank
        w_all[padded + hidden_units : 2 * padded, :] = blank
    w_all[2 * padded :, :] = ffn_a_ref[...]
    return copies


def ffn_up_kernel(stream, ffn_pieces, *refs):
    mine_ref, place_ref, refs = refs[0], refs[1], refs[2:]
    pieces, refs = refs[: len(stream.pieces)], refs[len(stream.pieces) :]
    weights, refs = windows(ffn_pieces, refs), refs[len(ffn_pieces) :]
    mask_ref, ffn_a_ref, both_b_ref, both_ref, hid_ref, mine_out_ref, w_all, slots, sems, ffn_sem = refs
    step = pl.program_id(0)
    stream.bind(pieces, slots, sems)
    padded = both_b_ref.shape[0] // 2
    wide = mine_out_ref.shape[1]

    @pl.when(step == 0)
    def _():
        go(load_both(weights, place_ref[0], w_all, ffn_a_ref, padded, ffn_sem), "wait")

    normed = stream.fetch(step)
    columns = pl.ds(pl.multiple_of(mine_ref[0] * wide, 128), wide)
    mine_out_ref[...] = slots[lax.rem(step, 2), :, columns]
    mask = mask_ref[...].astype(jnp.float32)
    main = mm(normed, w_all[...], NT)
    hid = (main[:, 2 * padded :] * jnp.concatenate([mask, mask], axis=1)).astype(jnp.bfloat16)
    hid_ref[...] = hid
    both_ref[...] = main[:, : 2 * padded] + mm(hid, both_b_ref[...], NT)


def ffn_up(mine, place, normed, weights, mask, ffn_a_t, both_b, wide):
    stream = Stream(normed)
    rows, model = stream.rows, ffn_a_t.shape[1]
    total = rows * len(normed)
    ranks = mask.shape[1]
    padded = both_b.shape[0] // 2
    return pl.pallas_call(
        lambda *refs: ffn_up_kernel(stream, weights, *refs),
        grid=(len(normed),),
        out_shape=(
            jax.ShapeDtypeStruct((total, 2 * padded), jnp.float32),
            jax.ShapeDtypeStruct((total, 2 * ranks), jnp.bfloat16),
            jax.ShapeDtypeStruct((total, wide), jnp.bfloat16),
        ),
        in_specs=[SMEM] * 2
        + [ANY] * (len(stream.pieces) + len(weights))
        + [tile_spec(rows, ranks), whole(ffn_a_t), whole(both_b)],
        out_specs=(tile_spec(rows, 2 * padded), tile_spec(rows, 2 * ranks), tile_spec(rows, wide)),
        scratch_shapes=[pltpu.VMEM((2 * padded + 2 * ranks, model), jnp.bfloat16)]
        + stream_scratch(rows, model)
        + [pltpu.SemaphoreType.DMA(())],
        compiler_params=params(62),
        cost_estimate=cost(28),
    )(mine, place, *stream.arrays, *arrays_of(weights), mask, ffn_a_t, both_b)


def ffn_back_kernel(stream, ffn_pieces, down_pieces, *refs):
    mine_ref, place_ref, refs = refs[0], refs[1], refs[2:]
    pieces, refs = refs[: len(stream.pieces)], refs[len(stream.pieces) :]
    weights, refs = windows(ffn_pieces, refs), refs[len(ffn_pieces) :]
    downs, refs = windows(down_pieces, refs), refs[len(down_pieces) :]
    (
        both_ref, hid_ref, mask_ref, ffn_a_ref, both_b_ref, down_a_ref, down_b_ref, fold_ref,
        back_ref, down_ref, small_ref, cot_mine_ref, down_rows, both_rows,
        w_all, w_down, left_both, left_down, slots, sems, ffn_sem, down_sem,
    ) = refs
    step = pl.program_id(0)
    stream.bind(pieces, slots, sems)
    padded = down_a_ref.shape[0]
    model = w_down.shape[1]
    wide = cot_mine_ref.shape[1]

    @pl.when(step == 0)
    def _():
        hidden_units = hidden_of(weights)
        if len(downs) == 1:
            down = line_copies(downs, place_ref[0], lambda w: window(w_down, 0, hidden_units), down_sem)
        else:
            strip = downs[0].shape[0]
            narrow = model * strip // hidden_units
            down = []
            for part in range(hidden_units // strip):
                down += line_copies(
                    [ref.at[:, pl.ds(part * narrow, narrow)] for ref in downs],
                    place_ref[0],
                    lambda w, part=part: w_down.at[pl.ds(part * strip, strip), pl.ds(w * narrow, narrow)],
                    down_sem,
                )
        go(down, "start")
        if padded > hidden_units:
            w_down[hidden_units:padded, :] = jnp.zeros((padded - hidden_units, model), jnp.bfloat16)
        w_down[padded:, :] = down_b_ref[...]
        load_both(weights, place_ref[0], w_all, ffn_a_ref, padded, ffn_sem)
        go(down, "wait")
        down_rows[...] = jnp.zeros_like(down_rows)
        both_rows[...] = jnp.zeros_like(both_rows)

    cot = stream.fetch(step)
    columns = pl.ds(pl.multiple_of(mine_ref[0] * wide, 128), wide)
    cot_mine_ref[...] = slots[lax.rem(step, 2), :, columns]
    mask = mask_ref[...].astype(jnp.float32)
    hid = hid_ref[...]
    main = mm(cot, w_down[...], NT)
    d_hid = (main[:, padded:] * mask).astype(jnp.bfloat16)
    d_hidden = main[:, :padded] + mm(d_hid, down_a_ref[...], NT)
    gate, upper = both_ref[:, :padded], both_ref[:, padded:]
    sigma = jax.nn.sigmoid(gate)
    silu = gate * sigma
    left_down[:, :padded] = (silu * upper).astype(jnp.bfloat16)
    left_both[:, :padded] = (d_hidden * upper * (sigma * (1.0 + gate * (1.0 - sigma)))).astype(jnp.bfloat16)
    left_both[:, padded : 2 * padded] = (d_hidden * silu).astype(jnp.bfloat16)
    mask_two = jnp.concatenate([mask, mask], axis=1)

    @pl.when(step == 0)
    def _():
        go(both_copies(weights, place_ref[0], w_all, padded, ffn_sem), "wait")

    through = (mm(left_both[:, : 2 * padded], both_b_ref[...]) * mask_two).astype(jnp.bfloat16)
    left_both[:, 2 * padded :] = through
    back_ref[...] = mm(left_both[...], w_all[...]).astype(jnp.bfloat16)
    low = (mm(left_down[:, :padded], down_a_ref[...]) * mask).astype(jnp.bfloat16)
    left_down[:, padded:] = low
    down_ref[...] = mm(left_down[...], w_down[...]).astype(jnp.bfloat16)
    small_ref[...] = mm(jnp.concatenate([low, through], axis=1), fold_ref[...]).astype(jnp.bfloat16)
    down_rows[...] += mm(d_hid, left_down[:, :padded], TN)
    both_rows[...] += mm(hid, left_both[:, : 2 * padded], TN)


def ffn_back(mine, place, cot, weights, downs, both, hid, mask, first, ffn_a_t, both_b, down_a, down_b_t, fold, wide):
    stream = Stream(cot)
    rows, model = stream.rows, ffn_a_t.shape[1]
    blocks = len(cot)
    total = rows * blocks
    padded, ranks = down_a.shape
    fixed = [ffn_a_t, both_b, down_a, down_b_t, fold]
    grown = jax.ShapeDtypeStruct((total, model), jnp.bfloat16)

    def from_first(columns):
        return pl.BlockSpec((rows, columns), lambda i: (i + first, 0))

    return pl.pallas_call(
        lambda *refs: ffn_back_kernel(stream, weights, downs, *refs),
        grid=(blocks,),
        out_shape=(
            grown, grown, jax.ShapeDtypeStruct((total, ranks), jnp.bfloat16),
            jax.ShapeDtypeStruct((total, wide), jnp.bfloat16),
            jax.ShapeDtypeStruct((ranks, padded), jnp.float32),
            jax.ShapeDtypeStruct((2 * ranks, 2 * padded), jnp.float32),
        ),
        in_specs=[SMEM] * 2
        + [ANY] * (len(stream.pieces) + len(weights) + len(downs))
        + [from_first(2 * padded), from_first(2 * ranks), from_first(ranks)]
        + [whole(array) for array in fixed],
        out_specs=(
            tile_spec(rows, model), tile_spec(rows, model), tile_spec(rows, ranks), tile_spec(rows, wide),
            first_block(ranks, padded), first_block(2 * ranks, 2 * padded),
        ),
        scratch_shapes=[
            pltpu.VMEM((2 * padded + 2 * ranks, model), jnp.bfloat16),
            pltpu.VMEM((padded + ranks, model), jnp.bfloat16),
            pltpu.VMEM((rows, 2 * padded + 2 * ranks), jnp.bfloat16),
            pltpu.VMEM((rows, padded + ranks), jnp.bfloat16),
        ]
        + stream_scratch(rows, model)
        + [pltpu.SemaphoreType.DMA(()), pltpu.SemaphoreType.DMA(())],
        compiler_params=params(62),
        cost_estimate=cost(33),
    )(mine, place, *stream.arrays, *arrays_of(weights), *arrays_of(downs), both, hid, mask, *fixed)


def pack_in_kernel(mine_ref, win_ref, wout_ref, out_ref, window, sems):
    wide, model = window.shape[1], window.shape[0]
    narrow = wout_ref.shape[1]
    strips = model // narrow
    strip = wide // strips
    start = pl.multiple_of(mine_ref[0] * wide, 128)
    copies = [pltpu.make_async_copy(win_ref.at[:, pl.ds(start, wide)], window, sems.at[0])]
    for part in range(strips):
        copies.append(
            pltpu.make_async_copy(
                wout_ref.at[pl.ds(pl.multiple_of(start + part * strip, 16), strip)],
                out_ref.at[pl.ds(wide, strip), pl.ds(part * narrow, narrow)],
                sems.at[1 + part],
            )
        )
    for copy in copies:
        copy.start()
    eye = lax.broadcasted_iota(jnp.int32, (wide, wide), 0) == lax.broadcasted_iota(jnp.int32, (wide, wide), 1)
    eye = jnp.where(eye, 1.0, 0.0).astype(jnp.bfloat16)
    for copy in copies:
        copy.wait()
    out_ref[0:wide, :] = mm(eye, window[...], NT).astype(jnp.bfloat16)


def pack_in(mine, w_in, w_out, wide):
    model, narrow = w_in.shape[0], w_out.shape[1]
    strips = model // narrow
    return pl.pallas_call(
        pack_in_kernel,
        out_shape=jax.ShapeDtypeStruct((wide + wide // strips, model), jnp.bfloat16),
        in_specs=[SMEM, ANY, ANY],
        out_specs=VMEM,
        scratch_shapes=[pltpu.VMEM((model, wide), jnp.bfloat16), pltpu.SemaphoreType.DMA((1 + strips,))],
        compiler_params=params(62),
        cost_estimate=cost(3),
    )(mine, w_in, w_out)


def pack_ffn_kernel(units, mine_ref, wffn_ref, wdown_ref, out_ref, held, sems):
    model, columns = wffn_ref.shape
    span = held.shape[1]
    narrow = wdown_ref.shape[1]
    parts = model // narrow
    shards = wdown_ref.shape[0] // (units * 8)
    strip = units * shards // parts
    wanted = mine_ref[0] * units
    start = jnp.minimum(wanted // 128 * 128, columns - span)
    copies = [pltpu.make_async_copy(wffn_ref.at[:, pl.ds(pl.multiple_of(start, 128), span)], held, sems.at[0])]
    for part in range(parts):
        shard, inside = part * strip // units, part * strip % units
        source = shard * units * 8 + wanted + inside
        copies.append(
            pltpu.make_async_copy(
                wdown_ref.at[pl.ds(pl.multiple_of(source, 16), strip)],
                out_ref.at[pl.ds(units, strip), pl.ds(part * narrow, narrow)],
                sems.at[1 + part],
            )
        )
    for copy in copies:
        copy.start()
    rows = lax.broadcasted_iota(jnp.int32, (units, span), 0) + (wanted - start)
    chosen = jnp.where(rows == lax.broadcasted_iota(jnp.int32, (units, span), 1), 1.0, 0.0).astype(jnp.bfloat16)
    for copy in copies:
        copy.wait()
    out_ref[0:units, :] = mm(chosen, held[...], NT).astype(jnp.bfloat16)


def pack_ffn(mine, w_ffn, w_down, units):
    model, columns = w_ffn.shape
    span = min(columns, (units + 127) // 128 * 128 + 128)
    parts = model // w_down.shape[1]
    return pl.pallas_call(
        lambda *refs: pack_ffn_kernel(units, *refs),
        out_shape=jax.ShapeDtypeStruct((units + 2 * units // parts, model), jnp.bfloat16),
        in_specs=[SMEM, ANY, ANY],
        out_specs=VMEM,
        scratch_shapes=[pltpu.VMEM((model, span), jnp.bfloat16), pltpu.SemaphoreType.DMA((1 + parts,))],
        compiler_params=params(62),
        cost_estimate=cost(3),
    )(mine, w_ffn, w_down)


def unpack_out_kernel(pieces, *refs):
    place_ref, out, sem = refs[0], refs[-2], refs[-1]
    refs = windows(pieces, refs[1:-2])
    strip = refs[0].shape[0]
    strips = out.shape[0] // strip
    narrow = out.shape[1] // strips
    copies = []
    for part in range(strips):
        copies += line_copies(
            [ref.at[:, pl.ds(part * narrow, narrow)] for ref in refs],
            place_ref[0],
            lambda w, part=part: out.at[pl.ds(part * strip, strip), pl.ds(w * narrow, narrow)],
            sem,
        )
    go(copies, "start")
    go(copies, "wait")


def unpack_out(place, pieces, wide):
    model = pieces[0][0].shape[1]
    return pl.pallas_call(
        lambda *refs: unpack_out_kernel(pieces, *refs),
        out_shape=jax.ShapeDtypeStruct((wide, model), pieces[0][0].dtype),
        in_specs=[SMEM] + [ANY] * len(pieces),
        out_specs=VMEM,
        scratch_shapes=[pltpu.SemaphoreType.DMA(())],
        compiler_params=params(62),
        cost_estimate=cost(2),
    )(place, *arrays_of(pieces))


ADAPTERS = 8
RANK = 16
RANKS = ADAPTERS * RANK
PROJECTIONS = 4
eps_norm = 1e-06
f32 = jnp.float32
bf16 = jnp.bfloat16


def sequence_of(positions, seq_lengths):
    bounds = jnp.cumsum(seq_lengths)[:-1]
    return jnp.sum((positions[:, None] >= bounds[None, :]).astype(jnp.int32), axis=1)


def adapter_of(seq_numbers, seq_ids):
    numbers = jnp.arange(seq_ids.shape[0], dtype=jnp.int32)
    return jnp.sum(
        (seq_numbers[:, None] == numbers[None, :]).astype(jnp.int32) * seq_ids[None, :], axis=1
    )


def adapter_mask(adapter, count=1):
    columns = jnp.arange(count * RANKS, dtype=jnp.int32) % RANKS // RANK
    return (columns[None, :] == adapter[:, None]).astype(bf16)


def norm_factor(values):
    return lax.rsqrt(jnp.mean(values * values, axis=-1, keepdims=True) + eps_norm)


def norm_back(values, factor, gain, grad):
    scaled = grad * gain
    return factor * scaled - values * factor**3 * jnp.mean(values * scaled, axis=-1, keepdims=True)


def silu_slope(values, sigma):
    return sigma * (1.0 + values * (1.0 - sigma))


def relative(blocks, index):
    count, rest = blocks.shape[0], blocks.shape[1:]
    bit = 1
    while bit < count:
        pairs = blocks.reshape((count // (2 * bit), 2, bit) + rest)
        blocks = jnp.where((index & bit) != 0, pairs[:, ::-1], pairs).reshape((count,) + rest)
        bit *= 2
    return blocks


def to_order(blocks, index):
    count = blocks.shape[0]
    blocks = relative(blocks, index)
    pairs = blocks.reshape((count // 2, 2) + blocks.shape[1:])
    return jnp.concatenate([pairs[:, 0], pairs[:, 1]])


def from_order(blocks, index):
    count = blocks.shape[0]
    pairs = jnp.stack([blocks[: count // 2], blocks[count // 2 :]], axis=1)
    return relative(pairs.reshape(blocks.shape), index)


def across(values, bits, axis="seq"):
    size = lax.axis_size(axis)
    return lax.ppermute(values, axis, [(i, i ^ bits) for i in range(size)])


def first_near(block):
    size = lax.axis_size("seq")
    return [across(block, k) for k in ((2, 4) if size == 8 else range(2, size, 2))]


def more_near(block, first):
    if len(first) != 2:
        return [[block]] + [[other] for other in first]
    by_x, by_y = first
    half = block.shape[0] // 2
    return [[block], [by_x], [by_y], [across(by_x[:half], 4), across(by_y[half:], 2)]]


def other_core(blocks):
    return [[across(piece, 1) for piece in block] for block in blocks]


def with_rows(blocks):
    return [[(piece, 0, piece.shape[0]) for piece in block] for block in blocks]


def two_blocks(blocks):
    half = blocks[0][0].shape[0] // 2
    upper = [[(block[0], 0, half)] for block in blocks]
    return upper, [[(block[0], half, half)] for block in blocks if block[0].shape[0] == 2 * half]


def scatter_parts(near, other):
    size = lax.axis_size("seq")
    rows = near.shape[0] // (size // 2)
    half = rows // 2

    def part(block, start, stop):
        at = slice(block * rows + start, block * rows + stop)
        return near[at].astype(f32) + other[at].astype(f32)

    if size != 8:
        return [part(i, 0, rows).astype(bf16) for i in range(1, size // 2)], []
    sent = [part(3, 0, half), part(3, half, rows), part(1, 0, half), part(2, half, rows)]
    return [piece.astype(bf16) for piece in sent], [part(1, half, rows), part(2, 0, half)]


def scatter_first(sent):
    bits = (2, 4, 2, 4) if lax.axis_size("seq") == 8 else [2 * i + 2 for i in range(len(sent))]
    return [across(piece, bit) for piece, bit in zip(sent, bits)]


def scatter_second(came, rest):
    if not rest:
        total = sum(piece.astype(f32) for piece in came).astype(bf16)
        return [total], []
    far_x, far_y, by_x, by_y = came
    by_x_more = across((rest[0] + far_y.astype(f32)).astype(bf16), 2)
    by_y_more = across((rest[1] + far_x.astype(f32)).astype(bf16), 4)
    return [by_x, by_x_more], [by_y_more, by_y]


def swap(values, axis="seq"):
    return lax.all_to_all(values, axis, split_axis=0, concat_axis=0, tiled=False)


def along(values, pairs):
    return lax.ppermute(values, "wt", pairs)


def first_pieces(block):
    return along(block, [(0, 1), (1, 2), (2, 3)]), along(block, [(1, 0), (2, 1), (3, 2)])


def more_pieces(first, start, size):
    place = lax.axis_index("wt")
    up, down = [piece[start : start + size] for piece in first]
    inner, outer = jnp.where(place == 1, up, down), jnp.where(place == 2, up, down)
    return [along(inner, [(1, 2), (2, 1)]), along(outer, [(2, 3), (1, 0)]), along(inner, [(1, 3), (2, 0)])]


def line_rows(block, first, more, start, size, more_start=0):
    return [(piece, start, size) for piece in (block,) + tuple(first)] + [(piece, more_start, size) for piece in more]


def after(values, *others):
    return lax.optimization_barrier((values,) + others)[0]


def to_owner(piece, count):
    size, lines = lax.axis_size("seq"), lax.axis_size("wt")
    each = lines // count
    moves = []
    for s in range(size):
        for q in range(lines):
            whole = (q // each) * size * each + s * each + q % each
            moves.append((s * lines + q, whole))
    return lax.ppermute(piece, ("seq", "wt"), moves)


def fold_columns(count, first):
    source = jnp.arange(count * RANKS)
    target = jnp.arange(RANKS)
    wanted = (first + source // RANKS) * RANK + source % RANK
    return (wanted[:, None] == target[None, :]).astype(bf16)


def local(
    tokens,
    cotangent,
    w_in,
    w_out,
    w_ffn,
    w_down,
    gain_mix,
    gain_gate,
    gain_ffn,
    forget_gap,
    in_a,
    in_b,
    out_a,
    out_b,
    ffn_a,
    ffn_b,
    down_a,
    down_b,
    order,
    lengths,
    adapter_ids,
):
    n, wt = lax.axis_size("seq"), lax.axis_size("wt")
    mine = lax.axis_index("seq")
    mine_ref = mine.astype(jnp.int32).reshape(1)
    place_ref = lax.axis_index("wt").astype(jnp.int32).reshape(1)
    x_rows = tokens[0]
    cot_rows = cotangent[0]
    rows, model = x_rows.shape
    total = n * rows
    wide = model // n
    units = w_ffn.shape[1] // n
    hidden_units = wt // 2 * units
    padded = (hidden_units + 127) // 128 * 128
    blocks = n // 2
    on_line = wt == PROJECTIONS and n == 8

    def my_columns(values, extent, axis):
        return lax.dynamic_slice_in_dim(values, mine * extent, extent, axis)

    def my_piece(values, axis):
        return lax.dynamic_index_in_dim(values, mine, axis, False)

    def pad_rows(values):
        return jnp.pad(values, ((0, padded - hidden_units), (0, 0)))

    if on_line:
        win_mine = pack_in(mine_ref, w_in, w_out, wide)
        win_first = lax.optimization_barrier(first_pieces(win_mine))
        win_more = more_pieces(win_first, 0, win_mine.shape[0])
        ffn_mine = pack_ffn(mine_ref, w_ffn, w_down, units)
    else:
        spread_in = lax.all_gather(w_in, "wt", axis=1, tiled=True)
        spread_in = my_piece(spread_in.reshape(model, PROJECTIONS, n, wide), 2)
        win_pieces = [jnp.transpose(spread_in, (1, 2, 0)).reshape(PROJECTIONS * wide, model)]
        win_pieces = [(win_pieces[0], 0, PROJECTIONS * wide)]
        wout_mine = lax.all_gather(my_columns(w_out, wide, 0), "wt", axis=1, tiled=True)
        down_mine = my_piece(w_down.reshape(wt // 2, n, units, -1), 1).reshape(hidden_units, -1)
        down_pieces = [(lax.all_gather(down_mine, "wt", axis=1, tiled=True), 0, hidden_units)]
        spread_ffn = lax.all_gather(my_columns(w_ffn, units, 1).T, "wt", axis=0)
        spread_ffn = [spread_ffn[: wt // 2].reshape(-1, model), spread_ffn[wt // 2 :].reshape(-1, model)]
        ffn_pieces = [(piece, 0, hidden_units) for piece in spread_ffn]

    inputs = (after(x_rows, win_mine) if on_line else x_rows).astype(f32)
    normed = (inputs * norm_factor(inputs) * gain_mix).astype(bf16)
    pair = jnp.concatenate([normed, cot_rows])
    order_mine = to_order(order[0].reshape(n, rows), mine).reshape(total)
    ends = jnp.cumsum(lengths[0])
    adapter = adapter_of(sequence_of(order_mine, lengths[0]), adapter_ids[0])
    mask = adapter_mask(adapter)
    mask_own = mask[:rows]
    gap_mine = my_columns(forget_gap, wide, 0)
    gain_mine = my_columns(gain_gate, wide, 0)
    in_b_mine = my_piece(in_b.reshape(PROJECTIONS, n, wide, RANKS), 1)
    in_b_wide = jnp.concatenate(
        [jnp.pad(in_b_mine[j], ((0, 0), (j * RANKS, (PROJECTIONS - 1 - j) * RANKS))) for j in range(PROJECTIONS)]
    )
    fold_in, fold_ffn, fold_out = fold_columns(PROJECTIONS, 0), fold_columns(3, PROJECTIONS), fold_columns(1, PROJECTIONS + 3)
    ffn_b_mine = my_piece(ffn_b.reshape(wt, n, units, RANKS), 1)
    b_gate = pad_rows(ffn_b_mine[: wt // 2].reshape(-1, RANKS))
    b_up = pad_rows(ffn_b_mine[wt // 2 :].reshape(-1, RANKS))
    both_b = jnp.concatenate([jnp.pad(b_gate, ((0, 0), (0, RANKS))), jnp.pad(b_up, ((0, 0), (RANKS, 0)))])
    down_a_mine = pad_rows(my_piece(down_a.reshape(wt // 2, n, units, RANKS), 1).reshape(-1, RANKS))
    pair_first = first_near(after(pair, in_b_wide, both_b))
    ready = lax.optimization_barrier(
        (
            pair_first, (order_mine.reshape(1, total), order_mine.reshape(total, 1)), mask, gap_mine, gain_mine,
            in_b_wide, both_b, down_a_mine, down_b.T, ffn_a.T, in_a.T,
        )
    )
    pair_first, order_both, mask, gap_mine, gain_mine, in_b_wide, both_b, down_a_mine, down_b_t, ffn_a_t, in_a_t = ready
    pair_near = [[pair]] + [[block] for block in pair_first]
    if n == 8:
        pair_near.append([across(pair_first[1][:rows], 2)])
    pair_other = [[across(after(pair, *pair_first), 1)]] + other_core(pair_near[1:])
    normed_near, cot_near = two_blocks(pair_near)
    normed_other, cot_other = two_blocks(pair_other)

    if on_line:
        win_more, ffn_mine = lax.optimization_barrier((win_more, ffn_mine))
        win_pieces = line_rows(win_mine, win_first, win_more, 0, wide)
        wout_mine = line_rows(win_mine, win_first, win_more, wide, win_mine.shape[0] - wide, wide)
        wout_mine = unpack_out(place_ref, wout_mine, wide)
    sent, hid_in, normed_mine, *kept = mixer_forward(
        ends, mine_ref, place_ref, order_both, normed_near + normed_other, win_pieces,
        after(in_a_t, wout_mine), in_b_wide, mask, gap_mine, gain_mine,
    )
    wout_first = [across(wout_mine, k) for k in range(2, n, 2)]
    if on_line:
        sent, wout_first, ffn_first = lax.optimization_barrier((sent, wout_first, first_pieces(ffn_mine)))
        early = units // 64 * 16
        early_more = more_pieces(ffn_first, 0, early)
        strip = ffn_mine.shape[0] - units
    else:
        sent, wout_first = lax.optimization_barrier((sent, wout_first))
    wout_near = [[wout_mine]] + [[block] for block in wout_first]
    wout_blocks = wout_near + other_core(wout_near)

    came = swap(sent)
    resid, normed2, hid_out = token_forward(
        mine_ref, came, x_rows, out_a, out_b, mask_own, gain_ffn, wout_blocks
    )

    if on_line:
        normed2, early_more = lax.optimization_barrier((normed2, early_more))
        late_more = more_pieces(after(ffn_first, *early_more), early, units - early)

    normed2_near = more_near(normed2, first_near(normed2))
    if on_line:
        normed2_near, late_more = lax.optimization_barrier((normed2_near, late_more))
        ffn_pieces = line_rows(ffn_mine, ffn_first, early_more, 0, early)
        ffn_pieces += line_rows(ffn_mine, ffn_first, late_more, early, units - early)
        down_more = more_pieces(after(ffn_first, *late_more), units, strip)
    both, hid_ffn, normed2_mine = ffn_up(
        mine_ref, place_ref, with_rows(normed2_near + other_core(normed2_near)), ffn_pieces, mask, ffn_a_t, both_b, wide
    )
    if on_line:
        cot_far = across(after(cot_rows, normed2), 6)
        both, down_more, cot_far = lax.optimization_barrier((both, down_more, cot_far))
        cot_near.append([(cot_far, 0, rows)])
        cot_other.append([(across(cot_far, 1), 0, rows)])
        down_pieces = line_rows(ffn_mine, ffn_first, down_more, units, strip)
    sides = []
    for cots, first in ((cot_other, blocks), (cot_near, 0)):
        sides.append(
            ffn_back(
                mine_ref, place_ref, cots, ffn_pieces, down_pieces, both, hid_ffn, mask, first,
                ffn_a_t, both_b, down_a_mine, down_b_t, fold_ffn, wide,
            )
        )
    back_far, down_far, small_far, *rest_far = sides[0]
    back, down, small, *rest = sides[1]
    back_far, down_far = across(back_far, 1), across(down_far, 1)
    back, down, back_far, down_far = lax.optimization_barrier((back, down, back_far, down_far))
    back_parts, back_rest = scatter_parts(back, back_far)
    from_x, from_y = scatter_second(scatter_first(back_parts), back_rest)
    d_sent, d_resid, d_hid_out, out_b_part = token_backward(
        mine_ref, came, cot_rows, resid, out_a, out_b, mask_own, gain_ffn, hid_out,
        (back, back_far, from_x, from_y), wout_blocks,
    )
    cot_mine = jnp.concatenate([rest[0], rest_far[0]])
    down_rows, both_rows = [rest[i] + rest_far[i] for i in (1, 2)]
    down_a_rows = down_rows[:, :hidden_units].T
    ffn_b_rows = jnp.concatenate(
        [both_rows[:RANKS, :hidden_units], both_rows[RANKS:, padded : padded + hidden_units]], axis=1
    ).T

    def packed_rows(arrays):
        return jnp.concatenate(
            [
                array[:, c * RANKS : (c + 1) * RANKS].reshape(wt, -1, RANKS)
                for array in arrays
                for c in range(array.shape[1] // RANKS)
            ],
            axis=1,
        )

    def unpacked_rows(summed, arrays):
        results, start = [], 0
        for array in arrays:
            height = array.shape[0] // wt
            parts = []
            for _ in range(array.shape[1] // RANKS):
                parts.append(summed[start : start + height])
                start += height
            results.append(jnp.concatenate(parts, axis=1))
        return results

    early = [ffn_b_rows, down_a_rows]
    early_sum = lax.psum_scatter(packed_rows(early), "wt", scatter_dimension=0, tiled=False)

    out_parts = [
        (down[i * rows : (i + 1) * rows].astype(f32) + down_far[i * rows : (i + 1) * rows].astype(f32)).astype(bf16)
        for i in range(1, blocks)
    ]
    out_parts = after(out_parts, d_sent)
    d_came = after(swap(d_sent), *out_parts)
    out_came = [across(part, 2 * i + 2) for i, part in enumerate(out_parts)]
    gated_heads, small_in, in_b_rows, back_in_far, back_in = mixer_backward(
        ends, mine_ref, place_ref, order_both, d_came, kept, win_pieces, gap_mine, gain_mine, hid_in, in_b_wide,
        mask, fold_in,
    )
    gated_heads, small_in, in_b_rows, back_in_far, back_in, out_came, early_sum = lax.optimization_barrier(
        (gated_heads, small_in, in_b_rows, back_in_far, back_in, out_came, early_sum)
    )
    in_b_early = [in_b_rows.T]
    in_b_sum = lax.psum_scatter(packed_rows(in_b_early), "wt", scatter_dimension=0, tiled=False)
    ffn_b_grad, down_a_grad = unpacked_rows(early_sum, early)

    small = (small_in + jnp.concatenate([small, small_far])).reshape(n, rows, RANKS)
    back_in_far = across(back_in_far, 1)
    small = swap(from_order(small, mine))
    in_parts, in_rest = scatter_parts(back_in, back_in_far)
    in_came = scatter_first(in_parts)
    block_out = resid + down[:rows].astype(f32) + down_far[:rows].astype(f32)
    block_out = (block_out + sum(piece.astype(f32) for piece in out_came)).astype(bf16)
    if in_rest:
        in_came[0], in_came[1], block_out = lax.optimization_barrier((in_came[0], in_came[1], block_out))
        in_rest = [in_rest[0] + in_came[1].astype(f32), in_rest[1] + in_came[0].astype(f32)]
        in_rest = [part.astype(bf16) for part in in_rest]
        from_x, from_y = [in_came[2], across(in_rest[0], 2)], [across(in_rest[1], 4), in_came[3]]
    else:
        from_x, from_y = scatter_second(in_came, in_rest)
    small = jnp.sum(after(small, *in_parts, *in_rest).astype(f32), axis=0)
    small = small.astype(bf16)
    d_hid_in_own = (mm(small, fold_in, NT) * adapter_mask(adapter[:rows], PROJECTIONS)).astype(bf16)
    small = small + mm(d_hid_out, fold_out).astype(bf16)
    small = jnp.broadcast_to(small, (n,) + small.shape)
    small = swap(jnp.concatenate([small, out_b_part.astype(bf16).reshape(n, rows, -1)], axis=2))
    if in_rest:
        small, from_x[0], from_y[1] = lax.optimization_barrier((small, from_x[0], from_y[1]))
    out_b_rows = jnp.sum(small[:, :, RANKS:].astype(f32), axis=0).reshape(wide, RANKS)
    small = to_order(small[:, :, :RANKS], mine).reshape(total, RANKS)
    d_hid_in = (mm(small, fold_in, NT) * adapter_mask(adapter, PROJECTIONS)).astype(bf16)

    wide_ffn = (mm(small, fold_ffn, NT) * adapter_mask(adapter, 3)).astype(bf16)
    late = [
        mm(cot_mine, wide_ffn[:, :RANKS], TN),
        mm(normed2_mine, wide_ffn[:, RANKS:], TN),
        mm(gated_heads, (mm(small, fold_out, NT) * mask).astype(bf16), TN),
        out_b_rows,
        mm(normed_mine, d_hid_in, TN),
    ]
    in_b_sum, small = lax.optimization_barrier((in_b_sum, small))
    (in_b_grad,) = unpacked_rows(in_b_sum, in_b_early)
    packed, from_x, from_y = lax.optimization_barrier((packed_rows(late).astype(bf16), from_x, from_y))
    late_sum = jnp.sum(swap(packed, "wt").astype(f32), axis=0)
    down_b_grad, ffn_a_grad, out_a_grad, out_b_grad, in_a_grad = unpacked_rows(late_sum, late)
    tokens_grad = token_end(
        x_rows, d_resid, d_hid_in_own, in_a, gain_mix, (back_in, back_in_far, from_x, from_y)
    )
    return (
        block_out[None],
        tokens_grad[None],
        in_a_grad,
        to_owner(in_b_grad, PROJECTIONS),
        out_a_grad,
        out_b_grad,
        ffn_a_grad,
        to_owner(ffn_b_grad, wt),
        to_owner(down_a_grad, wt // 2),
        down_b_grad,
    )


def solution(mesh):
    placed = (
        P("wt", "seq", None),
        P("wt", "seq", None),
        P(None, "wt"),
        P(None, "wt"),
        P(None, "wt"),
        P(None, "wt"),
        P(),
        P(),
        P(),
        P(),
        P(),
        P(),
        P(),
        P(),
        P(),
        P(),
        P(),
        P(),
        P("wt", None),
        P("wt", None),
        P("wt", None),
    )
    return jax.shard_map(
        local,
        mesh=mesh,
        in_specs=placed,
        out_specs=(
            P("wt", "seq", None),
            P("wt", "seq", None),
            P(("seq", "wt"), None),
            P(("seq", "wt"), None),
            P(("seq", "wt"), None),
            P(("seq", "wt"), None),
            P(("seq", "wt"), None),
            P(("seq", "wt"), None),
            P(("seq", "wt"), None),
            P(("seq", "wt"), None),
        ),
        check_vma=False,
    )
```

```python
import jax
import jax.numpy as jnp
from jax import lax
from jax.sharding import PartitionSpec as P
from jax.experimental import pallas as pl
from jax.experimental.pallas import tpu as pltpu

HEAD = 128
CHUNK = 128
TILE = 512
NN = (((1,), (0,)), ((), ()))
NT = (((1,), (1,)), ((), ()))
TN = (((0,), (0,)), ((), ()))


def mm(left, right, dims=NN):
    return lax.dot_general(left, right, dims, preferred_element_type=jnp.float32)


def halves(values):
    high = values.astype(jnp.bfloat16)
    return high, (values - high.astype(jnp.float32)).astype(jnp.bfloat16)


def mm3(left, right, dims=NN):
    return mm(left[0], right[0], dims) + (mm(left[0], right[1], dims) + mm(left[1], right[0], dims))


def mm2(left, right, dims=NN):
    return mm(left[0], right, dims) + mm(left[1], right, dims)


def mm2r(left, right, dims=NN):
    return mm(left, right[0], dims) + mm(left, right[1], dims)


def sum_with(ones, values):
    high, rest = halves(values)
    mid = (values - high.astype(jnp.float32) - rest.astype(jnp.float32)).astype(jnp.bfloat16)
    return mm(ones, high) + (mm(ones, rest) + mm(ones, mid))


def move_rows(picks, pairs):
    total = pairs[0][0].shape[0]

    @pl.loop(0, total // TILE)
    def _(tile):
        start = pl.multiple_of(tile * TILE, TILE)
        chosen = picks(start, total)
        for source, target in pairs:
            target[pl.ds(start, TILE), :] = mm(chosen, source[...]).astype(jnp.bfloat16)


def picks_natural(order_row_ref):
    def picks(start, total):
        places = lax.broadcasted_iota(jnp.int32, (TILE, total), 0) + start
        return jnp.where(order_row_ref[...] == places, 1.0, 0.0).astype(jnp.bfloat16)

    return picks


def picks_packed(order_column_ref):
    def picks(start, total):
        places = lax.broadcasted_iota(jnp.int32, (TILE, total), 1)
        return jnp.where(order_column_ref[pl.ds(start, TILE), :] == places, 1.0, 0.0).astype(jnp.bfloat16)

    return picks


def segment_terms(ends_ref, start):
    count = ends_ref.shape[0] - 1

    def seg_of(positions):
        return sum((positions >= ends_ref[j]).astype(jnp.int32) for j in range(count))

    rows = lax.broadcasted_iota(jnp.int32, (CHUNK, CHUNK), 0)
    cols = lax.broadcasted_iota(jnp.int32, (CHUNK, CHUNK), 1)
    same = seg_of(rows + start) == seg_of(cols + start)
    wide = seg_of(lax.broadcasted_iota(jnp.int32, (CHUNK, HEAD), 0) + start)
    before = jnp.where(start == 0, -1, seg_of(start - 1))
    last = seg_of(start + CHUNK - 1)
    carry_ok = (wide == before).astype(jnp.float32)
    tail_ok = (wide == last).astype(jnp.float32)
    keep = (last == before).astype(jnp.float32)
    return (rows >= cols) & same, (rows <= cols) & same, carry_ok, tail_ok, keep


def chunk_decays(forget, gap, lower):
    sigma = jax.nn.sigmoid(forget)
    keys = gap * (1.0 - sigma)
    cumulative = sum_with(lower, jnp.log1p(-keys))
    middle = cumulative[CHUNK // 2 - 1 : CHUNK // 2]
    total = cumulative[CHUNK - 1 : CHUNK]
    return sigma, keys, cumulative, middle, total


def lower_ones():
    rows = lax.broadcasted_iota(jnp.int32, (CHUNK, CHUNK), 0)
    cols = lax.broadcasted_iota(jnp.int32, (CHUNK, CHUNK), 1)
    return jnp.where(rows >= cols, 1.0, 0.0).astype(jnp.bfloat16)


VMEM = pl.BlockSpec(memory_space=pltpu.VMEM)
SMEM = pl.BlockSpec(memory_space=pltpu.SMEM)
ANY = pl.BlockSpec(memory_space=pl.ANY)


def params(mebibytes):
    return pltpu.CompilerParams(vmem_limit_bytes=mebibytes * 2**20)


def cost(tera_ops):
    return pl.CostEstimate(flops=int(tera_ops * 1e9), bytes_accessed=0, transcendentals=0)


def block_order(count):
    return list(range(0, count, 2)) + list(range(1, count, 2))


def tile_spec(rows, columns):
    return pl.BlockSpec((rows, columns), lambda i: (i, 0))


def row_to_column(row):
    size = row.shape[1]
    eye = lax.broadcasted_iota(jnp.int32, (size, size), 0) == lax.broadcasted_iota(jnp.int32, (size, size), 1)
    return jnp.sum(jnp.where(eye, row, 0.0), axis=1, keepdims=True)


def column_to_row(column):
    size = column.shape[0]
    eye = lax.broadcasted_iota(jnp.int32, (size, size), 0) == lax.broadcasted_iota(jnp.int32, (size, size), 1)
    return jnp.sum(jnp.where(eye, column, 0.0), axis=0, keepdims=True)


def packed_lines(rows_of, width):
    lines = []
    for row in rows_of:
        high, rest = halves(row)
        last = row - high.astype(jnp.float32) - rest.astype(jnp.float32)
        for part in (high.astype(jnp.float32), rest.astype(jnp.float32), last):
            lines += [part[:, i : i + width] for i in range(0, row.shape[1], width)]
    lines.append(jnp.zeros((16 - len(lines), width), jnp.float32))
    return jnp.concatenate(lines, axis=0).astype(jnp.bfloat16)


def unpacked_row(lines, which, each):
    first = 3 * each * which
    return [
        lines[first + i : first + i + 1]
        + lines[first + each + i : first + each + i + 1]
        + lines[first + 2 * each + i : first + 2 * each + i + 1]
        for i in range(each)
    ]


def window(ref, start, size):
    return ref.at[pl.ds(start, size)]


def windows(pieces, refs):
    return [window(ref, start, size) for ref, (_, start, size) in zip(refs, pieces)]


def arrays_of(pieces):
    return [array for array, _, _ in pieces]


def line_copies(refs, place, target, sem):
    if len(refs) == 1:
        return [(None, pltpu.make_async_copy(refs[0], target(None), sem))]
    own, up, down, a, b, c = refs
    held = ((own, down, b, c), (up, own, down, a), (a, up, own, down), (c, b, up, own))
    return [
        (place == p, pltpu.make_async_copy(ref, target(w), sem))
        for p, entries in enumerate(held)
        for w, ref in enumerate(entries)
    ]


def go(copies, what):
    for condition, copy in copies:
        if condition is None:
            getattr(copy, what)()
        else:
            pl.when(condition)(getattr(copy, what))


class Stream:
    def __init__(self, blocks):
        self.pieces = [piece for block in blocks for piece in block]
        self.arrays = arrays_of(self.pieces)
        self.blocks = [len(block) for block in blocks]
        self.rows = sum(size for _, _, size in blocks[0])

    def bind(self, refs, slots, sems):
        self.refs, self.slots, self.sems = windows(self.pieces, refs), slots, sems

    def copies(self, block, slot):
        first = sum(self.blocks[:block])
        result, start = [], 0
        for i in range(self.blocks[block]):
            size = self.pieces[first + i][2]
            result.append(
                pltpu.make_async_copy(
                    self.refs[first + i], self.slots.at[slot, pl.ds(start, size)], self.sems.at[slot, i]
                )
            )
            start += size
        return result

    def fetch(self, step):
        count = len(self.blocks)

        @pl.when(step == 0)
        def _():
            for copy in self.copies(0, 0):
                copy.start()

        for block in range(count):

            @pl.when(step == block)
            def _(block=block):
                if block + 1 < count:
                    for copy in self.copies(block + 1, (block + 1) % 2):
                        copy.start()
                for copy in self.copies(block, block % 2):
                    copy.wait()

        return self.slots[lax.rem(step, 2)]


def stream_scratch(rows, columns):
    return [pltpu.VMEM((2, rows, columns), jnp.bfloat16), pltpu.SemaphoreType.DMA((2, 2))]


def projection_copies(refs, place, target, sem):
    def at(w):
        rows = refs[0].shape[0] if w is None else refs[0].shape[0] * w
        return target.at[pl.ds(0, rows)] if w is None else target.at[pl.ds(rows, refs[0].shape[0])]

    return line_copies(refs, place, at, sem)


def forward_kernel(stream, win_pieces, *refs):
    ends_ref, mine_ref, place_ref, refs = refs[0], refs[1], refs[2], refs[3:]
    pieces, refs = refs[: len(stream.pieces)], refs[len(stream.pieces) :]
    win_refs, refs = refs[: len(win_pieces)], refs[len(win_pieces) :]
    (
        order_row_ref, order_column_ref, a_ref, b_ref, mask_ref, gap_ref, gain_ref,
        sent_ref, hid_out, normed_mine_out, zq_out, zg_out, mixed_ref, query_out, forget_out, value_out, states_ref,
        query_ref, forget_ref, value_ref, out_nat, state_now, win_ref, slots, sems, win_sem,
        hid_ref, normed_mine_ref, zq_ref, zg_ref, query_nat, forget_nat, value_nat, out_sems,
    ) = refs
    early = [(hid_ref, hid_out), (normed_mine_ref, normed_mine_out), (zq_ref, zq_out), (zg_ref, zg_out)]
    early += [(query_nat, query_out), (forget_nat, forget_out), (value_nat, value_out)]
    early = [pltpu.make_async_copy(here, there, out_sems.at[i]) for i, (here, there) in enumerate(early)]
    total, width = mixed_ref.shape
    heads = width // HEAD
    devices = sent_ref.shape[0]
    rows_each = total // devices
    stream.bind(pieces, slots, sems)
    win_copies = projection_copies(windows(win_pieces, win_refs), place_ref[0], win_ref, win_sem)
    go(win_copies, "start")
    win_ref[4 * width :, :] = a_ref[...]
    columns = pl.ds(pl.multiple_of(mine_ref[0] * width, 128), width)
    ranks = mask_ref.shape[1]
    go(win_copies, "wait")

    @pl.loop(0, devices)
    def _(step):
        block = stream.fetch(step)
        rows = pl.ds(pl.multiple_of(step * rows_each, rows_each), rows_each)
        normed_mine_ref[rows, :] = slots[lax.rem(step, 2), :, columns]
        main = mm(block, win_ref[...], NT)
        mask = mask_ref[rows, :].astype(jnp.float32)
        for j in range(4):
            lowered = main[:, 4 * width + j * ranks : 4 * width + (j + 1) * ranks] * mask
            hid_ref[rows, j * ranks : (j + 1) * ranks] = lowered.astype(jnp.bfloat16)
        main = main[:, : 4 * width] + mm(hid_ref[rows, :], b_ref[...], NT)
        zq = main[:, 0:width]
        zq_ref[rows, :] = zq
        query_ref[rows, :] = (zq * jax.nn.sigmoid(zq)).astype(jnp.bfloat16)
        forget_ref[rows, :] = main[:, width : 2 * width].astype(jnp.bfloat16)
        value_ref[rows, :] = main[:, 2 * width : 3 * width].astype(jnp.bfloat16)
        zg_ref[rows, :] = main[:, 3 * width : 4 * width]

    for copy in early[:4]:
        copy.start()
    move_rows(
        picks_natural(order_row_ref),
        ((query_ref, query_nat), (forget_ref, forget_nat), (value_ref, value_nat)),
    )
    for copy in early[4:]:
        copy.start()
    state_now[...] = jnp.zeros_like(state_now)
    lower = lower_ones()

    @pl.loop(0, total // CHUNK, unroll=2)
    def _(chunk):
        start = pl.multiple_of(chunk * CHUNK, CHUNK)
        rows = pl.ds(start, CHUNK)
        allowed, _, carry_ok, tail_ok, keep = segment_terms(ends_ref, start)
        for head in range(heads):
            lanes = slice(head * HEAD, (head + 1) * HEAD)
            query = query_nat[rows, lanes].astype(jnp.float32)
            value = value_nat[rows, lanes]
            _, keys, cumulative, middle, final = chunk_decays(
                forget_nat[rows, lanes].astype(jnp.float32), gap_ref[:, lanes], lower
            )
            grown = jnp.exp(cumulative - middle)
            shrunk = jnp.exp(middle - cumulative)
            scores = mm3(halves(query * grown), halves(keys * shrunk), NT)
            scores = jnp.where(allowed, scores, 0.0)
            state = state_now[head]
            states_ref[chunk, head] = state
            inter = mm3(halves(query * jnp.exp(cumulative) * carry_ok), halves(state), NT)
            out_nat[rows, lanes] = (mm2(halves(scores), value) + inter).astype(jnp.bfloat16)
            tail = keys * jnp.exp(final - cumulative) * tail_ok
            state_now[head] = state * (jnp.exp(final) * keep) + mm2r(value, halves(tail), TN)

    states_ref[total // CHUNK] = state_now[...]
    move_rows(picks_packed(order_column_ref), ((out_nat, mixed_ref),))

    for place, bits in enumerate(block_order(devices)):
        rows = slice(place * rows_each, (place + 1) * rows_each)
        target = mine_ref[0] ^ bits
        mixed = mixed_ref[rows, :].astype(jnp.float32)
        zg = zg_ref[rows, :]
        raw = mixed * gain_ref[...] * (zg * jax.nn.sigmoid(zg))
        sent_ref[target, 0:rows_each, :] = raw.astype(jnp.bfloat16)
        squares = halves(mixed * mixed)
        ones = jnp.ones((8, width), jnp.bfloat16)
        squares = (mm(ones, squares[0], NT) + mm(ones, squares[1], NT))[0:1]
        sent_ref[target, rows_each : rows_each + 16, :] = packed_lines([squares], width)
    for copy in early:
        copy.wait()


def mixer_forward(ends, mine, place, order, blocks, win_pieces, in_a_t, in_b_wide, mask, gap, gain):
    stream = Stream(blocks)
    devices = len(blocks)
    model = in_a_t.shape[1]
    total, width = stream.rows * devices, gap.shape[0]
    heads = width // HEAD
    ranks = mask.shape[1]
    rows = jax.ShapeDtypeStruct((total, width), jnp.bfloat16)
    wide_rows = jax.ShapeDtypeStruct((total, width), jnp.float32)
    states = jax.ShapeDtypeStruct((total // CHUNK + 1, heads, HEAD, HEAD), jnp.float32)
    sent = jax.ShapeDtypeStruct((devices, stream.rows + 16, width), jnp.bfloat16)
    hid = jax.ShapeDtypeStruct((total, 4 * ranks), jnp.bfloat16)
    return pl.pallas_call(
        lambda *refs: forward_kernel(stream, win_pieces, *refs),
        out_shape=(sent, hid, rows, wide_rows, wide_rows, rows, rows, rows, rows, states),
        in_specs=[SMEM] * 3 + [ANY] * (len(stream.pieces) + len(win_pieces)) + [VMEM] * 7,
        out_specs=(VMEM, ANY, ANY, ANY, ANY, VMEM, ANY, ANY, ANY, VMEM),
        scratch_shapes=[pltpu.VMEM((total, width), jnp.bfloat16)] * 4
        + [pltpu.VMEM((heads, HEAD, HEAD), jnp.float32), pltpu.VMEM((4 * (width + ranks), model), jnp.bfloat16)]
        + stream_scratch(stream.rows, model)
        + [pltpu.SemaphoreType.DMA(())]
        + [pltpu.VMEM(array.shape, array.dtype) for array in (hid, rows, wide_rows, wide_rows, rows, rows, rows)]
        + [pltpu.SemaphoreType.DMA((7,))],
        compiler_params=params(62),
        cost_estimate=cost(57),
    )(
        ends, mine, place, *stream.arrays, *arrays_of(win_pieces), *order,
        in_a_t, in_b_wide, mask, gap.reshape(1, width), gain.reshape(1, width),
    )


def backward_kernel(win_pieces, *refs):
    ends_ref, mine_ref, place_ref, refs = refs[0], refs[1], refs[2], refs[3:]
    win_refs, refs = windows(win_pieces, refs), refs[len(win_pieces) :]
    late, refs = refs[:7], refs[7:]
    (
        order_row_ref, order_column_ref, came_ref, zg_ref, mixed_ref, gap_ref, gain_ref, mask_ref, fold_ref,
        g_proj_ref, gated_ref, small_ref, b_rows_ref, spread_out,
        grad_ref, grad_nat, d_query_nat, d_forget_nat, d_value_nat, slope_now,
        query_nat, forget_nat, value_nat, states_ref, zq_ref, hid_ref, b_ref, late_sems,
        win_ref, win_sem, spread_ref, spread_sems,
    ) = refs
    late = [
        pltpu.make_async_copy(there, here, late_sems.at[i])
        for i, (there, here) in enumerate(
            zip(late, (query_nat, forget_nat, value_nat, states_ref, zq_ref, hid_ref, b_ref))
        )
    ]
    for copy in late:
        copy.start()
    win_copies = projection_copies(win_refs, place_ref[0], win_ref, win_sem)
    go(win_copies, "start")
    total, width = mixed_ref.shape
    heads = width // HEAD
    devices = came_ref.shape[0]
    rows_each = total // devices

    for place, bits in enumerate(block_order(devices)):
        rows = slice(place * rows_each, (place + 1) * rows_each)
        source = mine_ref[0] ^ bits
        d_gated = came_ref[source, 0:rows_each, :].astype(jnp.float32)
        scalars = came_ref[source, rows_each : rows_each + 16, :].astype(jnp.float32)
        factor, mean = [
            jnp.concatenate([row_to_column(row) for row in unpacked_row(scalars, i, rows_each // width)])
            for i in range(2)
        ]
        mixed = mixed_ref[rows, :].astype(jnp.float32)
        zg = zg_ref[rows, :]
        sigma = jax.nn.sigmoid(zg)
        silu = zg * sigma
        gained = mixed * gain_ref[...]
        gated_ref[rows, :] = ((gained * silu).astype(jnp.bfloat16).astype(jnp.float32) * factor).astype(jnp.bfloat16)
        d_zg = d_gated * (gained * factor) * (sigma * (1.0 + zg * (1.0 - sigma)))
        g_proj_ref[rows, 3 * width : 4 * width] = d_zg.astype(jnp.bfloat16)
        scaled = d_gated * gain_ref[...] * silu
        cube = factor * factor * factor
        grad_ref[rows, :] = (factor * scaled - mixed * (cube * mean)).astype(jnp.bfloat16)

    move_rows(picks_natural(order_row_ref), ((grad_ref, grad_nat),))
    for copy in late[:4]:
        copy.wait()
    slope_now[...] = jnp.zeros_like(slope_now)
    lower = lower_ones()

    @pl.loop(0, total // CHUNK, unroll=2)
    def _(step):
        chunk = total // CHUNK - 1 - step
        start = pl.multiple_of(chunk * CHUNK, CHUNK)
        rows = pl.ds(start, CHUNK)
        allowed, later, carry_ok, tail_ok, keep = segment_terms(ends_ref, start)
        later = jnp.where(later, 1.0, 0.0).astype(jnp.bfloat16)
        for head in range(heads):
            lanes = slice(head * HEAD, (head + 1) * HEAD)
            query = query_nat[rows, lanes].astype(jnp.float32)
            value = value_nat[rows, lanes]
            grad = grad_nat[rows, lanes]
            sigma, keys, cumulative, middle, final = chunk_decays(
                forget_nat[rows, lanes].astype(jnp.float32), gap_ref[:, lanes], lower
            )
            grown = jnp.exp(cumulative - middle)
            shrunk = jnp.exp(middle - cumulative)
            query_grown = halves(query * grown)
            keys_shrunk = halves(keys * shrunk)
            scores = halves(jnp.where(allowed, mm3(query_grown, keys_shrunk, NT), 0.0))
            d_scores = halves(jnp.where(allowed, mm(grad, value, NT), 0.0))
            state = halves(states_ref[chunk, head])
            slope = slope_now[head]
            slope_parts = halves(slope)
            from_start = jnp.exp(cumulative) * carry_ok
            to_end = jnp.exp(final - cumulative) * tail_ok
            d_query = mm3(d_scores, keys_shrunk) * grown + mm2r(grad, state) * from_start
            d_keys = mm3(d_scores, query_grown, TN) * shrunk + mm2r(value, slope_parts) * to_end
            d_value = mm2(scores, grad, TN) + mm3(halves(keys * to_end), slope_parts, NT)
            past = jnp.sum(states_ref[chunk + 1, head] * slope, axis=0, keepdims=True)
            d_logf = sum_with(later, query * d_query - keys * d_keys) + tail_ok * past
            d_keys = d_keys - d_logf / (1.0 - keys)
            slope_now[head] = slope * (jnp.exp(final) * keep) + mm2r(grad, halves(query * from_start), TN)
            d_query_nat[rows, lanes] = d_query.astype(jnp.bfloat16)
            d_forget_nat[rows, lanes] = (-d_keys * keys * sigma).astype(jnp.bfloat16)
            d_value_nat[rows, lanes] = d_value.astype(jnp.bfloat16)

    picks = picks_packed(order_column_ref)
    for copy in late[4:]:
        copy.wait()

    @pl.loop(0, total // TILE)
    def _(tile):
        start = pl.multiple_of(tile * TILE, TILE)
        rows = pl.ds(start, TILE)
        chosen = picks(start, total)
        zq = zq_ref[rows, :]
        sigma = jax.nn.sigmoid(zq)
        d_query = mm(chosen, d_query_nat[...])
        g_proj_ref[rows, 0:width] = (d_query * (sigma * (1.0 + zq * (1.0 - sigma)))).astype(jnp.bfloat16)
        g_proj_ref[rows, width : 2 * width] = mm(chosen, d_forget_nat[...]).astype(jnp.bfloat16)
        g_proj_ref[rows, 2 * width : 3 * width] = mm(chosen, d_value_nat[...]).astype(jnp.bfloat16)
        mask = mask_ref[rows, :].astype(jnp.float32)
        through = mm(g_proj_ref[rows, :], b_ref[...])
        ranks = mask.shape[1]
        parts = [(through[:, j * ranks : (j + 1) * ranks] * mask).astype(jnp.bfloat16) for j in range(4)]
        small_ref[rows, :] = mm(jnp.concatenate(parts, axis=1), fold_ref[...]).astype(jnp.bfloat16)

    go(win_copies, "wait")
    half = devices // 2

    def spread_copy(block, slot):
        rows = pl.ds(pl.multiple_of(block * rows_each, rows_each), rows_each)
        return pltpu.make_async_copy(spread_ref.at[slot], spread_out.at[rows], spread_sems.at[slot])

    @pl.loop(0, half)
    def _(block):
        slot = lax.rem(block, 2)

        @pl.when(block >= 2)
        def _():
            spread_copy(block - 2, slot).wait()

        rows = pl.ds(pl.multiple_of((block + half) * rows_each, rows_each), rows_each)
        spread_ref[slot] = mm(g_proj_ref[rows, :], win_ref[...]).astype(jnp.bfloat16)
        spread_copy(block, slot).start()

    ranks = mask_ref.shape[1]
    for j in range(4):
        b_rows_ref[:, j * width : (j + 1) * width] = mm(
            hid_ref[:, j * ranks : (j + 1) * ranks], g_proj_ref[:, j * width : (j + 1) * width], TN
        )
    for block in range(half - 2, half):
        spread_copy(block, block % 2).wait()


def mixer_backward(ends, mine, place, order, came, kept, win_pieces, gap, gain, hid_in, in_b_wide, mask, fold):
    zq, zg, mixed, query, forget, value, states = kept
    total, width = zq.shape
    ranks = mask.shape[1]
    heads = width // HEAD
    devices = came.shape[0]
    rows_each = total // devices
    model = win_pieces[0][0].shape[1]
    rows = jax.ShapeDtypeStruct((total, width), jnp.bfloat16)
    late = (query, forget, value, states, zq, hid_in, in_b_wide)
    return pl.pallas_call(
        lambda *refs: backward_kernel(win_pieces, *refs),
        out_shape=(
            jax.ShapeDtypeStruct((total, 4 * width), jnp.bfloat16),
            rows,
            jax.ShapeDtypeStruct((total, ranks), jnp.bfloat16),
            jax.ShapeDtypeStruct((ranks, 4 * width), jnp.float32),
            jax.ShapeDtypeStruct((total // 2, model), jnp.bfloat16),
        ),
        in_specs=[SMEM] * 3 + [ANY] * (len(win_pieces) + len(late)) + [VMEM] * 9,
        out_specs=(VMEM,) * 4 + (ANY,),
        scratch_shapes=[pltpu.VMEM((total, width), jnp.bfloat16)] * 5
        + [pltpu.VMEM((heads, HEAD, HEAD), jnp.float32)]
        + [pltpu.VMEM(array.shape, array.dtype) for array in late]
        + [pltpu.SemaphoreType.DMA((len(late),))]
        + [pltpu.VMEM((4 * width, model), jnp.bfloat16), pltpu.SemaphoreType.DMA(())]
        + [pltpu.VMEM((2, rows_each, model), jnp.bfloat16), pltpu.SemaphoreType.DMA((2,))],
        compiler_params=params(62),
        cost_estimate=cost(51),
    )(
        ends, mine, place, *arrays_of(win_pieces), *late, *order, came, zg, mixed,
        gap.reshape(1, width), gain.reshape(1, width), mask, fold,
    )


def spans(blocks):
    result = []
    for index, block in enumerate(blocks):
        start = 0
        for piece in block:
            result.append((index, start, piece.shape[0]))
            start += piece.shape[0]
    return result


def token_forward_kernel(where, count, *refs):
    mine_ref, came_ref, x_ref, a_ref, b_ref, mask_ref, gain_ref = refs[:7]
    weights, refs = refs[7 : 7 + count], refs[7 + count :]
    resid_ref, normed_ref, hid_ref, all_ref, gated_ref, a_mine, sems = refs
    devices = came_ref.shape[0]
    rows, model = x_ref.shape
    width = came_ref.shape[2]
    bits = block_order(devices)
    copies = [
        pltpu.make_async_copy(weights[i], all_ref.at[pl.ds(block * width + start, size)], sems.at[i])
        for i, (block, start, size) in enumerate(where)
    ]
    for copy in copies:
        copy.start()
    squares = jnp.zeros((1, rows), jnp.float32)
    for d in range(devices):
        lines = came_ref[d, rows : rows + 16, :].astype(jnp.float32)
        squares = squares + jnp.concatenate(unpacked_row(lines, 0, rows // width), axis=1)
    factor = lax.rsqrt(row_to_column(squares) / model + eps_norm)
    for place, bit in enumerate(bits):
        source = mine_ref[0] ^ bit
        lanes = slice(place * width, (place + 1) * width)
        raw = came_ref[source, 0:rows, :].astype(jnp.float32)
        gated_ref[:, lanes] = (raw * factor).astype(jnp.bfloat16)
        a_mine[lanes, :] = a_ref[pl.ds(pl.multiple_of(source * width, 128), width), :]
    gated = gated_ref[...]
    hid = (mm(gated, a_mine[...]) * mask_ref[...].astype(jnp.float32)).astype(jnp.bfloat16)
    hid_ref[...] = hid
    extra = mm(hid, b_ref[...], NT)
    for copy in copies:
        copy.wait()
    resid = x_ref[...].astype(jnp.float32) + mm(gated, all_ref[...]) + extra
    resid_ref[...] = resid
    factor = lax.rsqrt(jnp.mean(resid * resid, axis=-1, keepdims=True) + eps_norm)
    normed_ref[...] = (resid * factor * gain_ref[...]).astype(jnp.bfloat16)


def token_forward(mine, came, x, out_a, out_b, mask_own, gain, weights):
    rows, model = x.shape
    where = spans(weights)
    pieces = [piece for block in weights for piece in block]
    ranks = out_a.shape[1]
    return pl.pallas_call(
        lambda *refs: token_forward_kernel(where, len(pieces), *refs),
        out_shape=(
            jax.ShapeDtypeStruct((rows, model), jnp.float32),
            jax.ShapeDtypeStruct((rows, model), jnp.bfloat16),
            jax.ShapeDtypeStruct((rows, ranks), jnp.bfloat16),
        ),
        in_specs=[SMEM] + [VMEM] * 6 + [ANY] * len(pieces),
        out_specs=(VMEM,) * 3,
        scratch_shapes=[
            pltpu.VMEM((model, model), jnp.bfloat16),
            pltpu.VMEM((rows, model), jnp.bfloat16),
            pltpu.VMEM((model, ranks), jnp.bfloat16),
            pltpu.SemaphoreType.DMA((len(pieces),)),
        ],
        compiler_params=params(62),
        cost_estimate=cost(8),
    )(mine, came, x, out_a, out_b, mask_own, gain.reshape(1, model), *pieces)


def summed(refs):
    own, other, from_x, from_y = refs
    total = own[...].astype(jnp.float32) + other[...].astype(jnp.float32)
    for pieces in (from_x, from_y):
        if pieces:
            total = total + jnp.concatenate([piece[...] for piece in pieces]).astype(jnp.float32)
    return total


def first_block(rows, columns):
    return pl.BlockSpec((rows, columns), lambda i: (0, 0))


def whole(array):
    return pl.BlockSpec(array.shape, lambda i: (0,) * array.ndim)


def token_backward_kernel(where, count, near, nears, *refs):
    mine_ref, came_ref, cot_ref, resid_ref, a_ref, b_ref, mask_ref, gain_ref, hid_ref, own, other = refs[:11]
    refs = refs[11:]
    from_x, from_y, refs = refs[:near], refs[near:nears], refs[nears:]
    weights, refs = refs[:count], refs[count:]
    sent_ref, d_resid_ref, d_hid_ref, b_rows_ref, all_ref, sems = refs
    devices = came_ref.shape[0]
    rows, model = resid_ref.shape
    width = came_ref.shape[2]
    copies = [
        pltpu.make_async_copy(weights[i], all_ref.at[pl.ds(block * width + start, size)], sems.at[i])
        for i, (block, start, size) in enumerate(where)
    ]
    for copy in copies:
        copy.start()
    squares = jnp.zeros((1, rows), jnp.float32)
    for d in range(devices):
        lines = came_ref[d, rows : rows + 16, :].astype(jnp.float32)
        squares = squares + jnp.concatenate(unpacked_row(lines, 0, rows // width), axis=1)
    factor_two = lax.rsqrt(squares / model + eps_norm)

    resid = resid_ref[...]
    factor = lax.rsqrt(jnp.mean(resid * resid, axis=-1, keepdims=True) + eps_norm)
    scaled = summed((own, other, from_x, from_y)) * gain_ref[...]
    mean = jnp.mean(resid * scaled, axis=-1, keepdims=True)
    d_resid = cot_ref[...].astype(jnp.float32) + factor * scaled - resid * (factor * factor * factor * mean)
    d_resid_ref[...] = d_resid
    g_attn = d_resid.astype(jnp.bfloat16)
    d_hid = (mm(g_attn, b_ref[...]) * mask_ref[...].astype(jnp.float32)).astype(jnp.bfloat16)
    d_hid_ref[...] = d_hid
    b_rows_ref[...] = mm(g_attn, hid_ref[...], TN)
    for copy in copies:
        copy.wait()
    total = jnp.zeros((rows, 1), jnp.float32)
    for place, bit in enumerate(block_order(devices)):
        target = mine_ref[0] ^ bit
        block = slice(place * width, (place + 1) * width)
        a_block = a_ref[pl.ds(pl.multiple_of(target * width, 128), width), :]
        d_gated = mm(g_attn, all_ref[block, :], NT) + mm(d_hid, a_block, NT)
        raw = came_ref[target, 0:rows, :].astype(jnp.float32)
        total = total + jnp.sum(raw * d_gated, axis=-1, keepdims=True)
        sent_ref[target, 0:rows, :] = d_gated.astype(jnp.bfloat16)
    lines = packed_lines([factor_two, column_to_row(total / model)], width)
    for d in range(devices):
        sent_ref[d, rows : rows + 16, :] = lines


def token_backward(mine, came, cot, resid, out_a, out_b, mask_own, gain, hid, parts, weights):
    rows, model = resid.shape
    own, other, from_x, from_y = parts
    where = spans(weights)
    pieces = [piece for block in weights for piece in block]
    ranks = out_a.shape[1]
    fixed = [came, cot, resid, out_a, out_b, mask_own, gain.reshape(1, model), hid]
    return pl.pallas_call(
        lambda *refs: token_backward_kernel(where, len(pieces), len(from_x), len(from_x + from_y), *refs),
        grid=(1,),
        out_shape=(
            jax.ShapeDtypeStruct(came.shape, jnp.bfloat16),
            jax.ShapeDtypeStruct((rows, model), jnp.float32),
            jax.ShapeDtypeStruct((rows, ranks), jnp.bfloat16),
            jax.ShapeDtypeStruct((model, ranks), jnp.float32),
        ),
        in_specs=[SMEM] + [whole(array) for array in fixed] + [first_block(rows, model)] * 2
        + [whole(piece) for piece in from_x + from_y] + [ANY] * len(pieces),
        out_specs=(
            pl.BlockSpec(came.shape, lambda i: (0, 0, 0)),
            first_block(rows, model),
            first_block(rows, ranks),
            first_block(model, ranks),
        ),
        scratch_shapes=[
            pltpu.VMEM((model, model), jnp.bfloat16),
            pltpu.SemaphoreType.DMA((len(pieces),)),
        ],
        compiler_params=params(62),
        cost_estimate=cost(12),
    )(mine, *fixed, own, other, *from_x, *from_y, *pieces)


def token_end_kernel(near, nears, *refs):
    x_ref, d_resid_ref, d_hid_ref, a_ref, gain_ref, own, other = refs[:7]
    refs = refs[7:]
    from_x, from_y, out_ref = refs[:near], refs[near:nears], refs[nears]
    x = x_ref[...].astype(jnp.float32)
    factor = lax.rsqrt(jnp.mean(x * x, axis=-1, keepdims=True) + eps_norm)
    d_normed = summed((own, other, from_x, from_y)) + mm(d_hid_ref[...], a_ref[...], NT)
    scaled = d_normed * gain_ref[...]
    mean = jnp.mean(x * scaled, axis=-1, keepdims=True)
    out = d_resid_ref[...] + factor * scaled - x * (factor * factor * factor * mean)
    out_ref[...] = out.astype(jnp.bfloat16)


def token_end(x, d_resid, d_hid, in_a, gain, parts):
    rows, model = x.shape
    own, other, from_x, from_y = parts
    fixed = [x, d_resid]
    return pl.pallas_call(
        lambda *refs: token_end_kernel(len(from_x), len(from_x + from_y), *refs),
        grid=(1,),
        out_shape=jax.ShapeDtypeStruct((rows, model), jnp.bfloat16),
        in_specs=[whole(x), whole(d_resid), first_block(rows, d_hid.shape[1]), whole(in_a), first_block(1, model)]
        + [first_block(rows, model)] * 2 + [whole(piece) for piece in from_x + from_y],
        out_specs=first_block(rows, model),
        compiler_params=params(62),
        cost_estimate=cost(4),
    )(x, d_resid, d_hid, in_a, gain.reshape(1, model), own, other, *from_x, *from_y)


def both_copies(refs, place, target, padded, sem):
    if len(refs) == 2:
        size = refs[0].shape[0]
        return [(None, pltpu.make_async_copy(refs[i], window(target, i * padded, size), sem)) for i in range(2)]
    groups = [refs[i : i + 6] for i in range(0, len(refs), 6)]
    units = sum(group[0].shape[0] for group in groups)
    copies, first = [], 0
    for group in groups:
        size = group[0].shape[0]

        def at(w, first=first, size=size):
            return window(target, w // 2 * padded + w % 2 * units + first, size)

        copies += line_copies(group, place, at, sem)
        first += size
    return copies


def hidden_of(refs):
    if len(refs) == 2:
        return refs[0].shape[0]
    return 2 * sum(refs[i].shape[0] for i in range(0, len(refs), 6))


def load_both(refs, place, w_all, ffn_a_ref, padded, sem):
    copies = both_copies(refs, place, w_all, padded, sem)
    go(copies, "start")
    hidden_units = hidden_of(refs)
    if padded > hidden_units:
        blank = jnp.zeros((padded - hidden_units, w_all.shape[1]), jnp.bfloat16)
        w_all[hidden_units:padded, :] = blank
        w_all[padded + hidden_units : 2 * padded, :] = blank
    w_all[2 * padded :, :] = ffn_a_ref[...]
    return copies


def ffn_up_kernel(stream, ffn_pieces, *refs):
    mine_ref, place_ref, refs = refs[0], refs[1], refs[2:]
    pieces, refs = refs[: len(stream.pieces)], refs[len(stream.pieces) :]
    weights, refs = windows(ffn_pieces, refs), refs[len(ffn_pieces) :]
    mask_ref, ffn_a_ref, both_b_ref, both_ref, hid_ref, mine_out_ref, w_all, slots, sems, ffn_sem = refs
    step = pl.program_id(0)
    stream.bind(pieces, slots, sems)
    padded = both_b_ref.shape[0] // 2
    wide = mine_out_ref.shape[1]

    @pl.when(step == 0)
    def _():
        go(load_both(weights, place_ref[0], w_all, ffn_a_ref, padded, ffn_sem), "wait")

    normed = stream.fetch(step)
    columns = pl.ds(pl.multiple_of(mine_ref[0] * wide, 128), wide)
    mine_out_ref[...] = slots[lax.rem(step, 2), :, columns]
    mask = mask_ref[...].astype(jnp.float32)
    main = mm(normed, w_all[...], NT)
    hid = (main[:, 2 * padded :] * jnp.concatenate([mask, mask], axis=1)).astype(jnp.bfloat16)
    hid_ref[...] = hid
    both_ref[...] = main[:, : 2 * padded] + mm(hid, both_b_ref[...], NT)


def ffn_up(mine, place, normed, weights, mask, ffn_a_t, both_b, wide):
    stream = Stream(normed)
    rows, model = stream.rows, ffn_a_t.shape[1]
    total = rows * len(normed)
    ranks = mask.shape[1]
    padded = both_b.shape[0] // 2
    return pl.pallas_call(
        lambda *refs: ffn_up_kernel(stream, weights, *refs),
        grid=(len(normed),),
        out_shape=(
            jax.ShapeDtypeStruct((total, 2 * padded), jnp.float32),
            jax.ShapeDtypeStruct((total, 2 * ranks), jnp.bfloat16),
            jax.ShapeDtypeStruct((total, wide), jnp.bfloat16),
        ),
        in_specs=[SMEM] * 2
        + [ANY] * (len(stream.pieces) + len(weights))
        + [tile_spec(rows, ranks), whole(ffn_a_t), whole(both_b)],
        out_specs=(tile_spec(rows, 2 * padded), tile_spec(rows, 2 * ranks), tile_spec(rows, wide)),
        scratch_shapes=[pltpu.VMEM((2 * padded + 2 * ranks, model), jnp.bfloat16)]
        + stream_scratch(rows, model)
        + [pltpu.SemaphoreType.DMA(())],
        compiler_params=params(62),
        cost_estimate=cost(28),
    )(mine, place, *stream.arrays, *arrays_of(weights), mask, ffn_a_t, both_b)


def ffn_back_kernel(stream, ffn_pieces, down_pieces, *refs):
    mine_ref, place_ref, refs = refs[0], refs[1], refs[2:]
    pieces, refs = refs[: len(stream.pieces)], refs[len(stream.pieces) :]
    weights, refs = windows(ffn_pieces, refs), refs[len(ffn_pieces) :]
    downs, refs = windows(down_pieces, refs), refs[len(down_pieces) :]
    (
        both_ref, hid_ref, mask_ref, ffn_a_ref, both_b_ref, down_a_ref, down_b_ref, fold_ref,
        back_ref, down_ref, small_ref, cot_mine_ref, down_rows, both_rows,
        w_all, w_down, left_both, left_down, slots, sems, ffn_sem, down_sem,
    ) = refs
    step = pl.program_id(0)
    stream.bind(pieces, slots, sems)
    padded = down_a_ref.shape[0]
    model = w_down.shape[1]
    wide = cot_mine_ref.shape[1]

    @pl.when(step == 0)
    def _():
        hidden_units = hidden_of(weights)
        if len(downs) == 1:
            down = line_copies(downs, place_ref[0], lambda w: window(w_down, 0, hidden_units), down_sem)
        else:
            strip = downs[0].shape[0]
            narrow = model * strip // hidden_units
            down = []
            for part in range(hidden_units // strip):
                down += line_copies(
                    [ref.at[:, pl.ds(part * narrow, narrow)] for ref in downs],
                    place_ref[0],
                    lambda w, part=part: w_down.at[pl.ds(part * strip, strip), pl.ds(w * narrow, narrow)],
                    down_sem,
                )
        go(down, "start")
        if padded > hidden_units:
            w_down[hidden_units:padded, :] = jnp.zeros((padded - hidden_units, model), jnp.bfloat16)
        w_down[padded:, :] = down_b_ref[...]
        load_both(weights, place_ref[0], w_all, ffn_a_ref, padded, ffn_sem)
        go(down, "wait")
        down_rows[...] = jnp.zeros_like(down_rows)
        both_rows[...] = jnp.zeros_like(both_rows)

    cot = stream.fetch(step)
    columns = pl.ds(pl.multiple_of(mine_ref[0] * wide, 128), wide)
    cot_mine_ref[...] = slots[lax.rem(step, 2), :, columns]
    mask = mask_ref[...].astype(jnp.float32)
    hid = hid_ref[...]
    main = mm(cot, w_down[...], NT)
    d_hid = (main[:, padded:] * mask).astype(jnp.bfloat16)
    d_hidden = main[:, :padded] + mm(d_hid, down_a_ref[...], NT)
    gate, upper = both_ref[:, :padded], both_ref[:, padded:]
    sigma = jax.nn.sigmoid(gate)
    silu = gate * sigma
    left_down[:, :padded] = (silu * upper).astype(jnp.bfloat16)
    left_both[:, :padded] = (d_hidden * upper * (sigma * (1.0 + gate * (1.0 - sigma)))).astype(jnp.bfloat16)
    left_both[:, padded : 2 * padded] = (d_hidden * silu).astype(jnp.bfloat16)
    mask_two = jnp.concatenate([mask, mask], axis=1)

    @pl.when(step == 0)
    def _():
        go(both_copies(weights, place_ref[0], w_all, padded, ffn_sem), "wait")

    through = (mm(left_both[:, : 2 * padded], both_b_ref[...]) * mask_two).astype(jnp.bfloat16)
    left_both[:, 2 * padded :] = through
    back_ref[...] = mm(left_both[...], w_all[...]).astype(jnp.bfloat16)
    low = (mm(left_down[:, :padded], down_a_ref[...]) * mask).astype(jnp.bfloat16)
    left_down[:, padded:] = low
    down_ref[...] = mm(left_down[...], w_down[...]).astype(jnp.bfloat16)
    small_ref[...] = mm(jnp.concatenate([low, through], axis=1), fold_ref[...]).astype(jnp.bfloat16)
    down_rows[...] += mm(d_hid, left_down[:, :padded], TN)
    both_rows[...] += mm(hid, left_both[:, : 2 * padded], TN)


def ffn_back(mine, place, cot, weights, downs, both, hid, mask, first, ffn_a_t, both_b, down_a, down_b_t, fold, wide):
    stream = Stream(cot)
    rows, model = stream.rows, ffn_a_t.shape[1]
    blocks = len(cot)
    total = rows * blocks
    padded, ranks = down_a.shape
    fixed = [ffn_a_t, both_b, down_a, down_b_t, fold]
    grown = jax.ShapeDtypeStruct((total, model), jnp.bfloat16)

    def from_first(columns):
        return pl.BlockSpec((rows, columns), lambda i: (i + first, 0))

    return pl.pallas_call(
        lambda *refs: ffn_back_kernel(stream, weights, downs, *refs),
        grid=(blocks,),
        out_shape=(
            grown, grown, jax.ShapeDtypeStruct((total, ranks), jnp.bfloat16),
            jax.ShapeDtypeStruct((total, wide), jnp.bfloat16),
            jax.ShapeDtypeStruct((ranks, padded), jnp.float32),
            jax.ShapeDtypeStruct((2 * ranks, 2 * padded), jnp.float32),
        ),
        in_specs=[SMEM] * 2
        + [ANY] * (len(stream.pieces) + len(weights) + len(downs))
        + [from_first(2 * padded), from_first(2 * ranks), from_first(ranks)]
        + [whole(array) for array in fixed],
        out_specs=(
            tile_spec(rows, model), tile_spec(rows, model), tile_spec(rows, ranks), tile_spec(rows, wide),
            first_block(ranks, padded), first_block(2 * ranks, 2 * padded),
        ),
        scratch_shapes=[
            pltpu.VMEM((2 * padded + 2 * ranks, model), jnp.bfloat16),
            pltpu.VMEM((padded + ranks, model), jnp.bfloat16),
            pltpu.VMEM((rows, 2 * padded + 2 * ranks), jnp.bfloat16),
            pltpu.VMEM((rows, padded + ranks), jnp.bfloat16),
        ]
        + stream_scratch(rows, model)
        + [pltpu.SemaphoreType.DMA(()), pltpu.SemaphoreType.DMA(())],
        compiler_params=params(62),
        cost_estimate=cost(33),
    )(mine, place, *stream.arrays, *arrays_of(weights), *arrays_of(downs), both, hid, mask, *fixed)


def spread_kernel(win_pieces, *refs):
    place_ref, refs = refs[0], refs[1:]
    pieces, refs = windows(win_pieces, refs), refs[len(win_pieces) :]
    x_ref, out_ref, win_ref, sem = refs
    copies = projection_copies(pieces, place_ref[0], win_ref, sem)

    @pl.when(pl.program_id(0) == 0)
    def _():
        go(copies, "start")
        go(copies, "wait")

    out_ref[...] = mm(x_ref[...], win_ref[...]).astype(jnp.bfloat16)


def spread(place, values, win_pieces, first, blocks, rows):
    inner = values.shape[1]
    model = win_pieces[0][0].shape[1]
    return pl.pallas_call(
        lambda *refs: spread_kernel(win_pieces, *refs),
        grid=(blocks,),
        out_shape=jax.ShapeDtypeStruct((rows * blocks, model), jnp.bfloat16),
        in_specs=[SMEM] + [ANY] * len(win_pieces) + [pl.BlockSpec((rows, inner), lambda i: (i + first, 0))],
        out_specs=tile_spec(rows, model),
        scratch_shapes=[pltpu.VMEM((inner, model), jnp.bfloat16), pltpu.SemaphoreType.DMA(())],
        compiler_params=params(62),
        cost_estimate=cost(8),
    )(place, *arrays_of(win_pieces), values)


def pack_in_kernel(mine_ref, win_ref, wout_ref, out_ref, window, sems):
    wide, model = window.shape[1], window.shape[0]
    narrow = wout_ref.shape[1]
    strips = model // narrow
    strip = wide // strips
    start = pl.multiple_of(mine_ref[0] * wide, 128)
    copies = [pltpu.make_async_copy(win_ref.at[:, pl.ds(start, wide)], window, sems.at[0])]
    for part in range(strips):
        copies.append(
            pltpu.make_async_copy(
                wout_ref.at[pl.ds(pl.multiple_of(start + part * strip, 16), strip)],
                out_ref.at[pl.ds(wide, strip), pl.ds(part * narrow, narrow)],
                sems.at[1 + part],
            )
        )
    for copy in copies:
        copy.start()
    eye = lax.broadcasted_iota(jnp.int32, (wide, wide), 0) == lax.broadcasted_iota(jnp.int32, (wide, wide), 1)
    eye = jnp.where(eye, 1.0, 0.0).astype(jnp.bfloat16)
    for copy in copies:
        copy.wait()
    out_ref[0:wide, :] = mm(eye, window[...], NT).astype(jnp.bfloat16)


def pack_in(mine, w_in, w_out, wide):
    model, narrow = w_in.shape[0], w_out.shape[1]
    strips = model // narrow
    return pl.pallas_call(
        pack_in_kernel,
        out_shape=jax.ShapeDtypeStruct((wide + wide // strips, model), jnp.bfloat16),
        in_specs=[SMEM, ANY, ANY],
        out_specs=VMEM,
        scratch_shapes=[pltpu.VMEM((model, wide), jnp.bfloat16), pltpu.SemaphoreType.DMA((1 + strips,))],
        compiler_params=params(62),
        cost_estimate=cost(3),
    )(mine, w_in, w_out)


def pack_ffn_kernel(units, mine_ref, wffn_ref, wdown_ref, out_ref, held, sems):
    model, columns = wffn_ref.shape
    span = held.shape[1]
    narrow = wdown_ref.shape[1]
    parts = model // narrow
    shards = wdown_ref.shape[0] // (units * 8)
    strip = units * shards // parts
    wanted = mine_ref[0] * units
    start = jnp.minimum(wanted // 128 * 128, columns - span)
    copies = [pltpu.make_async_copy(wffn_ref.at[:, pl.ds(pl.multiple_of(start, 128), span)], held, sems.at[0])]
    for part in range(parts):
        shard, inside = part * strip // units, part * strip % units
        source = shard * units * 8 + wanted + inside
        copies.append(
            pltpu.make_async_copy(
                wdown_ref.at[pl.ds(pl.multiple_of(source, 16), strip)],
                out_ref.at[pl.ds(units, strip), pl.ds(part * narrow, narrow)],
                sems.at[1 + part],
            )
        )
    for copy in copies:
        copy.start()
    rows = lax.broadcasted_iota(jnp.int32, (units, span), 0) + (wanted - start)
    chosen = jnp.where(rows == lax.broadcasted_iota(jnp.int32, (units, span), 1), 1.0, 0.0).astype(jnp.bfloat16)
    for copy in copies:
        copy.wait()
    out_ref[0:units, :] = mm(chosen, held[...], NT).astype(jnp.bfloat16)


def pack_ffn(mine, w_ffn, w_down, units):
    model, columns = w_ffn.shape
    span = min(columns, (units + 127) // 128 * 128 + 128)
    parts = model // w_down.shape[1]
    return pl.pallas_call(
        lambda *refs: pack_ffn_kernel(units, *refs),
        out_shape=jax.ShapeDtypeStruct((units + 2 * units // parts, model), jnp.bfloat16),
        in_specs=[SMEM, ANY, ANY],
        out_specs=VMEM,
        scratch_shapes=[pltpu.VMEM((model, span), jnp.bfloat16), pltpu.SemaphoreType.DMA((1 + parts,))],
        compiler_params=params(62),
        cost_estimate=cost(3),
    )(mine, w_ffn, w_down)


def unpack_out_kernel(pieces, *refs):
    place_ref, out, sem = refs[0], refs[-2], refs[-1]
    refs = windows(pieces, refs[1:-2])
    strip = refs[0].shape[0]
    strips = out.shape[0] // strip
    narrow = out.shape[1] // strips
    copies = []
    for part in range(strips):
        copies += line_copies(
            [ref.at[:, pl.ds(part * narrow, narrow)] for ref in refs],
            place_ref[0],
            lambda w, part=part: out.at[pl.ds(part * strip, strip), pl.ds(w * narrow, narrow)],
            sem,
        )
    go(copies, "start")
    go(copies, "wait")


def unpack_out(place, pieces, wide):
    model = pieces[0][0].shape[1]
    return pl.pallas_call(
        lambda *refs: unpack_out_kernel(pieces, *refs),
        out_shape=jax.ShapeDtypeStruct((wide, model), pieces[0][0].dtype),
        in_specs=[SMEM] + [ANY] * len(pieces),
        out_specs=VMEM,
        scratch_shapes=[pltpu.SemaphoreType.DMA(())],
        compiler_params=params(62),
        cost_estimate=cost(2),
    )(place, *arrays_of(pieces))


ADAPTERS = 8
RANK = 16
RANKS = ADAPTERS * RANK
PROJECTIONS = 4
eps_norm = 1e-06
f32 = jnp.float32
bf16 = jnp.bfloat16


def sequence_of(positions, seq_lengths):
    bounds = jnp.cumsum(seq_lengths)[:-1]
    return jnp.sum((positions[:, None] >= bounds[None, :]).astype(jnp.int32), axis=1)


def adapter_of(seq_numbers, seq_ids):
    numbers = jnp.arange(seq_ids.shape[0], dtype=jnp.int32)
    return jnp.sum(
        (seq_numbers[:, None] == numbers[None, :]).astype(jnp.int32) * seq_ids[None, :], axis=1
    )


def adapter_mask(adapter, count=1):
    columns = jnp.arange(count * RANKS, dtype=jnp.int32) % RANKS // RANK
    return (columns[None, :] == adapter[:, None]).astype(bf16)


def norm_factor(values):
    return lax.rsqrt(jnp.mean(values * values, axis=-1, keepdims=True) + eps_norm)


def norm_back(values, factor, gain, grad):
    scaled = grad * gain
    return factor * scaled - values * factor**3 * jnp.mean(values * scaled, axis=-1, keepdims=True)


def silu_slope(values, sigma):
    return sigma * (1.0 + values * (1.0 - sigma))


def relative(blocks, index):
    count, rest = blocks.shape[0], blocks.shape[1:]
    bit = 1
    while bit < count:
        pairs = blocks.reshape((count // (2 * bit), 2, bit) + rest)
        blocks = jnp.where((index & bit) != 0, pairs[:, ::-1], pairs).reshape((count,) + rest)
        bit *= 2
    return blocks


def to_order(blocks, index):
    count = blocks.shape[0]
    blocks = relative(blocks, index)
    pairs = blocks.reshape((count // 2, 2) + blocks.shape[1:])
    return jnp.concatenate([pairs[:, 0], pairs[:, 1]])


def from_order(blocks, index):
    count = blocks.shape[0]
    pairs = jnp.stack([blocks[: count // 2], blocks[count // 2 :]], axis=1)
    return relative(pairs.reshape(blocks.shape), index)


def across(values, bits, axis="seq"):
    size = lax.axis_size(axis)
    return lax.ppermute(values, axis, [(i, i ^ bits) for i in range(size)])


def first_near(block):
    size = lax.axis_size("seq")
    return [across(block, k) for k in ((2, 4) if size == 8 else range(2, size, 2))]


def more_near(block, first):
    if len(first) != 2:
        return [[block]] + [[other] for other in first]
    by_x, by_y = first
    half = block.shape[0] // 2
    return [[block], [by_x], [by_y], [across(by_x[:half], 4), across(by_y[half:], 2)]]


def other_core(blocks):
    return [[across(piece, 1) for piece in block] for block in blocks]


def with_rows(blocks):
    return [[(piece, 0, piece.shape[0]) for piece in block] for block in blocks]


def two_blocks(blocks):
    half = blocks[0][0].shape[0] // 2
    upper = [[(block[0], 0, half)] for block in blocks]
    return upper, [[(block[0], half, half)] for block in blocks if block[0].shape[0] == 2 * half]


def scatter_parts(near, other):
    size = lax.axis_size("seq")
    rows = near.shape[0] // (size // 2)
    half = rows // 2

    def part(block, start, stop):
        at = slice(block * rows + start, block * rows + stop)
        return near[at].astype(f32) + other[at].astype(f32)

    if size != 8:
        return [part(i, 0, rows).astype(bf16) for i in range(1, size // 2)], []
    sent = [part(3, 0, half), part(3, half, rows), part(1, 0, half), part(2, half, rows)]
    return [piece.astype(bf16) for piece in sent], [part(1, half, rows), part(2, 0, half)]


def scatter_first(sent):
    bits = (2, 4, 2, 4) if lax.axis_size("seq") == 8 else [2 * i + 2 for i in range(len(sent))]
    return [across(piece, bit) for piece, bit in zip(sent, bits)]


def scatter_second(came, rest):
    if not rest:
        total = sum(piece.astype(f32) for piece in came).astype(bf16)
        return [total], []
    far_x, far_y, by_x, by_y = came
    by_x_more = across((rest[0] + far_y.astype(f32)).astype(bf16), 2)
    by_y_more = across((rest[1] + far_x.astype(f32)).astype(bf16), 4)
    return [by_x, by_x_more], [by_y_more, by_y]


def swap(values, axis="seq"):
    return lax.all_to_all(values, axis, split_axis=0, concat_axis=0, tiled=False)


def along(values, pairs):
    return lax.ppermute(values, "wt", pairs)


def first_pieces(block):
    return along(block, [(0, 1), (1, 2), (2, 3)]), along(block, [(1, 0), (2, 1), (3, 2)])


def more_pieces(first, start, size):
    place = lax.axis_index("wt")
    up, down = [piece[start : start + size] for piece in first]
    inner, outer = jnp.where(place == 1, up, down), jnp.where(place == 2, up, down)
    return [along(inner, [(1, 2), (2, 1)]), along(outer, [(2, 3), (1, 0)]), along(inner, [(1, 3), (2, 0)])]


def line_rows(block, first, more, start, size, more_start=0):
    return [(piece, start, size) for piece in (block,) + tuple(first)] + [(piece, more_start, size) for piece in more]


def after(values, *others):
    return lax.optimization_barrier((values,) + others)[0]


def to_owner(piece, count):
    size, lines = lax.axis_size("seq"), lax.axis_size("wt")
    each = lines // count
    moves = []
    for s in range(size):
        for q in range(lines):
            whole = (q // each) * size * each + s * each + q % each
            moves.append((s * lines + q, whole))
    return lax.ppermute(piece, ("seq", "wt"), moves)


def fold_columns(count, first):
    source = jnp.arange(count * RANKS)
    target = jnp.arange(RANKS)
    wanted = (first + source // RANKS) * RANK + source % RANK
    return (wanted[:, None] == target[None, :]).astype(bf16)


def local(
    tokens,
    cotangent,
    w_in,
    w_out,
    w_ffn,
    w_down,
    gain_mix,
    gain_gate,
    gain_ffn,
    forget_gap,
    in_a,
    in_b,
    out_a,
    out_b,
    ffn_a,
    ffn_b,
    down_a,
    down_b,
    order,
    lengths,
    adapter_ids,
):
    n, wt = lax.axis_size("seq"), lax.axis_size("wt")
    mine = lax.axis_index("seq")
    mine_ref = mine.astype(jnp.int32).reshape(1)
    place_ref = lax.axis_index("wt").astype(jnp.int32).reshape(1)
    x_rows = tokens[0]
    cot_rows = cotangent[0]
    rows, model = x_rows.shape
    total = n * rows
    wide = model // n
    units = w_ffn.shape[1] // n
    hidden_units = wt // 2 * units
    padded = (hidden_units + 127) // 128 * 128
    blocks = n // 2
    on_line = wt == PROJECTIONS and n == 8

    def my_columns(values, extent, axis):
        return lax.dynamic_slice_in_dim(values, mine * extent, extent, axis)

    def my_piece(values, axis):
        return lax.dynamic_index_in_dim(values, mine, axis, False)

    def pad_rows(values):
        return jnp.pad(values, ((0, padded - hidden_units), (0, 0)))

    if on_line:
        win_mine = pack_in(mine_ref, w_in, w_out, wide)
        win_first = lax.optimization_barrier(first_pieces(win_mine))
        win_more = more_pieces(win_first, 0, win_mine.shape[0])
        ffn_mine = pack_ffn(mine_ref, w_ffn, w_down, units)
    else:
        spread_in = lax.all_gather(w_in, "wt", axis=1, tiled=True)
        spread_in = my_piece(spread_in.reshape(model, PROJECTIONS, n, wide), 2)
        win_pieces = [jnp.transpose(spread_in, (1, 2, 0)).reshape(PROJECTIONS * wide, model)]
        win_pieces = [(win_pieces[0], 0, PROJECTIONS * wide)]
        wout_mine = lax.all_gather(my_columns(w_out, wide, 0), "wt", axis=1, tiled=True)
        down_mine = my_piece(w_down.reshape(wt // 2, n, units, -1), 1).reshape(hidden_units, -1)
        down_pieces = [(lax.all_gather(down_mine, "wt", axis=1, tiled=True), 0, hidden_units)]
        spread_ffn = lax.all_gather(my_columns(w_ffn, units, 1).T, "wt", axis=0)
        spread_ffn = [spread_ffn[: wt // 2].reshape(-1, model), spread_ffn[wt // 2 :].reshape(-1, model)]
        ffn_pieces = [(piece, 0, hidden_units) for piece in spread_ffn]

    inputs = (after(x_rows, win_mine) if on_line else x_rows).astype(f32)
    normed = (inputs * norm_factor(inputs) * gain_mix).astype(bf16)
    pair = jnp.concatenate([normed, cot_rows])
    order_mine = to_order(order[0].reshape(n, rows), mine).reshape(total)
    ends = jnp.cumsum(lengths[0])
    adapter = adapter_of(sequence_of(order_mine, lengths[0]), adapter_ids[0])
    mask = adapter_mask(adapter)
    mask_own = mask[:rows]
    gap_mine = my_columns(forget_gap, wide, 0)
    gain_mine = my_columns(gain_gate, wide, 0)
    in_b_mine = my_piece(in_b.reshape(PROJECTIONS, n, wide, RANKS), 1)
    in_b_wide = jnp.concatenate(
        [jnp.pad(in_b_mine[j], ((0, 0), (j * RANKS, (PROJECTIONS - 1 - j) * RANKS))) for j in range(PROJECTIONS)]
    )
    fold_in, fold_ffn, fold_out = fold_columns(PROJECTIONS, 0), fold_columns(3, PROJECTIONS), fold_columns(1, PROJECTIONS + 3)
    ffn_b_mine = my_piece(ffn_b.reshape(wt, n, units, RANKS), 1)
    b_gate = pad_rows(ffn_b_mine[: wt // 2].reshape(-1, RANKS))
    b_up = pad_rows(ffn_b_mine[wt // 2 :].reshape(-1, RANKS))
    both_b = jnp.concatenate([jnp.pad(b_gate, ((0, 0), (0, RANKS))), jnp.pad(b_up, ((0, 0), (RANKS, 0)))])
    down_a_mine = pad_rows(my_piece(down_a.reshape(wt // 2, n, units, RANKS), 1).reshape(-1, RANKS))
    pair_first = first_near(after(pair, in_b_wide, both_b))
    ready = lax.optimization_barrier(
        (
            pair_first, (order_mine.reshape(1, total), order_mine.reshape(total, 1)), mask, gap_mine, gain_mine,
            in_b_wide, both_b, down_a_mine, down_b.T, ffn_a.T, in_a.T,
        )
    )
    pair_first, order_both, mask, gap_mine, gain_mine, in_b_wide, both_b, down_a_mine, down_b_t, ffn_a_t, in_a_t = ready
    pair_near = [[pair]] + [[block] for block in pair_first]
    if n == 8:
        pair_near.append([across(pair_first[1][:rows], 2)])
    pair_other = [[across(after(pair, *pair_first), 1)]] + other_core(pair_near[1:])
    normed_near, cot_near = two_blocks(pair_near)
    normed_other, cot_other = two_blocks(pair_other)

    if on_line:
        win_more, ffn_mine = lax.optimization_barrier((win_more, ffn_mine))
        win_pieces = line_rows(win_mine, win_first, win_more, 0, wide)
        wout_mine = line_rows(win_mine, win_first, win_more, wide, win_mine.shape[0] - wide, wide)
        wout_mine = unpack_out(place_ref, wout_mine, wide)
    sent, hid_in, normed_mine, *kept = mixer_forward(
        ends, mine_ref, place_ref, order_both, normed_near + normed_other, win_pieces,
        after(in_a_t, wout_mine), in_b_wide, mask, gap_mine, gain_mine,
    )
    wout_first = [across(wout_mine, k) for k in range(2, n, 2)]
    if on_line:
        sent, wout_first, ffn_first = lax.optimization_barrier((sent, wout_first, first_pieces(ffn_mine)))
        early = units // 64 * 16
        early_more = more_pieces(ffn_first, 0, early)
        strip = ffn_mine.shape[0] - units
    else:
        sent, wout_first = lax.optimization_barrier((sent, wout_first))
    wout_near = [[wout_mine]] + [[block] for block in wout_first]
    wout_blocks = wout_near + other_core(wout_near)

    came = swap(sent)
    resid, normed2, hid_out = token_forward(
        mine_ref, came, x_rows, out_a, out_b, mask_own, gain_ffn, wout_blocks
    )

    if on_line:
        normed2, early_more = lax.optimization_barrier((normed2, early_more))
        late_more = more_pieces(after(ffn_first, *early_more), early, units - early)

    normed2_near = more_near(normed2, first_near(normed2))
    if on_line:
        normed2_near, late_more = lax.optimization_barrier((normed2_near, late_more))
        ffn_pieces = line_rows(ffn_mine, ffn_first, early_more, 0, early)
        ffn_pieces += line_rows(ffn_mine, ffn_first, late_more, early, units - early)
        down_more = more_pieces(after(ffn_first, *late_more), units, strip)
    both, hid_ffn, normed2_mine = ffn_up(
        mine_ref, place_ref, with_rows(normed2_near + other_core(normed2_near)), ffn_pieces, mask, ffn_a_t, both_b, wide
    )
    if on_line:
        cot_far = across(after(cot_rows, normed2), 6)
        both, down_more, cot_far = lax.optimization_barrier((both, down_more, cot_far))
        cot_near.append([(cot_far, 0, rows)])
        cot_other.append([(across(cot_far, 1), 0, rows)])
        down_pieces = line_rows(ffn_mine, ffn_first, down_more, units, strip)
    sides = []
    for cots, first in ((cot_other, blocks), (cot_near, 0)):
        sides.append(
            ffn_back(
                mine_ref, place_ref, cots, ffn_pieces, down_pieces, both, hid_ffn, mask, first,
                ffn_a_t, both_b, down_a_mine, down_b_t, fold_ffn, wide,
            )
        )
    back_far, down_far, small_far, *rest_far = sides[0]
    back, down, small, *rest = sides[1]
    back_far, down_far = across(back_far, 1), across(down_far, 1)
    back, down, back_far, down_far = lax.optimization_barrier((back, down, back_far, down_far))
    back_parts, back_rest = scatter_parts(back, back_far)
    from_x, from_y = scatter_second(scatter_first(back_parts), back_rest)
    d_sent, d_resid, d_hid_out, out_b_part = token_backward(
        mine_ref, came, cot_rows, resid, out_a, out_b, mask_own, gain_ffn, hid_out,
        (back, back_far, from_x, from_y), wout_blocks,
    )
    cot_mine = jnp.concatenate([rest[0], rest_far[0]])
    down_rows, both_rows = [rest[i] + rest_far[i] for i in (1, 2)]
    down_a_rows = down_rows[:, :hidden_units].T
    ffn_b_rows = jnp.concatenate(
        [both_rows[:RANKS, :hidden_units], both_rows[RANKS:, padded : padded + hidden_units]], axis=1
    ).T

    def packed_rows(arrays):
        return jnp.concatenate(
            [
                array[:, c * RANKS : (c + 1) * RANKS].reshape(wt, -1, RANKS)
                for array in arrays
                for c in range(array.shape[1] // RANKS)
            ],
            axis=1,
        )

    def unpacked_rows(summed, arrays):
        results, start = [], 0
        for array in arrays:
            height = array.shape[0] // wt
            parts = []
            for _ in range(array.shape[1] // RANKS):
                parts.append(summed[start : start + height])
                start += height
            results.append(jnp.concatenate(parts, axis=1))
        return results

    early = [ffn_b_rows, down_a_rows]
    early_sum = lax.psum_scatter(packed_rows(early), "wt", scatter_dimension=0, tiled=False)

    out_parts = [
        (down[i * rows : (i + 1) * rows].astype(f32) + down_far[i * rows : (i + 1) * rows].astype(f32)).astype(bf16)
        for i in range(1, blocks)
    ]
    out_parts = after(out_parts, d_sent)
    d_came = after(swap(d_sent), *out_parts)
    out_came = [across(part, 2 * i + 2) for i, part in enumerate(out_parts)]
    g_proj, gated_heads, small_in, in_b_rows, back_in_far = mixer_backward(
        ends, mine_ref, place_ref, order_both, d_came, kept, win_pieces, gap_mine, gain_mine, hid_in, in_b_wide,
        mask, fold_in,
    )
    g_proj, gated_heads, small_in, in_b_rows, back_in_far, out_came, early_sum = lax.optimization_barrier(
        (g_proj, gated_heads, small_in, in_b_rows, back_in_far, out_came, early_sum)
    )
    in_b_early = [in_b_rows.T]
    in_b_sum = lax.psum_scatter(packed_rows(in_b_early), "wt", scatter_dimension=0, tiled=False)
    ffn_b_grad, down_a_grad = unpacked_rows(early_sum, early)

    small = (small_in + jnp.concatenate([small, small_far])).reshape(n, rows, RANKS)
    small, g_proj = lax.optimization_barrier((from_order(small, mine), g_proj))
    small = swap(small)
    back_in_far = across(back_in_far, 1)
    back_in = spread(place_ref, g_proj, win_pieces, 0, blocks, rows)
    in_parts, in_rest = scatter_parts(back_in, back_in_far)
    in_came = scatter_first(in_parts)
    small = jnp.sum(after(small, *in_parts, *in_rest).astype(f32), axis=0)
    small = small.astype(bf16)
    d_hid_in_own = (mm(small, fold_in, NT) * adapter_mask(adapter[:rows], PROJECTIONS)).astype(bf16)
    small = small + mm(d_hid_out, fold_out).astype(bf16)
    small = jnp.broadcast_to(small, (n,) + small.shape)
    small = swap(jnp.concatenate([small, out_b_part.astype(bf16).reshape(n, rows, -1)], axis=2))
    block_out = resid + down[:rows].astype(f32) + down_far[:rows].astype(f32)
    block_out = (block_out + sum(piece.astype(f32) for piece in out_came)).astype(bf16)
    if in_rest:
        in_came[0], in_came[1], small, block_out = lax.optimization_barrier((in_came[0], in_came[1], small, block_out))
        in_rest = [in_rest[0] + in_came[1].astype(f32), in_rest[1] + in_came[0].astype(f32)]
        in_rest = [part.astype(bf16) for part in in_rest]
        small = after(small, *in_rest)
        from_x, from_y = [in_came[2], across(in_rest[0], 2)], [across(in_rest[1], 4), in_came[3]]
    else:
        from_x, from_y = scatter_second(in_came, in_rest)
    out_b_rows = jnp.sum(small[:, :, RANKS:].astype(f32), axis=0).reshape(wide, RANKS)
    small = to_order(small[:, :, :RANKS], mine).reshape(total, RANKS)
    d_hid_in = (mm(small, fold_in, NT) * adapter_mask(adapter, PROJECTIONS)).astype(bf16)

    wide_ffn = (mm(small, fold_ffn, NT) * adapter_mask(adapter, 3)).astype(bf16)
    late = [
        mm(cot_mine, wide_ffn[:, :RANKS], TN),
        mm(normed2_mine, wide_ffn[:, RANKS:], TN),
        mm(gated_heads, (mm(small, fold_out, NT) * mask).astype(bf16), TN),
        out_b_rows,
        mm(normed_mine, d_hid_in, TN),
    ]
    in_b_sum, small = lax.optimization_barrier((in_b_sum, small))
    (in_b_grad,) = unpacked_rows(in_b_sum, in_b_early)
    packed, from_x, from_y = lax.optimization_barrier((packed_rows(late).astype(bf16), from_x, from_y))
    late_sum = jnp.sum(swap(packed, "wt").astype(f32), axis=0)
    down_b_grad, ffn_a_grad, out_a_grad, out_b_grad, in_a_grad = unpacked_rows(late_sum, late)
    tokens_grad = token_end(
        x_rows, d_resid, d_hid_in_own, in_a, gain_mix, (back_in, back_in_far, from_x, from_y)
    )
    return (
        block_out[None],
        tokens_grad[None],
        in_a_grad,
        to_owner(in_b_grad, PROJECTIONS),
        out_a_grad,
        out_b_grad,
        ffn_a_grad,
        to_owner(ffn_b_grad, wt),
        to_owner(down_a_grad, wt // 2),
        down_b_grad,
    )


def solution(mesh):
    placed = (
        P("wt", "seq", None),
        P("wt", "seq", None),
        P(None, "wt"),
        P(None, "wt"),
        P(None, "wt"),
        P(None, "wt"),
        P(),
        P(),
        P(),
        P(),
        P(),
        P(),
        P(),
        P(),
        P(),
        P(),
        P(),
        P(),
        P("wt", None),
        P("wt", None),
        P("wt", None),
    )
    return jax.shard_map(
        local,
        mesh=mesh,
        in_specs=placed,
        out_specs=(
            P("wt", "seq", None),
            P("wt", "seq", None),
            P(("seq", "wt"), None),
            P(("seq", "wt"), None),
            P(("seq", "wt"), None),
            P(("seq", "wt"), None),
            P(("seq", "wt"), None),
            P(("seq", "wt"), None),
            P(("seq", "wt"), None),
            P(("seq", "wt"), None),
        ),
        check_vma=False,
    )
```
